512 devices in a mesh: ep: 64 (over x, z, core), tp: 8 (over y).
Axes of the slice: x: 4, y: 8, z: 8, core: 2. Of those that a mesh axis runs over, the one named last changes fastest.
Arguments:
- hidden: bfloat16 [1024, 3584], P('ep'), may hold values from -12 to 12
- norm_gain: bfloat16 [3584], replicated, may hold values from 0.099609375 to 1.8984375
- queries: bfloat16 [1024, 64, 576], P(('ep', 'tp')), may hold values from -96 to 96
- latent_cache: bfloat16 [1024, 384, 576], P(('ep', 'tp')), may hold values from -6 to 6
- lengths: int32 [1024], P(('ep', 'tp')), may hold values from 2 to 384, as said below
- expert_ids: int32 [1024, 8], P('ep'), may hold values from 0 to 63, all different within a row; in each aligned block of 16 rows (0 to 15, 16 to 31, ...) at most 4 rows name the same one
- router: bfloat16 [64, 3584], P('ep'), may hold values from -0.09375 to 0.09375
- w_gate: bfloat16 [64, 3584, 1024], P('ep', None, 'tp'), may hold values from -0.09375 to 0.09375
- w_up: bfloat16 [64, 3584, 1024], P('ep', None, 'tp'), may hold values from -0.09375 to 0.09375
- w_down: bfloat16 [64, 1024, 3584], P('ep', 'tp'), may hold values from -0.1875 to 0.1875
- w_uv: bfloat16 [64, 512, 128], P('tp'), may hold values from -0.5 to 0.5
- w_out: bfloat16 [8192, 3584], P('tp', 'ep'), may hold values from -0.125 to 0.125
Outputs:
- layer_out: bfloat16 [1024, 3584], P('ep', 'tp')
The draws below stay inside these ranges and needn't reach their ends.
Inputs may be any that keep to these rules, and one draw needn't show every extreme that they name: `expert_ids`: each row names 8 different experts. Among the 16 rows of one index of ep (aligned blocks of rows), no expert is named by more than 4 rows, a bound that some block reaches. `lengths`: some row holds all 384 positions in every draw.
All inputs are finite; a program needn't handle non-finite values.
Results may differ from the reference program's by a relative error of at most 0.009.
Values may be sent and summed in bfloat16 or wider, within the bound.
No kernel may reach another device: no remote copies, remote signals or barrier semaphores. Data moves between devices by JAX's collectives and lax.ppermute only.
A program may use at most 64 MiB of HBM per device.

```python
import math
import jax
import jax.numpy as jnp
import numpy as np
from jax import lax

D = 3584
FF_E = 1024
HEADS = 64
LAT = 512
ROPE = 64
VDIM = 128
TOP = 8
ROWS = 16
LEN = 384
EXPERTS = 64
TOKENS = 1024
CAP = 4
HEADS_G = 8
N_EP = 64
N_TP = 8


def draw_hidden(key, part):
    key = jax.random.fold_in(key, 3)
    spread = jnp.exp(jax.random.uniform(jax.random.fold_in(key, 1), (D,), minval=math.log(0.3), maxval=math.log(3.0)))
    values = jax.random.normal(jax.random.fold_in(key, 2), (TOKENS, D)) * spread[None, :]
    return jnp.clip(values, -12.0, 12.0).astype(jnp.bfloat16)


def draw_queries(key, part):
    key = jax.random.fold_in(key, 1)
    return jnp.clip(jax.random.normal(key, (TOKENS, HEADS, LAT + ROPE)), -6.0, 6.0).astype(jnp.bfloat16)


def draw_latent_cache(key, part):
    key = jax.random.fold_in(key, 2)
    return jnp.clip(jax.random.normal(key, (TOKENS, LEN, LAT + ROPE)), -6.0, 6.0).astype(jnp.bfloat16)


def draw_lengths(key, part):
    key = jax.random.fold_in(key, 4)
    drawn = jax.random.randint(key, (TOKENS,), 2, LEN + 1, dtype=jnp.int32)
    return drawn.at[0].set(LEN)


def steps_of(own_key, shape, shards, smallest, top_value):
    factor_of = 1.0
    for dim, shards_of in shards:
        heights = jax.random.uniform(jax.random.fold_in(jax.random.fold_in(own_key, 6), dim), (shards_of,), jnp.float32, smallest / len(shards), top_value / len(shards))
        factor_of = factor_of * jnp.repeat(jnp.exp(heights), shape[dim] // shards_of).reshape((-1,) + (1,) * (len(shape) - 1 - dim))
    return factor_of


def assign_block(own_key, own, number, rows, count, top, limit, skew):
    sequence = jax.random.permutation(own_key, count)
    heavy_load, usual = shares(count, rows * top, limit, skew, True), shares(count, rows * top, limit, skew, False)
    places = jnp.arange(count)

    def named(tallies, turn):
        used = int((tallies > 0).sum())
        fixed = max(1, used // 4)
        shifted = fixed + (places - fixed + turn * (used - fixed)) % max(1, count - fixed)
        return jnp.zeros((count,), jnp.int32).at[sequence[jnp.where(places < fixed, places, shifted)]].set(jnp.asarray(tallies, jnp.int32))

    tallies = jnp.where(number % 4 == 0, named(heavy_load, number // 4), named(usual, number - number // 4 - 1))
    mixed = jax.random.permutation(jax.random.fold_in(own, 3), count)
    donor, sink = mixed[0:count // 2 * 2:2], mixed[1:count // 2 * 2:2]
    margin = jnp.minimum(tallies[donor] - 1, limit - tallies[sink]) // 2
    margin = jnp.where((donor == sequence[0]) | (sink == sequence[0]) | (tallies[sink] == 0), 0, jnp.maximum(margin, 0))
    shifted = jax.random.randint(jax.random.fold_in(own, 4), (count // 2,), 0, 1 << 20) % (margin + 1)
    tallies = tallies.at[donor].add(-shifted).at[sink].add(shifted)
    members = jnp.searchsorted(jnp.cumsum(tallies), jnp.arange(rows * top), side="right").astype(jnp.int32)
    grid = members.reshape(top, rows).T
    grid = grid[jax.random.permutation(jax.random.fold_in(own, 1), rows)]
    turn = jax.random.randint(jax.random.fold_in(own, 2), (rows, 1), 0, top)
    return jnp.take_along_axis(grid, (jnp.arange(top)[None, :] + turn) % top, axis=1)


def shares(number_of, total, most, slope, full):
    weights = [(1 << 20) // math.isqrt(rank ** slope) + 1 for rank in range(1, number_of + 1)]
    largest = most if full else min(most, max(-(-total // number_of), total * weights[0] // sum(weights)))
    least = 1 if total - largest >= number_of - 1 else 0
    given, spare = [largest] + [least] * (number_of - 1), total - largest - least * (number_of - 1)
    while spare > 0:
        free = [i for i in range(1, number_of) if given[i] < largest] or [i for i in range(1, number_of) if given[i] < most]
        pool, remaining = sum([weights[i] for i in free]), spare
        for i in free:
            more = min(most - given[i], max(1, remaining * weights[i] // pool), spare)
            given[i] = given[i] + more
            spare = spare - more
    return np.array(given)


def scatter_about(own_key, dims, width, bound, shards=(), kind=jnp.bfloat16):
    factor_of = steps_of(own_key, dims, shards, -0.22, 0.18) if shards else 1.0
    result = jax.random.normal(own_key, dims, jnp.float32) * width * factor_of
    return jnp.minimum(jnp.maximum(result, -bound), bound).astype(kind)


def setup_inputs(seed: int = 0) -> dict:
    key_of = jax.random.split(jax.random.key(seed), 13)
    hidden = draw_hidden(jax.random.fold_in(key_of[12], 71), 0)
    norm_gain = jnp.clip(1.0 + 0.18 * jax.random.normal(key_of[1], (D,), jnp.float32), 0.099609375, 1.8984375).astype(jnp.bfloat16)
    queries = draw_queries(jax.random.fold_in(key_of[12], 71), 0)
    latent_cache = draw_latent_cache(jax.random.fold_in(key_of[12], 71), 0)
    lengths = draw_lengths(jax.random.fold_in(key_of[12], 71), 0)
    expert_ids_keys = jax.random.split(jax.random.fold_in(key_of[5], 1), TOKENS // ROWS)
    expert_ids_turns = jax.random.permutation(jax.random.fold_in(key_of[5], 3), TOKENS // ROWS)
    expert_ids = jax.vmap(lambda own, number: assign_block(jax.random.fold_in(key_of[5], 2), own, number, ROWS, EXPERTS, TOP, CAP, 2))(expert_ids_keys, expert_ids_turns).reshape((TOKENS, TOP))
    router = scatter_about(key_of[6], (EXPERTS, D), D ** -0.5, 0.09375, ((0, 64),))
    w_gate = scatter_about(key_of[7], (EXPERTS, D, FF_E), D ** -0.5, 0.09375, ((0, 64), (2, 8)))
    w_up = scatter_about(key_of[8], (EXPERTS, D, FF_E), D ** -0.5, 0.09375, ((0, 64), (2, 8)))
    w_down = scatter_about(key_of[9], (EXPERTS, FF_E, D), FF_E ** -0.5, 0.1875, ((0, 64), (1, 8)))
    w_uv = scatter_about(key_of[10], (HEADS, LAT, VDIM), (LAT // 4) ** -0.5, 0.5, ((0, 8),))
    w_out = scatter_about(key_of[11], (HEADS * VDIM, D), (HEADS * VDIM // 4) ** -0.5, 0.125, ((0, 8), (1, 64)))
    return dict(hidden=hidden, norm_gain=norm_gain, queries=queries, latent_cache=latent_cache, lengths=lengths, expert_ids=expert_ids, router=router, w_gate=w_gate, w_up=w_up, w_down=w_down, w_uv=w_uv, w_out=w_out)


ROUTE_SCALE = 2.5
EPSILON = 1e-06
SCORE_SCALE = 192.0 ** (-0.5)

def rounded(values):
    return lax.optimization_barrier(values.astype(jnp.bfloat16)).astype(jnp.float32)

def normalize(hidden, norm_gain):
    values = hidden.astype(jnp.float32)
    factor = lax.rsqrt(lax.optimization_barrier(jnp.mean(values * values, axis=-1, keepdims=True)) + EPSILON)
    return (values * factor * norm_gain.astype(jnp.float32)).astype(jnp.bfloat16)

def attend(block_items):
    block_queries, block_cache, block_lengths = block_items
    cache_float = block_cache.astype(jnp.float32)
    scores = jnp.einsum('rhc,rpc->rhp', block_queries.astype(jnp.float32), cache_float) * SCORE_SCALE
    positions = jnp.arange(block_cache.shape[1], dtype=jnp.int32)
    visible = positions[None, None, :] < block_lengths[:, None, None]
    scores = jnp.where(visible, scores, -1e+30)
    row_peak = lax.optimization_barrier(jnp.max(scores, axis=-1, keepdims=True))
    raised = jnp.exp(scores - row_peak)
    soft_weights = rounded(raised / lax.optimization_barrier(jnp.sum(raised, axis=-1, keepdims=True)))
    context = jnp.einsum('rhp,rpl->rhl', soft_weights, cache_float[:, :, :LAT])
    return context.astype(jnp.bfloat16)

def reference(hidden, norm_gain, queries, latent_cache, lengths, expert_ids, router, w_gate, w_up, w_down, w_uv, w_out):
    normalized = normalize(hidden, norm_gain)
    blocks = N_EP * N_TP
    per_block = TOKENS // blocks
    context = lax.map(attend, (queries.reshape(blocks, per_block, HEADS, LAT + ROPE), latent_cache.reshape(blocks, per_block, LEN, LAT + ROPE), lengths.reshape(blocks, per_block)))
    context = context.reshape(TOKENS, HEADS, LAT)
    head_values = jnp.einsum('thl,hlv->thv', context.astype(jnp.float32), w_uv.astype(jnp.float32))
    head_values = head_values.astype(jnp.bfloat16).reshape(TOKENS, HEADS * VDIM)
    group_width = HEADS_G * VDIM
    attn_total = jnp.zeros((TOKENS, D), jnp.float32)
    for block_index in range(N_TP):
        lower = block_index * group_width
        partial_value = jnp.dot(head_values[:, lower:lower + group_width], w_out[lower:lower + group_width], preferred_element_type=jnp.float32)
        attn_total = attn_total + rounded(partial_value)
    block_ids = expert_ids.reshape(N_EP, ROWS * TOP)
    expert_range = jnp.arange(EXPERTS, dtype=jnp.int32)
    onehot = (block_ids[:, :, None] == expert_range[None, None, :]).astype(jnp.int32)
    slot_index = lax.optimization_barrier(jnp.sum(onehot * (jnp.cumsum(onehot, axis=1) - 1), axis=2)).reshape(TOKENS, TOP)
    source_rows = normalized.reshape(N_EP, ROWS, D).astype(jnp.float32)
    slot_range = jnp.arange(CAP, dtype=jnp.int32)
    ff_width = FF_E // N_TP

    def run_expert(expert_index):
        matches = expert_ids == expert_index
        present = jnp.any(matches, axis=1).reshape(N_EP, ROWS)
        position = lax.optimization_barrier(jnp.sum(jnp.where(matches, slot_index, 0), axis=1)).reshape(N_EP, ROWS)
        select = ((position[:, None, :] == slot_range[None, :, None]) & present[:, None, :]).astype(jnp.float32)
        rows_in = jnp.einsum('bcr,brd->bcd', select, source_rows).astype(jnp.bfloat16).reshape(N_EP * CAP, D)
        gate_act = jnp.dot(rows_in, w_gate[expert_index], preferred_element_type=jnp.float32)
        lifted = jnp.dot(rows_in, w_up[expert_index], preferred_element_type=jnp.float32)
        inner_act = (jax.nn.silu(gate_act) * lifted).astype(jnp.bfloat16)
        down_rows = w_down[expert_index]
        running_sum = jnp.zeros((N_EP * CAP, D), jnp.float32)
        for block_index in range(N_TP):
            lower = block_index * ff_width
            term = jnp.dot(inner_act[:, lower:lower + ff_width], down_rows[lower:lower + ff_width], preferred_element_type=jnp.float32)
            running_sum = running_sum + rounded(term)
        logits = jnp.dot(rows_in, router[expert_index][:, None], preferred_element_type=jnp.float32)[:, 0]
        score_vals = rounded(jax.nn.sigmoid(logits))
        return (running_sum.reshape(N_EP, CAP, D), score_vals.reshape(N_EP, CAP))
    outputs, scores = lax.map(run_expert, expert_range)
    block_of = (jnp.arange(TOKENS, dtype=jnp.int32) // ROWS)[:, None]
    picked = outputs[expert_ids, block_of, slot_index]
    picked_scores = scores[expert_ids, block_of, slot_index]
    weights = ROUTE_SCALE * picked_scores / lax.optimization_barrier(jnp.sum(picked_scores, axis=1, keepdims=True))
    merged = attn_total + jnp.einsum('tk,tkd->td', weights, picked)
    return (hidden.astype(jnp.float32) + merged).astype(jnp.bfloat16)
```

```python
import jax
import jax.numpy as jnp
from jax import lax
from jax.experimental import pallas as pl
from jax.experimental.pallas import tpu as pltpu
from jax.sharding import Mesh, PartitionSpec as P

ROUTE_SCALE = 2.5
EPSILON = 1e-06
SCORE_SCALE = 192.0 ** (-0.5)
SLOTS = 4
EP = ("x", "z", "c")
XC = ("x", "c")
NT = (((1,), (1,)), ((), ()))
TN = (((0,), (0,)), ((), ()))
F32 = jnp.float32
BF16 = jnp.bfloat16


def kernel_call(body, outs, *args, smem=(), flops=0):
    in_specs = [
        pl.BlockSpec(memory_space=pltpu.SMEM if i in smem else pltpu.VMEM)
        for i in range(len(args))
    ]
    vmem = pl.BlockSpec(memory_space=pltpu.VMEM)
    nbytes = sum(a.size * a.dtype.itemsize for a in args)
    return pl.pallas_call(
        body,
        out_shape=tuple(jax.ShapeDtypeStruct(s, d) for s, d in outs),
        in_specs=in_specs,
        out_specs=tuple(vmem for _ in outs),
        compiler_params=pltpu.CompilerParams(vmem_limit_bytes=40 << 20),
        cost_estimate=pl.CostEstimate(flops=flops, bytes_accessed=nbytes, transcendentals=0),
    )(*args)


def prepare(hidden_ref, gain_ref, ids_ref, send_ref, place_ref):
    values = hidden_ref[...].astype(F32)
    factor = lax.rsqrt(jnp.mean(values * values, axis=-1, keepdims=True) + EPSILON)
    normalized = (values * factor * gain_ref[...].astype(F32)).astype(BF16)
    slots, rows = place_ref.shape
    slot = lax.broadcasted_iota(jnp.int32, (slots, rows), 0)
    named = jnp.zeros((slots, rows), jnp.bool_)
    for k in range(ids_ref.shape[0]):
        named = named | (ids_ref[k : k + 1, :] == slot // SLOTS)
    named = named.astype(F32)
    earlier = lax.broadcasted_iota(jnp.int32, (rows, rows), 0) < lax.broadcasted_iota(
        jnp.int32, (rows, rows), 1
    )
    rank = jnp.dot(
        named.astype(BF16), earlier.astype(F32).astype(BF16), preferred_element_type=F32
    )
    place = jnp.where(rank == (slot % SLOTS).astype(F32), named, 0.0)
    place_ref[...] = place
    send_ref[...] = jnp.dot(
        place.astype(BF16), normalized, preferred_element_type=F32
    ).astype(BF16)


def attend(lengths_ref, queries_ref, cache_ref, context_ref):
    rows, heads, _ = queries_ref.shape
    latent = context_ref.shape[2]
    groups = context_ref.shape[0]
    found = []
    for r in range(rows):
        keys = cache_ref[r]
        scores = jnp.dot(queries_ref[r], keys, preferred_element_type=F32) * SCORE_SCALE
        positions = lax.broadcasted_iota(jnp.int32, scores.shape, 1)
        scores = jnp.where(positions < lengths_ref[r], scores, -1e30)
        raised = jnp.exp(scores - jnp.max(scores, axis=-1, keepdims=True))
        soft = (raised / jnp.sum(raised, axis=-1, keepdims=True)).astype(BF16)
        context = lax.dot_general(soft, keys[:latent], NT, preferred_element_type=F32)
        found.append(context.reshape(groups, heads // groups, latent))
    context_ref[...] = jnp.concatenate(found, axis=1).astype(BF16)


def lift_heads(context_ref, w_uv_ref, values_ref):
    copies, rows, _ = values_ref.shape
    heads, latent, width = w_uv_ref.shape
    context = context_ref[...].reshape(rows * heads, latent)
    token = lax.broadcasted_iota(jnp.int32, (rows, rows * heads), 0)
    entry = lax.broadcasted_iota(jnp.int32, (rows, rows * heads), 1)
    for h in range(heads):
        lifted = jnp.dot(context, w_uv_ref[h], preferred_element_type=F32).astype(BF16)
        pick = (entry == token * heads + h).astype(F32).astype(BF16)
        mine = jnp.dot(pick, lifted, preferred_element_type=F32).astype(BF16)
        for copy in range(copies):
            values_ref[copy, :, h * width : (h + 1) * width] = mine


def project(values_ref, w_out_ref, parts_ref):
    blocks, rows, depth = values_ref.shape
    slices = parts_ref.shape[1]
    cols = w_out_ref.shape[0] * 2 // slices
    values = values_ref[...].reshape(blocks * rows, depth)
    for s in range(slices // 2):
        part = lax.dot_general(
            values, w_out_ref[s * cols : (s + 1) * cols, :], NT, preferred_element_type=F32
        )
        part = part.astype(BF16).reshape(blocks, rows, cols)
        parts_ref[:, 2 * s, :, :cols] = part
        parts_ref[:, 2 * s + 1, :, :cols] = part


def lift_experts(rows_ref, w_gate_ref, w_up_ref, router_ref, inner_ref, score_ref):
    rows = rows_ref[...]
    gate = jnp.dot(rows, w_gate_ref[...], preferred_element_type=F32)
    lifted = jnp.dot(rows, w_up_ref[...], preferred_element_type=F32)
    column = jnp.broadcast_to(router_ref[...], (128, rows.shape[1]))
    logits = lax.dot_general(rows, column, NT, preferred_element_type=F32)
    inner = (gate / (1.0 + jnp.exp(-gate)) * lifted).astype(BF16)
    for copy in range(inner_ref.shape[0]):
        inner_ref[copy] = inner
    score_ref[...] = (1.0 / (1.0 + jnp.exp(-logits))).astype(BF16)


def lower_experts(inner_ref, w_down_ref, score_ref, back_ref):
    blocks, slots, _ = inner_ref.shape
    width = w_down_ref.shape[2]
    total = jnp.zeros((slots, width), F32)
    for j in range(blocks):
        total += jnp.dot(inner_ref[j], w_down_ref[j], preferred_element_type=F32)
    back_ref[:, :width] = total.astype(BF16)
    back_ref[:, width:] = score_ref[:, : back_ref.shape[1] - width]


def combine(back_ref, place_ref, attn_ref, own_ref, out_ref):
    width = out_ref.shape[1]
    score = back_ref[:, width : width + 1].astype(F32)
    share = place_ref[...] * score
    share = ROUTE_SCALE * share / jnp.sum(share, axis=0, keepdims=True)
    upper = share.astype(BF16)
    lower = (share - upper.astype(F32)).astype(BF16)
    parts = back_ref[:, :width]
    merged = attn_ref[...] + (
        lax.dot_general(upper, parts, TN, preferred_element_type=F32)
        + lax.dot_general(lower, parts, TN, preferred_element_type=F32)
    )
    out_ref[...] = (own_ref[...].astype(F32) + merged).astype(BF16)


def on_device(
    hidden,
    norm_gain,
    queries,
    latent_cache,
    lengths,
    expert_ids,
    router,
    w_gate,
    w_up,
    w_down,
    w_uv,
    w_out,
):
    rows, model_width = hidden.shape
    ep_size = lax.axis_size(EP)
    tp_size = lax.axis_size("y")
    xc_size = lax.axis_size(XC)
    z_size = lax.axis_size("z")
    slots = ep_size * SLOTS
    width = model_width // tp_size
    hidden_units = w_gate.shape[2]
    latent = w_uv.shape[1]
    heads = w_uv.shape[0]
    out_cols, depth = w_out.shape[1], w_out.shape[0]
    tp = lax.axis_index("y")

    send, place = kernel_call(
        prepare,
        [((slots, model_width), BF16), ((slots, rows), F32)],
        hidden,
        norm_gain.reshape(1, model_width),
        expert_ids.T,
    )
    named_rows = lax.all_to_all(
        send.reshape(ep_size, SLOTS, model_width), EP, 0, 0, tiled=True
    ).reshape(slots, model_width)

    (context,) = kernel_call(
        attend,
        [((tp_size, 2 * heads, latent), BF16)],
        lengths,
        queries,
        jnp.swapaxes(latent_cache, 1, 2),
        smem=(0,),
    )
    context = lax.all_to_all(context, "y", 0, 0, tiled=True)

    out_weights = jnp.broadcast_to(w_out.T[None], (xc_size, out_cols, depth))
    out_weights = lax.all_to_all(out_weights, XC, 0, 0, tiled=True)
    out_weights = out_weights.reshape(xc_size * out_cols, depth)
    down = w_down[0].reshape(hidden_units, tp_size, width).transpose(1, 0, 2)
    down = lax.all_to_all(down, "y", 0, 0, tiled=True)

    (values,) = kernel_call(
        lift_heads, [((z_size, rows, heads * w_uv.shape[2]), BF16)], context, w_uv
    )
    values = lax.all_to_all(values, "z", 0, 0, tiled=True)
    (attn_parts,) = kernel_call(
        project, [((z_size, tp_size, rows, 128), BF16)], values, out_weights
    )
    attn_parts = lax.all_to_all(
        attn_parts.reshape(z_size * tp_size, rows, 128), ("z", "y"), 0, 0, tiled=True
    ).reshape(z_size, tp_size, rows, 128)
    half = z_size // 2
    attn_parts = lax.dynamic_slice_in_dim(attn_parts, (tp % 2) * half, half, 0)
    attn_rows = jnp.sum(attn_parts.astype(F32), axis=1)[:, :, : 2 * out_cols]
    attn_rows = attn_rows.transpose(1, 0, 2).reshape(rows, width)

    inner, score = kernel_call(
        lift_experts,
        [((tp_size, slots, hidden_units), BF16), ((slots, 128), BF16)],
        named_rows,
        w_gate[0],
        w_up[0],
        router,
    )
    inner = lax.all_to_all(inner, "y", 0, 0, tiled=True)
    padded = -(-(width + 1) // 128) * 128
    (back,) = kernel_call(
        lower_experts, [((slots, padded), BF16)], inner, down, score
    )
    back = lax.all_to_all(
        back.reshape(ep_size, SLOTS, padded), EP, 0, 0, tiled=True
    ).reshape(slots, padded)
    own = lax.dynamic_slice_in_dim(hidden, tp * width, width, 1)
    (out,) = kernel_call(combine, [((rows, width), BF16)], back, place, attn_rows, own)
    return out


def solution(mesh):
    split = Mesh(mesh.devices.reshape(4, 8, 2, 8), ("x", "z", "c", "y"))
    return jax.shard_map(
        on_device,
        mesh=split,
        in_specs=(
            P(EP, None),
            P(),
            P(EP + ("y",), None, None),
            P(EP + ("y",), None, None),
            P(EP + ("y",)),
            P(EP, None),
            P(EP, None),
            P(EP, None, "y"),
            P(EP, None, "y"),
            P(EP, "y", None),
            P("y", None, None),
            P("y", EP),
        ),
        out_specs=P(EP, "y"),
        check_vma=False,
    )
```

```python
import jax
import jax.numpy as jnp
from jax import lax
from jax.experimental import pallas as pl
from jax.experimental.pallas import tpu as pltpu
from jax.sharding import Mesh, PartitionSpec as P

ROUTE_SCALE = 2.5
EPSILON = 1e-06
SCORE_SCALE = 192.0 ** (-0.5)
SLOTS = 4
EP = ("x", "zh", "zl", "c")
TP, X, ZH, ZL, CORE = range(5)
PADDED = 512
ATTN = 224
NT = (((1,), (1,)), ((), ()))
TN = (((0,), (0,)), ((), ()))
F32 = jnp.float32
BF16 = jnp.bfloat16


def kernel_call(body, outs, *args, smem=(), flops=0):
    in_specs = [
        pl.BlockSpec(memory_space=pltpu.SMEM if i in smem else pltpu.VMEM)
        for i in range(len(args))
    ]
    vmem = pl.BlockSpec(memory_space=pltpu.VMEM)
    nbytes = sum(a.size * a.dtype.itemsize for a in args)
    return pl.pallas_call(
        body,
        out_shape=tuple(jax.ShapeDtypeStruct(s, d) for s, d in outs),
        in_specs=in_specs,
        out_specs=tuple(vmem for _ in outs),
        compiler_params=pltpu.CompilerParams(vmem_limit_bytes=40 << 20),
        cost_estimate=pl.CostEstimate(flops=flops, bytes_accessed=nbytes, transcendentals=0),
    )(*args)


def prepare(hidden_ref, gain_ref, ids_ref, send_ref, place_ref):
    values = hidden_ref[...].astype(F32)
    factor = lax.rsqrt(jnp.mean(values * values, axis=-1, keepdims=True) + EPSILON)
    normalized = (values * factor * gain_ref[...].astype(F32)).astype(BF16)
    slots, rows = place_ref.shape
    slot = lax.broadcasted_iota(jnp.int32, (slots, rows), 0)
    named = jnp.zeros((slots, rows), jnp.bool_)
    for k in range(ids_ref.shape[0]):
        named = named | (ids_ref[k : k + 1, :] == slot // SLOTS)
    named = named.astype(F32)
    earlier = lax.broadcasted_iota(jnp.int32, (rows, rows), 0) < lax.broadcasted_iota(
        jnp.int32, (rows, rows), 1
    )
    rank = jnp.dot(
        named.astype(BF16), earlier.astype(F32).astype(BF16), preferred_element_type=F32
    )
    place = jnp.where(rank == (slot % SLOTS).astype(F32), named, 0.0)
    place_ref[...] = place
    send_ref[...] = jnp.dot(
        place.astype(BF16), normalized, preferred_element_type=F32
    ).astype(BF16)


def attend(place_ref, lengths_ref, queries_ref, cache_ref, context_ref):
    rows, heads, _ = queries_ref.shape
    groups, _, latent = context_ref.shape
    found = []
    for r in range(rows):
        keys = cache_ref[r]
        scores = jnp.dot(queries_ref[r], keys, preferred_element_type=F32) * SCORE_SCALE
        positions = lax.broadcasted_iota(jnp.int32, scores.shape, 1)
        scores = jnp.where(positions < lengths_ref[r], scores, -1e30)
        raised = jnp.exp(scores - jnp.max(scores, axis=-1, keepdims=True))
        soft = (raised / jnp.sum(raised, axis=-1, keepdims=True)).astype(BF16)
        context = lax.dot_general(soft, keys[:latent], NT, preferred_element_type=F32)
        found.append(context.reshape(groups, heads // groups, latent))
    found = jnp.concatenate(found, axis=1).astype(BF16)
    for g in range(groups):
        context_ref[(g - place_ref[TP] + groups) % groups] = found[g]


def lift_heads(place_ref, *refs):
    *parts, w_uv_ref, values_ref = refs
    heads, _, width = w_uv_ref.shape
    rows = values_ref.shape[0]
    share = rows // len(parts)
    context = jnp.concatenate([part[...] for part in parts], axis=0)
    token = lax.broadcasted_iota(jnp.int32, (rows, rows * heads), 0)
    entry = lax.broadcasted_iota(jnp.int32, (rows, rows * heads), 1)
    source = (place_ref[TP] - entry // (share * heads) + len(parts)) % len(parts)
    named = source * share + entry // heads % share
    for h in range(heads):
        lifted = jnp.dot(context, w_uv_ref[h], preferred_element_type=F32).astype(BF16)
        pick = ((token == named) & (entry % heads == h)).astype(F32).astype(BF16)
        mine = jnp.dot(pick, lifted, preferred_element_type=F32).astype(BF16)
        values_ref[:, h * width : (h + 1) * width] = mine


def project(place_ref, *refs):
    *parts, out_ref = refs
    values = [part[...] for part in parts[:4]]
    depth = values[0].shape[2]
    values = jnp.concatenate([part.reshape(-1, depth) for part in values], axis=0)
    for k in range(4):
        for j in range(2):
            weights = parts[4 + k][j]
            part = lax.dot_general(values, weights, NT, preferred_element_type=F32)
            x = (place_ref[X] - k + 4) % 4
            half = (place_ref[ZH] + j) % 2
            out_ref[x * 2 + half] = jnp.concatenate(
                [part, jnp.zeros((part.shape[0], 128 - part.shape[1]), F32)], axis=1
            ).astype(BF16)


def lift_experts(rows_ref, w_gate_ref, w_up_ref, router_ref, attn_ref, inner_ref, score_ref):
    rows = rows_ref[...]
    slots = rows.shape[0]
    gate = jnp.dot(rows, w_gate_ref[...], preferred_element_type=F32)
    lifted = jnp.dot(rows, w_up_ref[...], preferred_element_type=F32)
    column = jnp.broadcast_to(router_ref[...], (128, rows.shape[1]))
    logits = lax.dot_general(rows, column, NT, preferred_element_type=F32)
    inner = (gate / (1.0 + jnp.exp(-gate)) * lifted).astype(BF16)
    for copy in range(inner_ref.shape[0]):
        inner_ref[copy, :slots] = inner
        inner_ref[copy, slots:] = attn_ref[copy]
    score_ref[...] = (1.0 / (1.0 + jnp.exp(-logits))).astype(BF16)


def one_hot(condition):
    return condition.astype(F32).astype(BF16)


def iotas(*shape):
    return lax.broadcasted_iota(jnp.int32, shape, 0), lax.broadcasted_iota(jnp.int32, shape, 1)


def lower_experts(place_ref, *refs):
    inner_ref, *parts, score_ref, back_ref = refs
    sources, _, _ = inner_ref.shape
    slots, _ = back_ref.shape
    width = parts[0].shape[1]
    total = jnp.zeros((slots, width), F32)
    for k in range(sources):
        source = (place_ref[TP] - k + sources) % sources
        total += jnp.dot(inner_ref[source, :slots], parts[k][...], preferred_element_type=F32)
    back_ref[:, :width] = total.astype(BF16)
    back_ref[:, width:PADDED] = score_ref[:, : PADDED - width]
    attn = jnp.zeros((inner_ref.shape[1] - slots, 128), F32)
    for k in range(sources):
        attn += inner_ref[k, slots:].astype(F32)
    attn = attn.astype(BF16)
    tokens = attn.shape[0]
    cols = ATTN // 4
    row, entry = iotas(tokens // 4, tokens)
    zl, core = row // 8, row // 4 % 2
    held = ((place_ref[ZL] - zl + 4) % 4) * 2 + (place_ref[CORE] - core + 2) % 2
    lane_in, lane_out = iotas(128, ATTN)
    packed = jnp.zeros((tokens // 4, ATTN), F32)
    for q in range(4):
        pick = one_hot(entry == held * 16 + row % 4 * 4 + q)
        mine = jnp.dot(pick, attn, preferred_element_type=F32).astype(BF16)
        spread = one_hot((lane_out == lane_in + q * cols) & (lane_in < cols))
        packed += jnp.dot(mine, spread, preferred_element_type=F32)
    packed = packed.astype(BF16)
    for copy in range(slots * 4 // tokens):
        back_ref[copy * tokens // 4 : (copy + 1) * tokens // 4, PADDED:] = packed


def combine(place_ref, back_ref, slot_ref, own_ref, out_ref):
    rows, width = out_ref.shape
    score = back_ref[:, width : width + 1].astype(F32)
    share = slot_ref[...] * score
    share = ROUTE_SCALE * share / jnp.sum(share, axis=0, keepdims=True)
    upper = share.astype(BF16)
    lower = (share - upper.astype(F32)).astype(BF16)
    parts = back_ref[:, :width]
    merged = lax.dot_general(upper, parts, TN, preferred_element_type=F32) + lax.dot_general(
        lower, parts, TN, preferred_element_type=F32
    )
    first = pl.multiple_of((place_ref[X] * 2 + place_ref[ZH]) * 32, 32)
    packed = back_ref[pl.ds(first, 32), PADDED:]
    cols = ATTN // 4
    lane_in, lane_out = iotas(ATTN, width)
    row, lane = iotas(32, width)
    token, entry = iotas(rows, 32)
    for q in range(4):
        spread = one_hot((lane_out % cols + q * cols == lane_in))
        mine = jnp.dot(packed, spread, preferred_element_type=F32)
        mine = jnp.where(lane // cols == row // 4, mine, 0.0).astype(BF16)
        pick = one_hot(token == entry % 4 * 4 + q)
        merged += jnp.dot(pick, mine, preferred_element_type=F32)
    out_ref[...] = (own_ref[...].astype(F32) + merged).astype(BF16)


def shift(value, axis, k):
    size = lax.axis_size(axis)
    return lax.ppermute(value, axis, [(i, (i + k) % size) for i in range(size)])


def spread(blocks, axis):
    return [blocks[0]] + [shift(blocks[k], axis, k) for k in range(1, lax.axis_size(axis))]


def gather(value, first, second):
    pair = jnp.stack([value, shift(value, first, 1)])
    return [pair] + [shift(pair, second, k) for k in range(1, lax.axis_size(second))]


def on_device(
    hidden,
    norm_gain,
    queries,
    latent_cache,
    lengths,
    expert_ids,
    router,
    w_gate,
    w_up,
    w_down,
    w_uv,
    w_out,
):
    rows, model_width = hidden.shape
    ep_size = lax.axis_size(EP)
    tp_size = lax.axis_size("y")
    slots = ep_size * SLOTS
    width = model_width // tp_size
    hidden_units = w_gate.shape[2]
    heads, latent, value_width = w_uv.shape
    out_cols, depth = w_out.shape[1], w_out.shape[0]
    here = jnp.stack([lax.axis_index(a) for a in ("y", "x", "zh", "zl", "c")]).astype(jnp.int32)
    tp = here[0]

    send, place = kernel_call(
        prepare,
        [((slots, model_width), BF16), ((slots, rows), F32)],
        hidden,
        norm_gain.reshape(1, model_width),
        expert_ids.T,
    )
    named_rows = lax.all_to_all(
        send.reshape(ep_size, SLOTS, model_width), EP, 0, 0, tiled=True
    ).reshape(slots, model_width)

    (context,) = kernel_call(
        attend,
        [((tp_size, 2 * heads, latent), BF16)],
        here,
        lengths,
        queries,
        jnp.swapaxes(latent_cache, 1, 2),
        smem=(0, 1),
    )
    context = spread(context, "y")
    (values,) = kernel_call(
        lift_heads, [((rows, depth), BF16)], here, *context, w_uv, smem=(0,)
    )
    values = gather(values, "c", "zl")
    out_weights = gather(w_out.T, "zh", "x")
    (attn_parts,) = kernel_call(
        project, [((tp_size, rows * 8, 128), BF16)], here, *values, *out_weights, smem=(0,)
    )

    down = w_down[0].reshape(hidden_units, tp_size, width).transpose(1, 0, 2)
    down = [lax.dynamic_index_in_dim(down, (tp + k) % tp_size, 0, False) for k in range(tp_size)]
    down = spread(down, "y")

    inner, score = kernel_call(
        lift_experts,
        [((tp_size, slots + rows * 8, hidden_units), BF16), ((slots, 128), BF16)],
        named_rows,
        w_gate[0],
        w_up[0],
        router,
        attn_parts,
    )
    inner = lax.all_to_all(inner, "y", 0, 0, tiled=True)
    (back,) = kernel_call(
        lower_experts,
        [((slots, PADDED + ATTN), BF16)],
        here,
        inner,
        *down,
        score,
        smem=(0,),
    )
    back = lax.all_to_all(
        back.reshape(ep_size, SLOTS, PADDED + ATTN), EP, 0, 0, tiled=True
    ).reshape(slots, PADDED + ATTN)
    own = lax.dynamic_slice_in_dim(hidden, tp * width, width, 1)
    (out,) = kernel_call(
        combine, [((rows, width), BF16)], here, back, place, own, smem=(0,)
    )
    return out


def solution(mesh):
    split = Mesh(mesh.devices.reshape(4, 2, 4, 2, 8), ("x", "zh", "zl", "c", "y"))
    return jax.shard_map(
        on_device,
        mesh=split,
        in_specs=(
            P(EP, None),
            P(),
            P(EP + ("y",), None, None),
            P(EP + ("y",), None, None),
            P(EP + ("y",)),
            P(EP, None),
            P(EP, None),
            P(EP, None, "y"),
            P(EP, None, "y"),
            P(EP, "y", None),
            P("y", None, None),
            P("y", EP),
        ),
        out_specs=P(EP, "y"),
        check_vma=False,
    )
```

```python
import jax
import jax.numpy as jnp
from jax import lax
from jax.experimental import pallas as pl
from jax.experimental.pallas import tpu as pltpu
from jax.sharding import Mesh, PartitionSpec as P

ROUTE_SCALE = 2.5
EPSILON = 1e-06
SCORE_SCALE = 192.0 ** (-0.5)
SLOTS = 4
EP = ("x", "zh", "zl", "c")
TP, X, ZH, ZL, CORE = range(5)
PADDED = 512
ATTN = 224
NT = (((1,), (1,)), ((), ()))
TN = (((0,), (0,)), ((), ()))
F32 = jnp.float32
BF16 = jnp.bfloat16


def kernel_call(body, outs, *args, smem=(), after=(), flops=0):
    in_specs = [
        pl.BlockSpec(memory_space=pltpu.SMEM if i in smem else pltpu.VMEM)
        for i in range(len(args))
    ] + [pl.BlockSpec(memory_space=pl.ANY) for _ in after]
    if after:
        inner, count = body, len(args)
        body = lambda *refs: inner(*refs[:count], *refs[count + len(after) :])
    vmem = pl.BlockSpec(memory_space=pltpu.VMEM)
    nbytes = sum(a.size * a.dtype.itemsize for a in args)
    return pl.pallas_call(
        body,
        out_shape=tuple(jax.ShapeDtypeStruct(s, d) for s, d in outs),
        in_specs=in_specs,
        out_specs=tuple(vmem for _ in outs),
        compiler_params=pltpu.CompilerParams(vmem_limit_bytes=40 << 20),
        cost_estimate=pl.CostEstimate(flops=flops, bytes_accessed=nbytes, transcendentals=0),
    )(*args, *after)


def one_hot(condition):
    return condition.astype(F32).astype(BF16)


def iotas(*shape):
    return lax.broadcasted_iota(jnp.int32, shape, 0), lax.broadcasted_iota(jnp.int32, shape, 1)


def prepare(hidden_ref, gain_ref, ids_ref, send_ref, place_ref):
    values = hidden_ref[...].astype(F32)
    factor = lax.rsqrt(jnp.mean(values * values, axis=-1, keepdims=True) + EPSILON)
    normalized = (values * factor * gain_ref[...].astype(F32)).astype(BF16)
    slots, rows = place_ref.shape
    slot = lax.broadcasted_iota(jnp.int32, (slots, rows), 0)
    named = jnp.zeros((slots, rows), jnp.bool_)
    for k in range(ids_ref.shape[0]):
        named = named | (ids_ref[k : k + 1, :] == slot // SLOTS)
    named = named.astype(F32)
    earlier = lax.broadcasted_iota(jnp.int32, (rows, rows), 0) < lax.broadcasted_iota(
        jnp.int32, (rows, rows), 1
    )
    rank = jnp.dot(
        named.astype(BF16), earlier.astype(F32).astype(BF16), preferred_element_type=F32
    )
    place = jnp.where(rank == (slot % SLOTS).astype(F32), named, 0.0)
    place_ref[...] = place
    send_ref[...] = jnp.dot(
        place.astype(BF16), normalized, preferred_element_type=F32
    ).astype(BF16)


def attend(lengths_ref, queries_ref, cache_ref, context_ref):
    rows, heads, _ = queries_ref.shape
    groups, _, latent = context_ref.shape
    found = []
    for r in range(rows):
        keys = cache_ref[r]
        scores = jnp.dot(queries_ref[r], keys, preferred_element_type=F32) * SCORE_SCALE
        positions = lax.broadcasted_iota(jnp.int32, scores.shape, 1)
        scores = jnp.where(positions < lengths_ref[r], scores, -1e30)
        raised = jnp.exp(scores - jnp.max(scores, axis=-1, keepdims=True))
        soft = (raised / jnp.sum(raised, axis=-1, keepdims=True)).astype(BF16)
        context = lax.dot_general(soft, keys[:latent], NT, preferred_element_type=F32)
        found.append(context.reshape(groups, heads // groups, latent))
    context_ref[...] = jnp.concatenate(found, axis=1).astype(BF16)


def lift_heads(place_ref, context_ref, w_uv_ref, values_ref):
    heads, latent, width = w_uv_ref.shape
    rows = values_ref.shape[0]
    sources = context_ref.shape[0]
    context = jnp.concatenate([context_ref[k, place_ref[TP]] for k in range(sources)], axis=0)
    token, entry = iotas(rows, rows * heads)
    for h in range(heads):
        lifted = jnp.dot(context, w_uv_ref[h], preferred_element_type=F32).astype(BF16)
        pick = one_hot(entry == token * heads + h)
        mine = jnp.dot(pick, lifted, preferred_element_type=F32).astype(BF16)
        values_ref[:, h * width : (h + 1) * width] = mine


def split_down(place_ref, w_down_ref, keep_ref, send_ref):
    pairs, _, width = keep_ref.shape
    even = place_ref[TP] % 2 == 0
    for p in range(pairs):
        first = w_down_ref[:, 2 * p * width : (2 * p + 1) * width]
        second = w_down_ref[:, (2 * p + 1) * width : (2 * p + 2) * width]
        k = (p - place_ref[TP] // 2 + pairs) % pairs
        keep_ref[k] = jnp.where(even, first, second)
        send_ref[k] = jnp.where(even, second, first)


def project(place_ref, *refs):
    *parts, out_ref = refs
    values = [part[...] for part in parts[:4]]
    depth = values[0].shape[2]
    values = jnp.concatenate([part.reshape(-1, depth) for part in values], axis=0)
    for k in range(4):
        for j in range(2):
            weights = parts[4 + k][j]
            part = lax.dot_general(values, weights, NT, preferred_element_type=F32)
            x = (place_ref[X] - k + 4) % 4
            half = (place_ref[ZH] + j) % 2
            out_ref[x * 2 + half] = jnp.concatenate(
                [part, jnp.zeros((part.shape[0], 128 - part.shape[1]), F32)], axis=1
            ).astype(BF16)


def lift_experts(rows_ref, w_gate_ref, w_up_ref, router_ref, attn_ref, inner_ref, score_ref):
    rows = rows_ref[...]
    slots = rows.shape[0]
    gate = jnp.dot(rows, w_gate_ref[...], preferred_element_type=F32)
    lifted = jnp.dot(rows, w_up_ref[...], preferred_element_type=F32)
    column = jnp.broadcast_to(router_ref[...], (128, rows.shape[1]))
    logits = lax.dot_general(rows, column, NT, preferred_element_type=F32)
    inner = (gate / (1.0 + jnp.exp(-gate)) * lifted).astype(BF16)
    for copy in range(inner_ref.shape[0]):
        inner_ref[copy, :slots] = inner
        inner_ref[copy, slots:] = attn_ref[copy]
    score_ref[...] = (1.0 / (1.0 + jnp.exp(-logits))).astype(BF16)


def lower_experts(place_ref, *refs):
    inner_ref, *parts, score_ref, back_ref = refs
    sources, _, _ = inner_ref.shape
    slots, _ = back_ref.shape
    width = parts[0].shape[2]
    total = jnp.zeros((slots, width), F32)
    for k in range(len(parts)):
        pair = (place_ref[TP] // 2 - k + len(parts)) % len(parts)
        for j in range(2):
            source = pair * 2 + (place_ref[TP] + j) % 2
            total += jnp.dot(
                inner_ref[source, :slots], parts[k][j], preferred_element_type=F32
            )
    back_ref[:, :width] = total.astype(BF16)
    back_ref[:, width:PADDED] = score_ref[:, : PADDED - width]
    attn = jnp.zeros((inner_ref.shape[1] - slots, 128), F32)
    for k in range(sources):
        attn += inner_ref[k, slots:].astype(F32)
    attn = attn.astype(BF16)
    tokens = attn.shape[0]
    cols = ATTN // 4
    row, entry = iotas(tokens // 4, tokens)
    zl, core = row // 8, row // 4 % 2
    held = ((place_ref[ZL] - zl + 4) % 4) * 2 + (place_ref[CORE] - core + 2) % 2
    lane_in, lane_out = iotas(128, ATTN)
    packed = jnp.zeros((tokens // 4, ATTN), F32)
    for q in range(4):
        pick = one_hot(entry == held * 16 + row % 4 * 4 + q)
        mine = jnp.dot(pick, attn, preferred_element_type=F32).astype(BF16)
        spread = one_hot((lane_out == lane_in + q * cols) & (lane_in < cols))
        packed += jnp.dot(mine, spread, preferred_element_type=F32)
    packed = packed.astype(BF16)
    for copy in range(slots * 4 // tokens):
        back_ref[copy * tokens // 4 : (copy + 1) * tokens // 4, PADDED:] = packed


def combine(place_ref, back_ref, slot_ref, own_ref, out_ref):
    rows, width = out_ref.shape
    score = back_ref[:, width : width + 1].astype(F32)
    share = slot_ref[...] * score
    share = ROUTE_SCALE * share / jnp.sum(share, axis=0, keepdims=True)
    upper = share.astype(BF16)
    lower = (share - upper.astype(F32)).astype(BF16)
    parts = back_ref[:, :width]
    merged = lax.dot_general(upper, parts, TN, preferred_element_type=F32) + lax.dot_general(
        lower, parts, TN, preferred_element_type=F32
    )
    first = pl.multiple_of((place_ref[X] * 2 + place_ref[ZH]) * 32, 32)
    packed = back_ref[pl.ds(first, 32), PADDED:]
    cols = ATTN // 4
    lane_in, lane_out = iotas(ATTN, width)
    row, lane = iotas(32, width)
    token, entry = iotas(rows, 32)
    for q in range(4):
        spread = one_hot((lane_out % cols + q * cols == lane_in))
        mine = jnp.dot(packed, spread, preferred_element_type=F32)
        mine = jnp.where(lane // cols == row // 4, mine, 0.0).astype(BF16)
        pick = one_hot(token == entry % 4 * 4 + q)
        merged += jnp.dot(pick, mine, preferred_element_type=F32)
    out_ref[...] = (own_ref[...].astype(F32) + merged).astype(BF16)


def shift(value, axis, k):
    size = lax.axis_size(axis)
    return lax.ppermute(value, axis, [(i, (i + k) % size) for i in range(size)])


def pair_up(value, axis):
    return jnp.stack([value, shift(value, axis, 1)])


def gather(value, axis):
    return [value] + [shift(value, axis, k) for k in range(1, lax.axis_size(axis))]


def on_device(
    hidden,
    norm_gain,
    queries,
    latent_cache,
    lengths,
    expert_ids,
    router,
    w_gate,
    w_up,
    w_down,
    w_uv,
    w_out,
):
    rows, model_width = hidden.shape
    ep_size = lax.axis_size(EP)
    tp_size = lax.axis_size("y")
    slots = ep_size * SLOTS
    width = model_width // tp_size
    hidden_units = w_gate.shape[2]
    heads, latent, value_width = w_uv.shape
    out_cols, depth = w_out.shape[1], w_out.shape[0]
    here = jnp.stack([lax.axis_index(a) for a in ("y", "x", "zh", "zl", "c")]).astype(jnp.int32)
    tp = here[0]

    (context,) = kernel_call(
        attend,
        [((tp_size, 2 * heads, latent), BF16)],
        lengths,
        queries,
        jnp.swapaxes(latent_cache, 1, 2),
        smem=(0,),
    )
    contexts = lax.all_gather(context, "y", axis=0)
    out_pair = pair_up(w_out.T, "zh")

    send, place = kernel_call(
        prepare,
        [((slots, model_width), BF16), ((slots, rows), F32)],
        hidden,
        norm_gain.reshape(1, model_width),
        expert_ids.T,
        after=(context,),
    )
    named_rows = lax.all_to_all(
        send.reshape(ep_size, SLOTS, model_width), EP, 0, 0, tiled=True
    ).reshape(slots, model_width)

    out_weights = gather(out_pair, "x")
    keep, pass_on = kernel_call(
        split_down,
        [((tp_size // 2, hidden_units, width), BF16)] * 2,
        here,
        w_down[0],
        smem=(0,),
        after=(send,),
    )
    arrived = lax.ppermute(pass_on, "y", [(i, i ^ 1) for i in range(tp_size)])
    down = [jnp.stack([keep[k], arrived[k]]) for k in range(tp_size // 2)]
    down = [down[0]] + [shift(down[k], "y", 2 * k) for k in range(1, tp_size // 2)]
    (values,) = kernel_call(
        lift_heads,
        [((rows, depth), BF16)],
        here,
        contexts,
        w_uv,
        smem=(0,),
        after=(arrived,),
        flops=30_000_000_000,
    )
    values = gather(pair_up(values, "c"), "zl")
    (attn_parts,) = kernel_call(
        project, [((tp_size, rows * 8, 128), BF16)], here, *values, *out_weights, smem=(0,)
    )

    inner, score = kernel_call(
        lift_experts,
        [((tp_size, slots + rows * 8, hidden_units), BF16), ((slots, 128), BF16)],
        named_rows,
        w_gate[0],
        w_up[0],
        router,
        attn_parts,
    )
    inner = lax.all_to_all(inner, "y", 0, 0, tiled=True)
    (back,) = kernel_call(
        lower_experts,
        [((slots, PADDED + ATTN), BF16)],
        here,
        inner,
        *down,
        score,
        smem=(0,),
    )
    back = lax.all_to_all(
        back.reshape(ep_size, SLOTS, PADDED + ATTN), EP, 0, 0, tiled=True
    ).reshape(slots, PADDED + ATTN)
    own = lax.dynamic_slice_in_dim(hidden, tp * width, width, 1)
    (out,) = kernel_call(
        combine, [((rows, width), BF16)], here, back, place, own, smem=(0,)
    )
    return out


def solution(mesh):
    split = Mesh(mesh.devices.reshape(4, 2, 4, 2, 8), ("x", "zh", "zl", "c", "y"))
    return jax.shard_map(
        on_device,
        mesh=split,
        in_specs=(
            P(EP, None),
            P(),
            P(EP + ("y",), None, None),
            P(EP + ("y",), None, None),
            P(EP + ("y",)),
            P(EP, None),
            P(EP, None),
            P(EP, None, "y"),
            P(EP, None, "y"),
            P(EP, "y", None),
            P("y", None, None),
            P("y", EP),
        ),
        out_specs=P(EP, "y"),
        check_vma=False,
    )
```

```python
import jax
import jax.numpy as jnp
from jax import lax
from jax.experimental import pallas as pl
from jax.experimental.pallas import tpu as pltpu
from jax.sharding import Mesh, PartitionSpec as P

ROUTE_SCALE = 2.5
EPSILON = 1e-06
SCORE_SCALE = 192.0 ** (-0.5)
SLOTS = 4
EP = ("x", "zh", "zl", "c")
TP, X, ZH, ZL, CORE = range(5)
PADDED = 512
ATTN = 224
NT = (((1,), (1,)), ((), ()))
TN = (((0,), (0,)), ((), ()))
F32 = jnp.float32
BF16 = jnp.bfloat16


def kernel_call(body, outs, *args, smem=(), after=(), flops=0):
    in_specs = [
        pl.BlockSpec(memory_space=pltpu.SMEM if i in smem else pltpu.VMEM)
        for i in range(len(args))
    ] + [pl.BlockSpec(memory_space=pltpu.VMEM) for _ in after]
    if after:
        inner, count = body, len(args)
        body = lambda *refs: inner(*refs[:count], *refs[count + len(after) :])
    vmem = pl.BlockSpec(memory_space=pltpu.VMEM)
    nbytes = sum(a.size * a.dtype.itemsize for a in args)
    return pl.pallas_call(
        body,
        out_shape=tuple(jax.ShapeDtypeStruct(s, d) for s, d in outs),
        in_specs=in_specs,
        out_specs=tuple(vmem for _ in outs),
        compiler_params=pltpu.CompilerParams(vmem_limit_bytes=40 << 20),
        cost_estimate=pl.CostEstimate(flops=flops, bytes_accessed=nbytes, transcendentals=0),
    )(*args, *after)


def one_hot(condition):
    return condition.astype(F32).astype(BF16)


def iotas(*shape):
    return lax.broadcasted_iota(jnp.int32, shape, 0), lax.broadcasted_iota(jnp.int32, shape, 1)


def prepare(hidden_ref, gain_ref, ids_ref, send_ref, place_ref):
    values = hidden_ref[...].astype(F32)
    factor = lax.rsqrt(jnp.mean(values * values, axis=-1, keepdims=True) + EPSILON)
    normalized = (values * factor * gain_ref[...].astype(F32)).astype(BF16)
    slots, rows = place_ref.shape
    slot = lax.broadcasted_iota(jnp.int32, (slots, rows), 0)
    named = jnp.zeros((slots, rows), jnp.bool_)
    for k in range(ids_ref.shape[0]):
        named = named | (ids_ref[k : k + 1, :] == slot // SLOTS)
    named = named.astype(F32)
    earlier = lax.broadcasted_iota(jnp.int32, (rows, rows), 0) < lax.broadcasted_iota(
        jnp.int32, (rows, rows), 1
    )
    rank = jnp.dot(
        named.astype(BF16), earlier.astype(F32).astype(BF16), preferred_element_type=F32
    )
    place = jnp.where(rank == (slot % SLOTS).astype(F32), named, 0.0)
    place_ref[...] = place
    sent = jnp.dot(place.astype(BF16), normalized, preferred_element_type=F32)
    send_ref[...] = sent.reshape(send_ref.shape).astype(BF16)


def attend(lengths_ref, queries_ref, cache_ref, context_ref):
    rows, heads, _ = queries_ref.shape
    groups, _, latent = context_ref.shape
    found = []
    for r in range(rows):
        keys = cache_ref[r]
        scores = jnp.dot(queries_ref[r], keys, preferred_element_type=F32) * SCORE_SCALE
        positions = lax.broadcasted_iota(jnp.int32, scores.shape, 1)
        scores = jnp.where(positions < lengths_ref[r], scores, -1e30)
        raised = jnp.exp(scores - jnp.max(scores, axis=-1, keepdims=True))
        soft = (raised / jnp.sum(raised, axis=-1, keepdims=True)).astype(BF16)
        context = lax.dot_general(soft, keys[:latent], NT, preferred_element_type=F32)
        found.append(context.reshape(groups, heads // groups, latent))
    context_ref[...] = jnp.concatenate(found, axis=1).astype(BF16)


def lift_heads(context_ref, w_uv_ref, values_ref):
    heads, latent, width = w_uv_ref.shape
    rows = values_ref.shape[0]
    context = context_ref[...].reshape(rows * heads, latent)
    token, entry = iotas(rows, rows * heads)
    for h in range(heads):
        lifted = jnp.dot(context, w_uv_ref[h], preferred_element_type=F32).astype(BF16)
        pick = one_hot(entry == token * heads + h)
        mine = jnp.dot(pick, lifted, preferred_element_type=F32).astype(BF16)
        values_ref[:, h * width : (h + 1) * width] = mine


def pair(first_ref, second_ref, out_ref):
    out_ref[0] = first_ref[...]
    out_ref[1] = second_ref[...]


def split_down(place_ref, w_down_ref, keep_ref, send_ref):
    pairs, _, width = keep_ref.shape
    even = place_ref[TP] % 2 == 0
    for p in range(pairs):
        first = w_down_ref[:, 2 * p * width : (2 * p + 1) * width]
        second = w_down_ref[:, (2 * p + 1) * width : (2 * p + 2) * width]
        k = (p - place_ref[TP] // 2 + pairs) % pairs
        keep_ref[k] = jnp.where(even, first, second)
        send_ref[k] = jnp.where(even, second, first)


def project(place_ref, *refs):
    *parts, out_ref = refs
    values = [part[...] for part in parts[:4]]
    depth = values[0].shape[2]
    values = jnp.concatenate([part.reshape(-1, depth) for part in values], axis=0)
    for k in range(4):
        for j in range(2):
            weights = parts[4 + k][j]
            part = lax.dot_general(values, weights, NT, preferred_element_type=F32)
            x = (place_ref[X] - k + 4) % 4
            half = (place_ref[ZH] + j) % 2
            out_ref[x * 2 + half] = jnp.concatenate(
                [part, jnp.zeros((part.shape[0], 128 - part.shape[1]), F32)], axis=1
            ).astype(BF16)


def lift_experts(rows_ref, w_gate_ref, w_up_ref, router_ref, attn_ref, inner_ref, score_ref):
    slots, width = score_ref.shape[0], rows_ref.shape[2]
    rows = rows_ref[...].astype(F32).reshape(slots, width).astype(BF16)
    gate = jnp.dot(rows, w_gate_ref[...], preferred_element_type=F32)
    lifted = jnp.dot(rows, w_up_ref[...], preferred_element_type=F32)
    column = jnp.broadcast_to(router_ref[...], (128, rows.shape[1]))
    logits = lax.dot_general(rows, column, NT, preferred_element_type=F32)
    inner = (gate / (1.0 + jnp.exp(-gate)) * lifted).astype(BF16)
    for copy in range(inner_ref.shape[0]):
        inner_ref[copy, :slots] = inner
        inner_ref[copy, slots:] = attn_ref[copy]
    score_ref[...] = (1.0 / (1.0 + jnp.exp(-logits))).astype(BF16)


def lower_experts(place_ref, *refs):
    inner_ref, *parts, score_ref, back_ref = refs
    sources, _, _ = inner_ref.shape
    slots, _ = back_ref.shape
    width = parts[0].shape[2]
    total = jnp.zeros((slots, width), F32)
    for k in range(len(parts)):
        pair = (place_ref[TP] // 2 - k + len(parts)) % len(parts)
        for j in range(2):
            source = pair * 2 + (place_ref[TP] + j) % 2
            total += jnp.dot(
                inner_ref[source, :slots], parts[k][j], preferred_element_type=F32
            )
    back_ref[:, :width] = total.astype(BF16)
    back_ref[:, width:PADDED] = score_ref[:, : PADDED - width]
    attn = jnp.zeros((inner_ref.shape[1] - slots, 128), F32)
    for k in range(sources):
        attn += inner_ref[k, slots:].astype(F32)
    attn = attn.astype(BF16)
    tokens = attn.shape[0]
    cols = ATTN // 4
    row, entry = iotas(tokens // 4, tokens)
    zl, core = row // 8, row // 4 % 2
    held = ((place_ref[ZL] - zl + 4) % 4) * 2 + (place_ref[CORE] - core + 2) % 2
    lane_in, lane_out = iotas(128, ATTN)
    packed = jnp.zeros((tokens // 4, ATTN), F32)
    for q in range(4):
        pick = one_hot(entry == held * 16 + row % 4 * 4 + q)
        mine = jnp.dot(pick, attn, preferred_element_type=F32).astype(BF16)
        spread = one_hot((lane_out == lane_in + q * cols) & (lane_in < cols))
        packed += jnp.dot(mine, spread, preferred_element_type=F32)
    packed = packed.astype(BF16)
    for copy in range(slots * 4 // tokens):
        back_ref[copy * tokens // 4 : (copy + 1) * tokens // 4, PADDED:] = packed


def combine(place_ref, back_ref, slot_ref, own_ref, out_ref):
    rows, width = out_ref.shape
    score = back_ref[:, width : width + 1].astype(F32)
    share = slot_ref[...] * score
    share = ROUTE_SCALE * share / jnp.sum(share, axis=0, keepdims=True)
    upper = share.astype(BF16)
    lower = (share - upper.astype(F32)).astype(BF16)
    parts = back_ref[:, :width]
    merged = lax.dot_general(upper, parts, TN, preferred_element_type=F32) + lax.dot_general(
        lower, parts, TN, preferred_element_type=F32
    )
    first = pl.multiple_of((place_ref[X] * 2 + place_ref[ZH]) * 32, 32)
    packed = back_ref[pl.ds(first, 32), PADDED:]
    cols = ATTN // 4
    lane_in, lane_out = iotas(ATTN, width)
    row, lane = iotas(32, width)
    token, entry = iotas(rows, 32)
    for q in range(4):
        spread = one_hot((lane_out % cols + q * cols == lane_in))
        mine = jnp.dot(packed, spread, preferred_element_type=F32)
        mine = jnp.where(lane // cols == row // 4, mine, 0.0).astype(BF16)
        pick = one_hot(token == entry % 4 * 4 + q)
        merged += jnp.dot(pick, mine, preferred_element_type=F32)
    out_ref[...] = (own_ref[...].astype(F32) + merged).astype(BF16)


def shift(value, axis, k):
    size = lax.axis_size(axis)
    return lax.ppermute(value, axis, [(i, (i + k) % size) for i in range(size)])


def pair_up(value, axis):
    return jnp.stack([value, shift(value, axis, 1)])


def gather(value, axis):
    return [value] + [shift(value, axis, k) for k in range(1, lax.axis_size(axis))]


def on_device(
    hidden,
    norm_gain,
    queries,
    latent_cache,
    lengths,
    expert_ids,
    router,
    w_gate,
    w_up,
    w_down,
    w_uv,
    w_out,
):
    rows, model_width = hidden.shape
    ep_size = lax.axis_size(EP)
    tp_size = lax.axis_size("y")
    slots = ep_size * SLOTS
    width = model_width // tp_size
    hidden_units = w_gate.shape[2]
    heads, latent, value_width = w_uv.shape
    out_cols, depth = w_out.shape[1], w_out.shape[0]
    here = jnp.stack([lax.axis_index(a) for a in ("y", "x", "zh", "zl", "c")]).astype(jnp.int32)
    tp = here[0]

    (context,) = kernel_call(
        attend,
        [((tp_size, 2 * heads, latent), BF16)],
        lengths,
        queries,
        jnp.swapaxes(latent_cache, 1, 2),
        smem=(0,),
    )
    contexts = lax.all_to_all(context, "y", 0, 0, tiled=True)
    out_other = shift(w_out.T, "zh", 1)
    (out_pair,) = kernel_call(
        pair, [((2, out_cols, depth), BF16)], w_out.T, out_other, after=(contexts,)
    )

    send, place = kernel_call(
        prepare,
        [((ep_size, SLOTS, model_width), BF16), ((slots, rows), F32)],
        hidden,
        norm_gain.reshape(1, model_width),
        expert_ids.T,
        after=(out_other,),
    )
    named_rows = lax.all_to_all(send, EP, 0, 0, tiled=True)

    out_weights = gather(out_pair, "x")
    keep, pass_on = kernel_call(
        split_down,
        [((tp_size // 2, hidden_units, width), BF16)] * 2,
        here,
        w_down[0],
        smem=(0,),
        after=(context,),
    )
    arrived = lax.ppermute(pass_on, "y", [(i, i ^ 1) for i in range(tp_size)])
    down = [jnp.stack([keep[k], arrived[k]]) for k in range(tp_size // 2)]
    down = [down[0]] + [shift(down[k], "y", 2 * k) for k in range(1, tp_size // 2)]
    (values,) = kernel_call(
        lift_heads,
        [((rows, depth), BF16)],
        contexts,
        w_uv,
        after=(*down[1:], *out_weights[1:]),
        flops=30_000_000_000,
    )
    values = gather(pair_up(values, "c"), "zl")
    (attn_parts,) = kernel_call(
        project,
        [((tp_size, rows * 8, 128), BF16)],
        here,
        *values,
        *out_weights,
        smem=(0,),
    )

    inner, score = kernel_call(
        lift_experts,
        [((tp_size, slots + rows * 8, hidden_units), BF16), ((slots, 128), BF16)],
        named_rows,
        w_gate[0],
        w_up[0],
        router,
        attn_parts,
    )
    inner = lax.all_to_all(inner, "y", 0, 0, tiled=True)
    (back,) = kernel_call(
        lower_experts,
        [((slots, PADDED + ATTN), BF16)],
        here,
        inner,
        *down,
        score,
        smem=(0,),
    )
    back = lax.all_to_all(
        back.reshape(ep_size, SLOTS, PADDED + ATTN), EP, 0, 0, tiled=True
    ).reshape(slots, PADDED + ATTN)
    own = lax.dynamic_slice_in_dim(hidden, tp * width, width, 1)
    (out,) = kernel_call(
        combine, [((rows, width), BF16)], here, back, place, own, smem=(0,)
    )
    return out


def solution(mesh):
    split = Mesh(mesh.devices.reshape(4, 2, 4, 2, 8), ("x", "zh", "zl", "c", "y"))
    return jax.shard_map(
        on_device,
        mesh=split,
        in_specs=(
            P(EP, None),
            P(),
            P(EP + ("y",), None, None),
            P(EP + ("y",), None, None),
            P(EP + ("y",)),
            P(EP, None),
            P(EP, None),
            P(EP, None, "y"),
            P(EP, None, "y"),
            P(EP, "y", None),
            P("y", None, None),
            P("y", EP),
        ),
        out_specs=P(EP, "y"),
        check_vma=False,
    )
```

```python
import jax
import jax.numpy as jnp
from jax import lax
from jax.experimental import pallas as pl
from jax.experimental.pallas import tpu as pltpu
from jax.sharding import Mesh, PartitionSpec as P

ROUTE_SCALE = 2.5
EPSILON = 1e-06
SCORE_SCALE = 192.0 ** (-0.5)
SLOTS = 4
EP = ("x", "zh", "zl", "c")
TP, X, ZH, ZL, CORE = range(5)
PADDED = 512
NT = (((1,), (1,)), ((), ()))
TN = (((0,), (0,)), ((), ()))
F32 = jnp.float32
BF16 = jnp.bfloat16


def kernel_call(body, outs, *args, smem=(), after=(), flops=0):
    in_specs = [
        pl.BlockSpec(memory_space=pltpu.SMEM if i in smem else pltpu.VMEM)
        for i in range(len(args))
    ] + [pl.BlockSpec(memory_space=pltpu.VMEM) for _ in after]
    if after:
        inner, count = body, len(args)
        body = lambda *refs: inner(*refs[:count], *refs[count + len(after) :])
    vmem = pl.BlockSpec(memory_space=pltpu.VMEM)
    nbytes = sum(a.size * a.dtype.itemsize for a in args)
    return pl.pallas_call(
        body,
        out_shape=tuple(jax.ShapeDtypeStruct(s, d) for s, d in outs),
        in_specs=in_specs,
        out_specs=tuple(vmem for _ in outs),
        compiler_params=pltpu.CompilerParams(vmem_limit_bytes=40 << 20),
        cost_estimate=pl.CostEstimate(flops=flops, bytes_accessed=nbytes, transcendentals=0),
    )(*args, *after)


def one_hot(condition):
    return condition.astype(F32).astype(BF16)


def iotas(*shape):
    return lax.broadcasted_iota(jnp.int32, shape, 0), lax.broadcasted_iota(jnp.int32, shape, 1)


def prepare(hidden_ref, gain_ref, ids_ref, send_ref, place_ref):
    values = hidden_ref[...].astype(F32)
    factor = lax.rsqrt(jnp.mean(values * values, axis=-1, keepdims=True) + EPSILON)
    normalized = (values * factor * gain_ref[...].astype(F32)).astype(BF16)
    slots, rows = place_ref.shape
    slot = lax.broadcasted_iota(jnp.int32, (slots, rows), 0)
    named = jnp.zeros((slots, rows), jnp.bool_)
    for k in range(ids_ref.shape[0]):
        named = named | (ids_ref[k : k + 1, :] == slot // SLOTS)
    named = named.astype(F32)
    earlier = lax.broadcasted_iota(jnp.int32, (rows, rows), 0) < lax.broadcasted_iota(
        jnp.int32, (rows, rows), 1
    )
    rank = jnp.dot(
        named.astype(BF16), earlier.astype(F32).astype(BF16), preferred_element_type=F32
    )
    place = jnp.where(rank == (slot % SLOTS).astype(F32), named, 0.0)
    place_ref[...] = place
    sent = jnp.dot(place.astype(BF16), normalized, preferred_element_type=F32)
    send_ref[...] = sent.reshape(send_ref.shape).astype(BF16)


def attend(lengths_ref, queries_ref, cache_ref, context_ref):
    rows, heads, _ = queries_ref.shape
    groups, _, latent = context_ref.shape
    found = []
    for r in range(rows):
        keys = cache_ref[r]
        scores = jnp.dot(queries_ref[r], keys, preferred_element_type=F32) * SCORE_SCALE
        positions = lax.broadcasted_iota(jnp.int32, scores.shape, 1)
        scores = jnp.where(positions < lengths_ref[r], scores, -1e30)
        raised = jnp.exp(scores - jnp.max(scores, axis=-1, keepdims=True))
        soft = (raised / jnp.sum(raised, axis=-1, keepdims=True)).astype(BF16)
        context = lax.dot_general(soft, keys[:latent], NT, preferred_element_type=F32)
        found.append(context.reshape(groups, heads // groups, latent))
    context_ref[...] = jnp.concatenate(found, axis=1).astype(BF16)


def lift_heads(inner_ref, w_uv_ref, values_ref):
    heads, latent, width = w_uv_ref.shape
    rows = values_ref.shape[0]
    sources, depth, lanes = inner_ref.shape
    share = rows * heads // sources
    first = depth - share * latent // lanes
    context = jnp.concatenate(
        [
            inner_ref[:, first + q * share : first + (q + 1) * share, :]
            for q in range(latent // lanes)
        ],
        axis=2,
    ).reshape(rows * heads, latent)
    token, entry = iotas(rows, rows * heads)
    for h in range(heads):
        lifted = jnp.dot(context, w_uv_ref[h], preferred_element_type=F32).astype(BF16)
        pick = one_hot(entry == token * heads + h)
        mine = jnp.dot(pick, lifted, preferred_element_type=F32).astype(BF16)
        values_ref[:, h * width : (h + 1) * width] = mine


def split_down(place_ref, w_down_ref, *out_refs):
    slices = len(out_refs)
    width = out_refs[0].shape[1]
    for s in range(slices):
        for k in range(slices):

            @pl.when((s - place_ref[TP] + slices) % slices == k)
            def _(s=s, k=k):
                out_refs[k][...] = w_down_ref[:, s * width : (s + 1) * width]


def project(place_ref, *refs):
    *parts, out_ref = refs
    slices = 8
    values = jnp.concatenate(
        [part[...].reshape(-1, part.shape[2]) for part in parts[:4]], axis=0
    )
    rows = values.shape[0] // slices
    for k in range(4):
        for j in range(2):
            weights = parts[4 + k][j]
            part = lax.dot_general(values, weights, NT, preferred_element_type=F32)
            part = jnp.concatenate(
                [part, jnp.zeros((part.shape[0], 64 - part.shape[1]), F32)], axis=1
            ).reshape(slices, rows, 64)
            part = jnp.concatenate([part[:, : rows // 2], part[:, rows // 2 :]], axis=2)
            part = part.astype(BF16)
            tp = (place_ref[X] - k + 4) % 4 * 2 + (place_ref[ZH] + j) % 2
            for b in range(slices):
                zl = (place_ref[ZL] - b // 2 + 4) % 4
                core = (place_ref[CORE] + b) % 2
                out_ref[(zl * 2 + core) * slices + tp] = part[b]


def lift_experts(rows_ref, w_gate_ref, w_up_ref, router_ref, context_ref, inner_ref, score_ref):
    slots, width = score_ref.shape[0], rows_ref.shape[2]
    rows = rows_ref[...].astype(F32).reshape(slots, width).astype(BF16)
    gate = jnp.dot(rows, w_gate_ref[...], preferred_element_type=F32)
    lifted = jnp.dot(rows, w_up_ref[...], preferred_element_type=F32)
    column = jnp.broadcast_to(router_ref[...], (128, width))
    logits = lax.dot_general(rows, column, NT, preferred_element_type=F32)
    inner = (gate / (1.0 + jnp.exp(-gate)) * lifted).astype(BF16)
    copies, share, latent = context_ref.shape
    lanes = inner_ref.shape[2]
    for copy in range(copies):
        inner_ref[copy, :slots] = inner
        for q in range(latent // lanes):
            first = slots + q * share
            inner_ref[copy, first : first + share] = context_ref[
                copy, :, q * lanes : (q + 1) * lanes
            ]
    score_ref[...] = (1.0 / (1.0 + jnp.exp(-logits))).astype(BF16)


def lower_experts(place_ref, *refs):
    inner_ref, *parts, score_ref, back_ref = refs
    sources = inner_ref.shape[0]
    blocks, _, padded = back_ref.shape
    slots = score_ref.shape[0]
    width = parts[0].shape[1]
    total = jnp.zeros((slots, width), F32)
    for k in range(sources):
        source = (place_ref[TP] - k + sources) % sources
        total += jnp.dot(inner_ref[source, :slots], parts[k][...], preferred_element_type=F32)
    total = jnp.concatenate([total, score_ref[:, : padded - width].astype(F32)], axis=1)
    back_ref[...] = total.reshape(blocks, SLOTS, padded).astype(BF16)


def merge_experts(back_ref, slot_ref, own_ref, out_ref):
    slots, width = slot_ref.shape[0], out_ref.shape[1]
    back = back_ref[...].astype(F32).reshape(slots, back_ref.shape[2])
    share = slot_ref[...] * back[:, width : width + 1]
    share = ROUTE_SCALE * share / jnp.sum(share, axis=0, keepdims=True)
    upper = share.astype(BF16)
    lower = (share - upper.astype(F32)).astype(BF16)
    parts = back[:, :width].astype(BF16)
    merged = lax.dot_general(upper, parts, TN, preferred_element_type=F32) + lax.dot_general(
        lower, parts, TN, preferred_element_type=F32
    )
    out_ref[...] = own_ref[...].astype(F32) + merged


def add_attention(parts_ref, sum_ref, out_ref):
    rows, width = out_ref.shape
    blocks, held, lanes = parts_ref.shape
    slices = blocks // 8
    cols = width // 8
    attn = jnp.sum(
        parts_ref[...].astype(F32).reshape(8, slices, held, lanes), axis=1
    ).reshape(8 * held, lanes)
    attn = attn.astype(BF16)
    merged = sum_ref[...]
    lane_in, lane_out = iotas(lanes, width)
    row, lane = iotas(8 * held, width)
    token, entry = iotas(rows, 8 * held)
    for q in range(2):
        spread = one_hot(lane_out % cols + q * (lanes // 2) == lane_in)
        mine = jnp.dot(attn, spread, preferred_element_type=F32)
        mine = jnp.where(lane // cols == row // held, mine, 0.0).astype(BF16)
        pick = one_hot(token == entry % held + q * held)
        merged += jnp.dot(pick, mine, preferred_element_type=F32)
    out_ref[...] = merged.astype(BF16)


def shift(value, axis, k):
    size = lax.axis_size(axis)
    return lax.ppermute(value, axis, [(i, (i + k) % size) for i in range(size)])


def pair_up(value, axis):
    return jnp.stack([value, shift(value, axis, 1)])


def gather(value, axis):
    return [value] + [shift(value, axis, k) for k in range(1, lax.axis_size(axis))]


def on_device(
    hidden,
    norm_gain,
    queries,
    latent_cache,
    lengths,
    expert_ids,
    router,
    w_gate,
    w_up,
    w_down,
    w_uv,
    w_out,
):
    rows, model_width = hidden.shape
    ep_size = lax.axis_size(EP)
    tp_size = lax.axis_size("y")
    slots = ep_size * SLOTS
    width = model_width // tp_size
    hidden_units = w_gate.shape[2]
    heads, latent, value_width = w_uv.shape
    out_cols, depth = w_out.shape[1], w_out.shape[0]
    here = jnp.stack([lax.axis_index(a) for a in ("y", "x", "zh", "zl", "c")]).astype(jnp.int32)
    tp = here[0]

    send, place = kernel_call(
        prepare,
        [((ep_size, SLOTS, model_width), BF16), ((slots, rows), F32)],
        hidden,
        norm_gain.reshape(1, model_width),
        expert_ids.T,
    )
    named_rows = lax.all_to_all(send, EP, 0, 0, tiled=True)

    down = kernel_call(
        split_down, [((hidden_units, width), BF16)] * tp_size, here, w_down[0], smem=(0,)
    )
    down = [down[0]] + [shift(down[k], "y", k) for k in range(1, tp_size)]

    (context,) = kernel_call(
        attend,
        [((tp_size, 2 * heads, latent), BF16)],
        lengths,
        queries,
        jnp.swapaxes(latent_cache, 1, 2),
        smem=(0,),
        after=down[1:],
    )

    out_other = shift(w_out.T, "zh", 1)
    inner, score = kernel_call(
        lift_experts,
        [((tp_size, slots + 8 * heads, hidden_units), BF16), ((slots, 128), BF16)],
        named_rows,
        w_gate[0],
        w_up[0],
        router,
        context,
        after=(out_other,),
    )
    inner = lax.all_to_all(inner, "y", 0, 0, tiled=True)

    out_weights = gather(jnp.stack([w_out.T, out_other]), "x")
    (values,) = kernel_call(
        lift_heads,
        [((rows, depth), BF16)],
        inner,
        w_uv,
        after=out_weights[1:],
        flops=10_000_000_000,
    )
    values = gather(pair_up(values, "c"), "zl")
    (attn_parts,) = kernel_call(
        project,
        [((8 * tp_size, rows // 2, 128), BF16)],
        here,
        *values,
        *out_weights,
        smem=(0,),
    )
    attn_parts = lax.all_to_all(attn_parts, ("zl", "c", "y"), 0, 0, tiled=True)

    (back,) = kernel_call(
        lower_experts,
        [((ep_size, SLOTS, PADDED), BF16)],
        here,
        inner,
        *down,
        score,
        smem=(0,),
    )
    back = lax.all_to_all(back, EP, 0, 0, tiled=True)
    own = lax.dynamic_slice_in_dim(hidden, tp * width, width, 1)
    (merged,) = kernel_call(merge_experts, [((rows, width), F32)], back, place, own)
    (out,) = kernel_call(add_attention, [((rows, width), BF16)], attn_parts, merged)
    return out


def solution(mesh):
    split = Mesh(mesh.devices.reshape(4, 2, 4, 2, 8), ("x", "zh", "zl", "c", "y"))
    return jax.shard_map(
        on_device,
        mesh=split,
        in_specs=(
            P(EP, None),
            P(),
            P(EP + ("y",), None, None),
            P(EP + ("y",), None, None),
            P(EP + ("y",)),
            P(EP, None),
            P(EP, None),
            P(EP, None, "y"),
            P(EP, None, "y"),
            P(EP, "y", None),
            P("y", None, None),
            P("y", EP),
        ),
        out_specs=P(EP, "y"),
        check_vma=False,
    )
```

```python
import jax
import jax.numpy as jnp
from jax import lax
from jax.experimental import pallas as pl
from jax.experimental.pallas import tpu as pltpu
from jax.sharding import Mesh, PartitionSpec as P

ROUTE_SCALE = 2.5
EPSILON = 1e-06
SCORE_SCALE = 192.0 ** (-0.5)
SLOTS = 4
EP = ("x", "zh", "zl", "c")
PADDED = 1024
GROUP = 4
NT = (((1,), (1,)), ((), ()))
TN = (((0,), (0,)), ((), ()))
F32 = jnp.float32
BF16 = jnp.bfloat16


def kernel_call(body, outs, *args, smem=(), load=(), store=(), after=(), flops=0, vmem=16):
    def place(n, moved):
        space = pltpu.HBM if n in moved else pltpu.VMEM
        return pl.BlockSpec(memory_space=space)

    def scratch(a, n):
        return (pltpu.SMEM if n in smem else pltpu.VMEM)(a.shape, a.dtype)

    shapes = [jax.ShapeDtypeStruct(s, d) for s, d in outs]
    count = len(args) + len(after)

    def kernel(*refs):
        given = list(refs[: len(args)])
        made = list(refs[count : count + len(outs)])
        held = list(refs[count + len(outs) :])
        sems = held.pop() if load or store else None
        copies = []
        for i, n in enumerate(load):
            copies.append(pltpu.make_async_copy(given[n], held[i], sems.at[i]))
            copies[-1].start()
            given[n] = held[i]
        for copy in copies:
            copy.wait()
        copies = []
        for i, n in enumerate(store, len(load)):
            copies.append(pltpu.make_async_copy(held[i], made[n], sems.at[i]))
            made[n] = held[i]
        body(*given, *made)
        for copy in copies:
            copy.start()
        for copy in copies:
            copy.wait()

    scratch_shapes = [scratch(args[n], n) for n in load]
    scratch_shapes += [pltpu.VMEM(shapes[n].shape, shapes[n].dtype) for n in store]
    if scratch_shapes:
        scratch_shapes.append(pltpu.SemaphoreType.DMA((len(load) + len(store),)))
    nbytes = sum(a.size * a.dtype.itemsize for a in args)
    return pl.pallas_call(
        kernel,
        out_shape=tuple(shapes),
        in_specs=[place(n, load) for n in range(len(args))]
        + [pl.BlockSpec(memory_space=pl.ANY) for _ in after],
        out_specs=tuple(place(n, store) for n in range(len(outs))),
        scratch_shapes=scratch_shapes,
        compiler_params=pltpu.CompilerParams(vmem_limit_bytes=vmem << 20),
        cost_estimate=pl.CostEstimate(flops=flops, bytes_accessed=nbytes, transcendentals=0),
    )(*args, *after)


def one_hot(condition):
    return condition.astype(F32).astype(BF16)


def iotas(*shape):
    return lax.broadcasted_iota(jnp.int32, shape, 0), lax.broadcasted_iota(jnp.int32, shape, 1)


def prepare(hidden_ref, gain_ref, ids_ref, send_ref, place_ref):
    values = hidden_ref[...].astype(F32)
    factor = lax.rsqrt(jnp.mean(values * values, axis=-1, keepdims=True) + EPSILON)
    gain = gain_ref[...].astype(F32).reshape(1, values.shape[1])
    normalized = (values * factor * gain).astype(BF16)
    slots, rows = place_ref.shape
    slot = lax.broadcasted_iota(jnp.int32, (slots, rows), 0)
    named = jnp.zeros((slots, rows), jnp.bool_)
    for k in range(ids_ref.shape[0]):
        named = named | (ids_ref[k : k + 1, :] == slot // SLOTS)
    named = named.astype(F32)
    earlier = lax.broadcasted_iota(jnp.int32, (rows, rows), 0) < lax.broadcasted_iota(
        jnp.int32, (rows, rows), 1
    )
    rank = jnp.dot(
        named.astype(BF16), earlier.astype(F32).astype(BF16), preferred_element_type=F32
    )
    place = jnp.where(rank == (slot % SLOTS).astype(F32), named, 0.0)
    place_ref[...] = place
    sent = jnp.dot(place.astype(BF16), normalized, preferred_element_type=F32)
    send_ref[...] = sent.reshape(send_ref.shape).astype(BF16)


def attend(lengths_ref, queries_ref, cache_ref, context_ref):
    rows, heads, _ = queries_ref.shape
    groups, _, latent = context_ref.shape
    found = []
    for r in range(rows):
        keys = cache_ref[r]
        scores = jnp.dot(queries_ref[r], keys, preferred_element_type=F32) * SCORE_SCALE
        positions = lax.broadcasted_iota(jnp.int32, scores.shape, 1)
        scores = jnp.where(positions < lengths_ref[r], scores, -1e30)
        raised = jnp.exp(scores - jnp.max(scores, axis=-1, keepdims=True))
        soft = (raised / jnp.sum(raised, axis=-1, keepdims=True)).astype(BF16)
        context = lax.dot_general(soft, keys[:latent], NT, preferred_element_type=F32)
        found.append(context.reshape(groups, heads // groups, latent))
    context_ref[...] = jnp.concatenate(found, axis=1).astype(BF16)


def lift_heads(inner_ref, w_uv_ref, values_ref):
    heads, latent, width = w_uv_ref.shape
    rows = values_ref.shape[0]
    sources, depth, lanes = inner_ref.shape
    share = rows * heads // sources
    first = depth - share * latent // lanes
    context = jnp.concatenate(
        [
            inner_ref[:, first + q * share : first + (q + 1) * share, :]
            for q in range(latent // lanes)
        ],
        axis=2,
    ).reshape(rows * heads, latent)
    token, entry = iotas(rows, rows * heads)
    for h in range(heads):
        lifted = jnp.dot(context, w_uv_ref[h], preferred_element_type=F32).astype(BF16)
        pick = one_hot(entry == token * heads + h)
        mine = jnp.dot(pick, lifted, preferred_element_type=F32).astype(BF16)
        values_ref[:, h * width : (h + 1) * width] = mine


def split_down(w_down_ref, *out_refs):
    group = len(out_refs)
    width = out_refs[0].shape[1] // 2
    for s in range(group):
        for k in range(group):

            @pl.when(lax.axis_index("y") % group ^ k == s)
            def _(s=s, k=k):
                for half in range(2):
                    first = (half * group + s) * width
                    out_refs[k][:, half * width : (half + 1) * width] = w_down_ref[
                        :, first : first + width
                    ]


def project(*refs):
    *parts, out_ref = refs
    slices = 8
    values = jnp.concatenate(
        [part[...].reshape(-1, part.shape[2]) for part in parts[:4]], axis=0
    )
    rows = values.shape[0] // slices
    for k in range(4):
        for j in range(2):
            weights = parts[4 + k][j]
            part = lax.dot_general(values, weights, NT, preferred_element_type=F32)
            part = jnp.concatenate(
                [part, jnp.zeros((part.shape[0], 64 - part.shape[1]), F32)], axis=1
            ).reshape(slices, rows, 64)
            part = jnp.concatenate([part[:, : rows // 2], part[:, rows // 2 :]], axis=2)
            part = part.astype(BF16)
            tp = (lax.axis_index("x") - k + 4) % 4 * 2 + (lax.axis_index("zh") + j) % 2
            for b in range(slices):
                zl = lax.axis_index("zl") ^ (b // 2)
                core = (lax.axis_index("c") + b) % 2
                out_ref[(zl * 2 + core) * slices + tp] = part[b]


def lift_experts(rows_ref, w_gate_ref, w_up_ref, router_ref, context_ref, inner_ref, score_ref):
    slots, width = score_ref.shape[0], rows_ref.shape[2]
    rows = rows_ref[...].astype(F32).reshape(slots, width).astype(BF16)
    gate = jnp.dot(rows, w_gate_ref[...], preferred_element_type=F32)
    lifted = jnp.dot(rows, w_up_ref[...], preferred_element_type=F32)
    column = jnp.broadcast_to(router_ref[...], (128, width))
    logits = lax.dot_general(rows, column, NT, preferred_element_type=F32)
    inner = (gate / (1.0 + jnp.exp(-gate)) * lifted).astype(BF16)
    copies, share, latent = context_ref.shape
    lanes = inner_ref.shape[2]
    for copy in range(copies):
        inner_ref[copy, :slots] = inner
        for q in range(latent // lanes):
            first = slots + q * share
            inner_ref[copy, first : first + share] = context_ref[
                copy, :, q * lanes : (q + 1) * lanes
            ]
    score_ref[...] = (1.0 / (1.0 + jnp.exp(-logits))).astype(BF16)


def lower_experts(*refs):
    inner_ref, *parts, score_ref, back_ref = refs
    blocks, _, padded = back_ref.shape
    slots = score_ref.shape[0]
    width = parts[0].shape[1]
    total = jnp.zeros((slots, width), F32)
    for k in range(len(parts)):
        source = lax.axis_index("y") ^ k
        total += jnp.dot(inner_ref[source, :slots], parts[k][...], preferred_element_type=F32)
    total = jnp.concatenate([total, score_ref[:, : padded - width].astype(F32)], axis=1)
    back_ref[...] = total.reshape(blocks, SLOTS, padded).astype(BF16)


def merge_experts(back_ref, slot_ref, own_ref, keep_ref, pass_ref):
    slots, width = slot_ref.shape[0], own_ref.shape[1]
    back = back_ref[...].astype(F32).reshape(slots, back_ref.shape[2])
    share = slot_ref[...] * back[:, 2 * width : 2 * width + 1]
    share = ROUTE_SCALE * share / jnp.sum(share, axis=0, keepdims=True)
    upper = share.astype(BF16)
    lower = (share - upper.astype(F32)).astype(BF16)
    parts = back[:, : 2 * width].astype(BF16)
    merged = lax.dot_general(upper, parts, TN, preferred_element_type=F32) + lax.dot_general(
        lower, parts, TN, preferred_element_type=F32
    )
    first = lax.axis_index("y") < 4
    near, far = merged[:, :width], merged[:, width:]
    keep_ref[...] = own_ref[...].astype(F32) + jnp.where(first, near, far)
    pass_ref[...] = jnp.where(first, far, near)


def add_attention(parts_ref, keep_ref, passed_ref, out_ref):
    rows, width = out_ref.shape
    blocks, held, lanes = parts_ref.shape
    slices = blocks // 8
    cols = width // 8
    attn = jnp.sum(
        parts_ref[...].astype(F32).reshape(8, slices, held, lanes), axis=1
    ).reshape(8 * held, lanes)
    attn = attn.astype(BF16)
    merged = keep_ref[...] + passed_ref[...]
    lane_in, lane_out = iotas(lanes, width)
    row, lane = iotas(8 * held, width)
    token, entry = iotas(rows, 8 * held)
    for q in range(2):
        spread = one_hot(lane_out % cols + q * (lanes // 2) == lane_in)
        mine = jnp.dot(attn, spread, preferred_element_type=F32)
        mine = jnp.where(lane // cols == row // held, mine, 0.0).astype(BF16)
        pick = one_hot(token == entry % held + q * held)
        merged += jnp.dot(pick, mine, preferred_element_type=F32)
    out_ref[...] = merged.astype(BF16)


def shift(value, axis, k):
    size = lax.axis_size(axis)
    return lax.ppermute(value, axis, [(i, (i + k) % size) for i in range(size)])


def pair_up(value, axis):
    return jnp.stack([value, shift(value, axis, 1)])


def gather(value, axis):
    return [value] + [shift(value, axis, k) for k in range(1, lax.axis_size(axis))]


def swap(value, axis, k):
    return lax.ppermute(value, axis, [(i, i ^ k) for i in range(lax.axis_size(axis))])


def trade(value, axis):
    return [value] + [swap(value, axis, k) for k in range(1, lax.axis_size(axis))]


def on_device(
    hidden,
    norm_gain,
    queries,
    latent_cache,
    lengths,
    expert_ids,
    router,
    w_gate,
    w_up,
    w_down,
    w_uv,
    w_out,
):
    rows, model_width = hidden.shape
    ep_size = lax.axis_size(EP)
    tp_size = lax.axis_size("y")
    slots = ep_size * SLOTS
    width = model_width // tp_size
    hidden_units = w_gate.shape[2]
    heads, latent, value_width = w_uv.shape
    out_cols, depth = w_out.shape[1], w_out.shape[0]
    tp = lax.axis_index("y")

    send, place = kernel_call(
        prepare,
        [((ep_size, SLOTS, model_width), BF16), ((slots, rows), F32)],
        hidden,
        norm_gain,
        expert_ids.T,
        load=(0, 1, 2),
        store=(0, 1),
        vmem=60,
    )
    named_rows = lax.all_to_all(send, EP, 0, 0, tiled=True)

    down = kernel_call(
        split_down,
        [((hidden_units, 2 * width), BF16)] * GROUP,
        w_down[0],
        load=(0,),
        store=(0,),
    )
    down = [down[0]] + [swap(down[k], "y", k) for k in range(1, GROUP)]

    (context,) = kernel_call(
        attend,
        [((tp_size, 2 * heads, latent), BF16)],
        lengths,
        queries,
        jnp.swapaxes(latent_cache, 1, 2),
        smem=(0,),
        load=(0, 1, 2),
    )

    out_other = shift(w_out.T, "zh", 1)
    inner, score = kernel_call(
        lift_experts,
        [((tp_size, slots + 8 * heads, hidden_units), BF16), ((slots, 128), BF16)],
        named_rows,
        w_gate[0],
        w_up[0],
        router,
        context,
        load=(1, 2, 3),
        store=(1,),
        after=down[1:],
    )
    inner = lax.all_to_all(inner, "y", 0, 0, tiled=True)

    out_weights = gather(jnp.stack([w_out.T, out_other]), "x")
    (values,) = kernel_call(
        lift_heads,
        [((rows, depth), BF16)],
        inner,
        w_uv,
        load=(1,),
        after=out_weights[1:],
        flops=10_000_000_000,
    )
    pairs = pair_up(values, "c")
    all_values = trade(pairs, "zl")
    (attn_parts,) = kernel_call(
        project,
        [((8 * tp_size, rows // 2, 128), BF16)],
        *all_values,
        *out_weights,
    )
    attn_parts = lax.all_to_all(attn_parts, ("zl", "c", "y"), 0, 0, tiled=True)

    (back,) = kernel_call(
        lower_experts,
        [((ep_size, SLOTS, PADDED), BF16)],
        inner,
        *down,
        score,
        load=(1, 1 + GROUP),
        after=(values,),
    )
    back = lax.all_to_all(back, EP, 0, 0, tiled=True)
    own = lax.dynamic_slice_in_dim(hidden, tp * width, width, 1)
    keep, passed = kernel_call(
        merge_experts, [((rows, width), F32)] * 2, back, place, own, load=(1,)
    )
    passed = swap(passed, "y", GROUP)
    (out,) = kernel_call(
        add_attention, [((rows, width), BF16)], attn_parts, keep, passed
    )
    return out


def solution(mesh):
    split = Mesh(mesh.devices.reshape(4, 2, 4, 2, 8), ("x", "zh", "zl", "c", "y"))
    return jax.shard_map(
        on_device,
        mesh=split,
        in_specs=(
            P(EP, None),
            P(),
            P(EP + ("y",), None, None),
            P(EP + ("y",), None, None),
            P(EP + ("y",)),
            P(EP, None),
            P(EP, None),
            P(EP, None, "y"),
            P(EP, None, "y"),
            P(EP, "y", None),
            P("y", None, None),
            P("y", EP),
        ),
        out_specs=P(EP, "y"),
        check_vma=False,
    )
```

```python
import jax
import jax.numpy as jnp
from jax import lax
from jax.experimental import pallas as pl
from jax.experimental.pallas import tpu as pltpu
from jax.sharding import Mesh, PartitionSpec as P

ROUTE_SCALE = 2.5
EPSILON = 1e-06
SCORE_SCALE = 192.0 ** (-0.5)
SLOTS = 4
EP = ("x", "zh", "zl", "c")
PADDED = 1024
GROUP = 4
NT = (((1,), (1,)), ((), ()))
TN = (((0,), (0,)), ((), ()))
F32 = jnp.float32
BF16 = jnp.bfloat16


def kernel_call(body, outs, *args, smem=(), load=(), store=(), after=(), flops=0, vmem=16):
    def place(n, moved):
        space = pltpu.HBM if n in moved else pltpu.VMEM
        return pl.BlockSpec(memory_space=space)

    def scratch(a, n):
        return (pltpu.SMEM if n in smem else pltpu.VMEM)(a.shape, a.dtype)

    shapes = [jax.ShapeDtypeStruct(s, d) for s, d in outs]
    count = len(args) + len(after)

    def kernel(*refs):
        given = list(refs[: len(args)])
        made = list(refs[count : count + len(outs)])
        held = list(refs[count + len(outs) :])
        sems = held.pop() if load or store else None
        copies = []
        for i, n in enumerate(load):
            copies.append(pltpu.make_async_copy(given[n], held[i], sems.at[i]))
            copies[-1].start()
            given[n] = held[i]
        for copy in copies:
            copy.wait()
        copies = []
        for i, n in enumerate(store, len(load)):
            copies.append(pltpu.make_async_copy(held[i], made[n], sems.at[i]))
            made[n] = held[i]
        body(*given, *made)
        for copy in copies:
            copy.start()
        for copy in copies:
            copy.wait()

    scratch_shapes = [scratch(args[n], n) for n in load]
    scratch_shapes += [pltpu.VMEM(shapes[n].shape, shapes[n].dtype) for n in store]
    if scratch_shapes:
        scratch_shapes.append(pltpu.SemaphoreType.DMA((len(load) + len(store),)))
    nbytes = sum(a.size * a.dtype.itemsize for a in args)
    return pl.pallas_call(
        kernel,
        out_shape=tuple(shapes),
        in_specs=[place(n, load) for n in range(len(args))]
        + [pl.BlockSpec(memory_space=pl.ANY) for _ in after],
        out_specs=tuple(place(n, store) for n in range(len(outs))),
        scratch_shapes=scratch_shapes,
        compiler_params=pltpu.CompilerParams(vmem_limit_bytes=vmem << 20),
        cost_estimate=pl.CostEstimate(flops=flops, bytes_accessed=nbytes, transcendentals=0),
    )(*args, *after)


def one_hot(condition):
    return condition.astype(F32).astype(BF16)


def iotas(*shape):
    return lax.broadcasted_iota(jnp.int32, shape, 0), lax.broadcasted_iota(jnp.int32, shape, 1)


def prepare(hidden_ref, gain_ref, ids_ref, send_ref, place_ref):
    values = hidden_ref[...].astype(F32)
    factor = lax.rsqrt(jnp.mean(values * values, axis=-1, keepdims=True) + EPSILON)
    gain = gain_ref[...].astype(F32).reshape(1, values.shape[1])
    normalized = (values * factor * gain).astype(BF16)
    slots, rows = place_ref.shape
    slot = lax.broadcasted_iota(jnp.int32, (slots, rows), 0)
    named = jnp.zeros((slots, rows), jnp.bool_)
    for k in range(ids_ref.shape[0]):
        named = named | (ids_ref[k : k + 1, :] == slot // SLOTS)
    named = named.astype(F32)
    earlier = lax.broadcasted_iota(jnp.int32, (rows, rows), 0) < lax.broadcasted_iota(
        jnp.int32, (rows, rows), 1
    )
    rank = jnp.dot(
        named.astype(BF16), earlier.astype(F32).astype(BF16), preferred_element_type=F32
    )
    place = jnp.where(rank == (slot % SLOTS).astype(F32), named, 0.0)
    place_ref[...] = place
    sent = jnp.dot(place.astype(BF16), normalized, preferred_element_type=F32)
    send_ref[...] = sent.reshape(send_ref.shape).astype(BF16)


def attend(lengths_ref, queries_ref, cache_ref, context_ref):
    rows, heads, _ = queries_ref.shape
    groups, _, latent = context_ref.shape
    found = []
    for r in range(rows):
        keys = cache_ref[r]
        scores = jnp.dot(queries_ref[r], keys, preferred_element_type=F32) * SCORE_SCALE
        positions = lax.broadcasted_iota(jnp.int32, scores.shape, 1)
        scores = jnp.where(positions < lengths_ref[r], scores, -1e30)
        raised = jnp.exp(scores - jnp.max(scores, axis=-1, keepdims=True))
        soft = (raised / jnp.sum(raised, axis=-1, keepdims=True)).astype(BF16)
        context = lax.dot_general(soft, keys[:latent], NT, preferred_element_type=F32)
        found.append(context.reshape(groups, heads // groups, latent))
    context_ref[...] = jnp.concatenate(found, axis=1).astype(BF16)


def lift_heads(inner_ref, w_uv_ref, values_ref):
    heads, latent, width = w_uv_ref.shape
    rows = values_ref.shape[0]
    sources, depth, lanes = inner_ref.shape
    share = rows * heads // sources
    first = depth - share * latent // lanes
    context = jnp.concatenate(
        [
            inner_ref[:, first + q * share : first + (q + 1) * share, :]
            for q in range(latent // lanes)
        ],
        axis=2,
    ).reshape(rows * heads, latent)
    token, entry = iotas(rows, rows * heads)
    for h in range(heads):
        lifted = jnp.dot(context, w_uv_ref[h], preferred_element_type=F32).astype(BF16)
        pick = one_hot(entry == token * heads + h)
        mine = jnp.dot(pick, lifted, preferred_element_type=F32).astype(BF16)
        values_ref[:, h * width : (h + 1) * width] = mine


def split_down(w_down_ref, *out_refs):
    group = len(out_refs)
    width = out_refs[0].shape[1] // 2
    for s in range(group):
        for k in range(group):

            @pl.when(lax.axis_index("y") % group ^ k == s)
            def _(s=s, k=k):
                for half in range(2):
                    first = (half * group + s) * width
                    out_refs[k][:, half * width : (half + 1) * width] = w_down_ref[
                        :, first : first + width
                    ]


def mark(out_ref):
    out_ref[...] = jnp.zeros(out_ref.shape, F32)


def project(*refs):
    *parts, out_ref = refs
    blocks, slices = 4, 8
    rows = parts[0].shape[0]
    values = jnp.concatenate([part[...] for part in parts[:blocks]], axis=0)
    first = lax.axis_index("c") == 0
    for k in range(4):
        for j in range(2):
            cols = parts[blocks + k].shape[2]
            mine, other = [
                lax.dot_general(
                    values, parts[blocks + k][j, core], NT, preferred_element_type=F32
                )
                for core in range(2)
            ]
            pad = jnp.zeros((mine.shape[0], 128 - 2 * cols), F32)
            part = jnp.concatenate(
                [jnp.where(first, mine, other), jnp.where(first, other, mine), pad], axis=1
            )
            part = part.reshape(blocks, rows, 128).astype(BF16)
            tp = (lax.axis_index("x") - k + 4) % 4 * 2 + (lax.axis_index("zh") + j) % 2
            for b in range(blocks):
                out_ref[(lax.axis_index("zl") ^ b) * slices + tp] = part[b]


def lift_experts(rows_ref, w_gate_ref, w_up_ref, router_ref, context_ref, inner_ref, score_ref):
    slots, width = score_ref.shape[0], rows_ref.shape[2]
    rows = rows_ref[...].astype(F32).reshape(slots, width).astype(BF16)
    gate = jnp.dot(rows, w_gate_ref[...], preferred_element_type=F32)
    lifted = jnp.dot(rows, w_up_ref[...], preferred_element_type=F32)
    column = jnp.broadcast_to(router_ref[...], (128, width))
    logits = lax.dot_general(rows, column, NT, preferred_element_type=F32)
    inner = (gate / (1.0 + jnp.exp(-gate)) * lifted).astype(BF16)
    copies, share, latent = context_ref.shape
    lanes = inner_ref.shape[2]
    for copy in range(copies):
        inner_ref[copy, :slots] = inner
        for q in range(latent // lanes):
            first = slots + q * share
            inner_ref[copy, first : first + share] = context_ref[
                copy, :, q * lanes : (q + 1) * lanes
            ]
    score_ref[...] = (1.0 / (1.0 + jnp.exp(-logits))).astype(BF16)


def lower_experts(*refs):
    inner_ref, *parts, score_ref, back_ref = refs
    blocks, _, padded = back_ref.shape
    slots = score_ref.shape[0]
    width = parts[0].shape[1]
    total = jnp.zeros((slots, width), F32)
    for k in range(len(parts)):
        source = lax.axis_index("y") ^ k
        total += jnp.dot(inner_ref[source, :slots], parts[k][...], preferred_element_type=F32)
    total = jnp.concatenate([total, score_ref[:, : padded - width].astype(F32)], axis=1)
    back_ref[...] = total.reshape(blocks, SLOTS, padded).astype(BF16)


def merge_experts(back_ref, slot_ref, own_ref, keep_ref, pass_ref):
    slots, width = slot_ref.shape[0], own_ref.shape[1]
    back = back_ref[...].astype(F32).reshape(slots, back_ref.shape[2])
    share = slot_ref[...] * back[:, 2 * width : 2 * width + 1]
    share = ROUTE_SCALE * share / jnp.sum(share, axis=0, keepdims=True)
    upper = share.astype(BF16)
    lower = (share - upper.astype(F32)).astype(BF16)
    parts = back[:, : 2 * width].astype(BF16)
    merged = lax.dot_general(upper, parts, TN, preferred_element_type=F32) + lax.dot_general(
        lower, parts, TN, preferred_element_type=F32
    )
    first = lax.axis_index("y") < 4
    near, far = merged[:, :width], merged[:, width:]
    keep_ref[...] = own_ref[...].astype(F32) + jnp.where(first, near, far)
    pass_ref[...] = jnp.where(first, far, near)


def add_attention(parts_ref, keep_ref, passed_ref, out_ref):
    rows, width = out_ref.shape
    blocks = 4
    slices = parts_ref.shape[0] // blocks
    attn = jnp.concatenate(
        [
            jnp.sum(parts_ref[b * slices : (b + 1) * slices].astype(F32), axis=0)[
                :, : width // blocks
            ]
            for b in range(blocks)
        ],
        axis=1,
    )
    out_ref[...] = (keep_ref[...] + passed_ref[...] + attn).astype(BF16)


def shift(value, axis, k):
    size = lax.axis_size(axis)
    return lax.ppermute(value, axis, [(i, (i + k) % size) for i in range(size)])


def pair_up(value, axis):
    return jnp.stack([value, shift(value, axis, 1)])


def gather(value, axis):
    return [value] + [shift(value, axis, k) for k in range(1, lax.axis_size(axis))]


def swap(value, axis, k):
    return lax.ppermute(value, axis, [(i, i ^ k) for i in range(lax.axis_size(axis))])


def trade(value, axis):
    return [value] + [swap(value, axis, k) for k in range(1, lax.axis_size(axis))]


def on_device(
    hidden,
    norm_gain,
    queries,
    latent_cache,
    lengths,
    expert_ids,
    router,
    w_gate,
    w_up,
    w_down,
    w_uv,
    w_out,
):
    rows, model_width = hidden.shape
    ep_size = lax.axis_size(EP)
    tp_size = lax.axis_size("y")
    slots = ep_size * SLOTS
    width = model_width // tp_size
    hidden_units = w_gate.shape[2]
    heads, latent, value_width = w_uv.shape
    out_cols, depth = w_out.shape[1], w_out.shape[0]
    tp = lax.axis_index("y")

    send, place = kernel_call(
        prepare,
        [((ep_size, SLOTS, model_width), BF16), ((slots, rows), F32)],
        hidden,
        norm_gain,
        expert_ids.T,
        load=(0, 1, 2),
        store=(0, 1),
        vmem=60,
    )
    named_rows = lax.all_to_all(send, EP, 0, 0, tiled=True)

    down = kernel_call(
        split_down,
        [((hidden_units, 2 * width), BF16)] * GROUP,
        w_down[0],
        load=(0,),
        store=(0,),
    )
    down = [down[0]] + [swap(down[k], "y", k) for k in range(1, GROUP)]

    (context,) = kernel_call(
        attend,
        [((tp_size, 2 * heads, latent), BF16)],
        lengths,
        queries,
        jnp.swapaxes(latent_cache, 1, 2),
        smem=(0,),
        load=(0, 1, 2),
        after=down[1:],
    )

    out_pair = pair_up(w_out.T, "c")
    out_other = shift(out_pair, "zh", 1)
    inner, score = kernel_call(
        lift_experts,
        [((tp_size, slots + 8 * heads, hidden_units), BF16), ((slots, 128), BF16)],
        named_rows,
        w_gate[0],
        w_up[0],
        router,
        context,
        load=(1, 2, 3),
        store=(0, 1),
        after=(out_other,),
    )
    inner = lax.all_to_all(inner, "y", 0, 0, tiled=True)

    out_weights = gather(jnp.stack([out_pair, out_other]), "x")
    (values,) = kernel_call(
        lift_heads,
        [((rows, depth), BF16)],
        inner,
        w_uv,
        load=(1,),
        flops=10_000_000_000,
    )

    all_values = trade(values, "zl")
    (gathered,) = kernel_call(
        mark, [((8, 128), F32)], after=out_weights[1:], flops=10_000_000_000
    )
    (attn_parts,) = kernel_call(
        project,
        [((4 * tp_size, rows, 128), BF16)],
        *all_values,
        *out_weights,
        after=(gathered,),
    )
    attn_parts = lax.all_to_all(attn_parts, ("zl", "y"), 0, 0, tiled=True)

    (back,) = kernel_call(
        lower_experts,
        [((ep_size, SLOTS, PADDED), BF16)],
        inner,
        *down,
        score,
        load=(1, 1 + GROUP),
    )
    back = lax.all_to_all(back, EP, 0, 0, tiled=True)
    own = lax.dynamic_slice_in_dim(hidden, tp * width, width, 1)
    keep, passed = kernel_call(
        merge_experts, [((rows, width), F32)] * 2, back, place, own, load=(1,)
    )
    passed = swap(passed, "y", GROUP)
    (out,) = kernel_call(
        add_attention, [((rows, width), BF16)], attn_parts, keep, passed
    )
    return out


def solution(mesh):
    split = Mesh(mesh.devices.reshape(4, 2, 4, 2, 8), ("x", "zh", "zl", "c", "y"))
    return jax.shard_map(
        on_device,
        mesh=split,
        in_specs=(
            P(EP, None),
            P(),
            P(EP + ("y",), None, None),
            P(EP + ("y",), None, None),
            P(EP + ("y",)),
            P(EP, None),
            P(EP, None),
            P(EP, None, "y"),
            P(EP, None, "y"),
            P(EP, "y", None),
            P("y", None, None),
            P("y", EP),
        ),
        out_specs=P(EP, "y"),
        check_vma=False,
    )
```

```python
import jax
import jax.numpy as jnp
from jax import lax
from jax.experimental import pallas as pl
from jax.experimental.pallas import tpu as pltpu
from jax.sharding import Mesh, PartitionSpec as P

ROUTE_SCALE = 2.5
EPSILON = 1e-06
SCORE_SCALE = 192.0 ** (-0.5)
SLOTS = 4
EP = ("x", "zh", "zl", "c")
PADDED = 1024
GROUP = 4
HELD = (0, 3, 5)
NT = (((1,), (1,)), ((), ()))
TN = (((0,), (0,)), ((), ()))
F32 = jnp.float32
BF16 = jnp.bfloat16


def kernel_call(body, outs, *args, smem=(), load=(), store=(), after=(), flops=0, vmem=16):
    def place(n, moved):
        space = pltpu.HBM if n in moved else pltpu.VMEM
        return pl.BlockSpec(memory_space=space)

    def scratch(a, n):
        return (pltpu.SMEM if n in smem else pltpu.VMEM)(a.shape, a.dtype)

    shapes = [jax.ShapeDtypeStruct(s, d) for s, d in outs]
    count = len(args) + len(after)

    def kernel(*refs):
        given = list(refs[: len(args)])
        made = list(refs[count : count + len(outs)])
        held = list(refs[count + len(outs) :])
        sems = held.pop() if load or store else None
        copies = []
        for i, n in enumerate(load):
            copies.append(pltpu.make_async_copy(given[n], held[i], sems.at[i]))
            copies[-1].start()
            given[n] = held[i]
        for copy in copies:
            copy.wait()
        copies = []
        for i, n in enumerate(store, len(load)):
            copies.append(pltpu.make_async_copy(held[i], made[n], sems.at[i]))
            made[n] = held[i]
        body(*given, *made)
        for copy in copies:
            copy.start()
        for copy in copies:
            copy.wait()

    scratch_shapes = [scratch(args[n], n) for n in load]
    scratch_shapes += [pltpu.VMEM(shapes[n].shape, shapes[n].dtype) for n in store]
    if scratch_shapes:
        scratch_shapes.append(pltpu.SemaphoreType.DMA((len(load) + len(store),)))
    nbytes = sum(a.size * a.dtype.itemsize for a in args)
    return pl.pallas_call(
        kernel,
        out_shape=tuple(shapes),
        in_specs=[place(n, load) for n in range(len(args))]
        + [pl.BlockSpec(memory_space=pl.ANY) for _ in after],
        out_specs=tuple(place(n, store) for n in range(len(outs))),
        scratch_shapes=scratch_shapes,
        compiler_params=pltpu.CompilerParams(vmem_limit_bytes=vmem << 20),
        cost_estimate=pl.CostEstimate(flops=flops, bytes_accessed=nbytes, transcendentals=0),
    )(*args, *after)


def one_hot(condition):
    return condition.astype(F32).astype(BF16)


def iotas(*shape):
    return lax.broadcasted_iota(jnp.int32, shape, 0), lax.broadcasted_iota(jnp.int32, shape, 1)


def prepare(hidden_ref, gain_ref, ids_ref, send_ref, place_ref):
    values = hidden_ref[...].astype(F32)
    factor = lax.rsqrt(jnp.mean(values * values, axis=-1, keepdims=True) + EPSILON)
    gain = gain_ref[...].astype(F32).reshape(1, values.shape[1])
    normalized = values * factor * gain
    width = values.shape[1] // 8
    pad = jnp.zeros((values.shape[0], send_ref.shape[2] - 3 * width), F32)
    sent = jnp.zeros((values.shape[0], send_ref.shape[2]), F32)
    for s in range(8):
        taken = [
            normalized[:, (s + k) % 8 * width : ((s + k) % 8 + 1) * width] for k in HELD
        ]
        taken = jnp.concatenate([*taken, pad], axis=1)
        sent = jnp.where(lax.axis_index("y") == s, taken, sent)
    normalized = sent.astype(BF16)
    slots, rows = place_ref.shape
    slot = lax.broadcasted_iota(jnp.int32, (slots, rows), 0)
    named = jnp.zeros((slots, rows), jnp.bool_)
    for k in range(ids_ref.shape[0]):
        named = named | (ids_ref[k : k + 1, :] == slot // SLOTS)
    named = named.astype(F32)
    earlier = lax.broadcasted_iota(jnp.int32, (rows, rows), 0) < lax.broadcasted_iota(
        jnp.int32, (rows, rows), 1
    )
    rank = jnp.dot(
        named.astype(BF16), earlier.astype(F32).astype(BF16), preferred_element_type=F32
    )
    place = jnp.where(rank == (slot % SLOTS).astype(F32), named, 0.0)
    place_ref[...] = place
    sent = jnp.dot(place.astype(BF16), normalized, preferred_element_type=F32)
    send_ref[...] = sent.reshape(send_ref.shape).astype(BF16)


def attend(lengths_ref, queries_ref, cache_ref, context_ref):
    rows, heads, _ = queries_ref.shape
    groups, _, latent = context_ref.shape
    found = []
    for r in range(rows):
        keys = cache_ref[r]
        scores = jnp.dot(queries_ref[r], keys, preferred_element_type=F32) * SCORE_SCALE
        positions = lax.broadcasted_iota(jnp.int32, scores.shape, 1)
        scores = jnp.where(positions < lengths_ref[r], scores, -1e30)
        raised = jnp.exp(scores - jnp.max(scores, axis=-1, keepdims=True))
        soft = (raised / jnp.sum(raised, axis=-1, keepdims=True)).astype(BF16)
        context = lax.dot_general(soft, keys[:latent], NT, preferred_element_type=F32)
        found.append(context.reshape(groups, heads // groups, latent))
    context_ref[...] = jnp.concatenate(found, axis=1).astype(BF16)


def lift_heads(inner_ref, w_uv_ref, values_ref):
    heads, latent, width = w_uv_ref.shape
    rows = values_ref.shape[0]
    sources, depth, lanes = inner_ref.shape
    share = rows * heads // sources
    first = depth - share * latent // lanes
    context = jnp.concatenate(
        [
            inner_ref[:, first + q * share : first + (q + 1) * share, :]
            for q in range(latent // lanes)
        ],
        axis=2,
    ).reshape(rows * heads, latent)
    token, entry = iotas(rows, rows * heads)
    for h in range(heads):
        lifted = jnp.dot(context, w_uv_ref[h], preferred_element_type=F32).astype(BF16)
        pick = one_hot(entry == token * heads + h)
        mine = jnp.dot(pick, lifted, preferred_element_type=F32).astype(BF16)
        values_ref[:, h * width : (h + 1) * width] = mine


def split_down(w_down_ref, *out_refs):
    group = len(out_refs)
    width = out_refs[0].shape[1] // 2
    for s in range(group):
        for k in range(group):

            @pl.when(lax.axis_index("y") % group ^ k == s)
            def _(s=s, k=k):
                for half in range(2):
                    first = (half * group + s) * width
                    out_refs[k][:, half * width : (half + 1) * width] = w_down_ref[
                        :, first : first + width
                    ]


def mark(out_ref):
    out_ref[...] = jnp.zeros(out_ref.shape, F32)


def project(*refs):
    *parts, out_ref = refs
    blocks, slices = 4, 8
    rows = parts[0].shape[0]
    values = jnp.concatenate([part[...] for part in parts[:blocks]], axis=0)
    first = lax.axis_index("c") == 0
    for k in range(4):
        for j in range(2):
            cols = parts[blocks + k].shape[2]
            mine, other = [
                lax.dot_general(
                    values, parts[blocks + k][j, core], NT, preferred_element_type=F32
                )
                for core in range(2)
            ]
            pad = jnp.zeros((mine.shape[0], 128 - 2 * cols), F32)
            part = jnp.concatenate(
                [jnp.where(first, mine, other), jnp.where(first, other, mine), pad], axis=1
            )
            part = part.reshape(blocks, rows, 128).astype(BF16)
            tp = (lax.axis_index("x") - k + 4) % 4 * 2 + (lax.axis_index("zh") + j) % 2
            for b in range(blocks):
                out_ref[(lax.axis_index("zl") ^ b) * slices + tp] = part[b]


def relay(rows_ref, held_ref, up_ref, down_ref):
    slots, width = held_ref.shape
    rows = rows_ref[...].astype(F32).reshape(slots, width)
    held_ref[...] = rows.astype(BF16)
    w = 448
    pad = jnp.zeros((slots, 64), F32)
    up_ref[...] = jnp.concatenate(
        [rows[:, : 2 * w], rows[:, 2 * w + 256 : 3 * w], pad], axis=1
    ).astype(BF16)
    down_ref[...] = jnp.concatenate(
        [rows[:, :w], rows[:, 2 * w : 3 * w], rows[:, w : w + 256]], axis=1
    ).astype(BF16)


def lift_experts(
    held_ref,
    before_ref,
    after_ref,
    w_gate_ref,
    w_up_ref,
    router_ref,
    context_ref,
    inner_ref,
    score_ref,
):
    slots = score_ref.shape[0]
    w = router_ref.shape[1]
    units = w_gate_ref.shape[1]
    tp = lax.axis_index("y")

    def weights(pieces):
        both, scores = [], []
        total = 0
        for k, first, size in pieces:
            s = (tp + k) % 8
            rows = pl.ds(pl.multiple_of(s * w + first, 64), size)
            both.append(jnp.concatenate([w_gate_ref[rows, :], w_up_ref[rows, :]], axis=1))
            scores.append(router_ref[pl.ds(s, 1), :][:, first : first + size])
            total += size
        pad = -total % 128
        if pad:
            both.append(jnp.zeros((pad, 2 * units), BF16))
            scores.append(jnp.zeros((1, pad), F32))
        scores = jnp.concatenate(scores, axis=1)
        return jnp.concatenate(both, axis=0), scores.astype(BF16)

    lifted = jnp.zeros((slots, 2 * units), F32)
    logits = jnp.zeros((slots, 128), F32)
    for ref, pieces in (
        (held_ref, [(k, 0, w) for k in HELD]),
        (before_ref, [(7, 0, w), (2, 0, w), (4, 256, w - 256)]),
        (after_ref, [(1, 0, w), (6, 0, w), (4, 0, 256)]),
    ):
        both, scores = weights(pieces)
        rows = ref[...]
        lifted += jnp.dot(rows, both, preferred_element_type=F32)
        column = jnp.broadcast_to(scores, (128, scores.shape[1]))
        logits += lax.dot_general(rows, column, NT, preferred_element_type=F32)
    gate, lifted = lifted[:, :units], lifted[:, units:]
    inner = (gate / (1.0 + jnp.exp(-gate)) * lifted).astype(BF16)
    copies, share, latent = context_ref.shape
    lanes = inner_ref.shape[2]
    for copy in range(copies):
        inner_ref[copy, :slots] = inner
        for q in range(latent // lanes):
            first = slots + q * share
            inner_ref[copy, first : first + share] = context_ref[
                copy, :, q * lanes : (q + 1) * lanes
            ]
    score_ref[...] = (1.0 / (1.0 + jnp.exp(-logits))).astype(BF16)


def lower_experts(*refs):
    inner_ref, *parts, score_ref, back_ref = refs
    blocks, _, padded = back_ref.shape
    slots = score_ref.shape[0]
    width = parts[0].shape[1]
    total = jnp.zeros((slots, width), F32)
    for k in range(len(parts)):
        source = lax.axis_index("y") ^ k
        total += jnp.dot(inner_ref[source, :slots], parts[k][...], preferred_element_type=F32)
    total = jnp.concatenate([total, score_ref[:, : padded - width].astype(F32)], axis=1)
    back_ref[...] = total.reshape(blocks, SLOTS, padded).astype(BF16)


def merge_experts(back_ref, slot_ref, own_ref, keep_ref, pass_ref):
    slots, width = slot_ref.shape[0], own_ref.shape[1]
    back = back_ref[...].astype(F32).reshape(slots, back_ref.shape[2])
    share = slot_ref[...] * back[:, 2 * width : 2 * width + 1]
    share = ROUTE_SCALE * share / jnp.sum(share, axis=0, keepdims=True)
    upper = share.astype(BF16)
    lower = (share - upper.astype(F32)).astype(BF16)
    parts = back[:, : 2 * width].astype(BF16)
    merged = lax.dot_general(upper, parts, TN, preferred_element_type=F32) + lax.dot_general(
        lower, parts, TN, preferred_element_type=F32
    )
    first = lax.axis_index("y") < 4
    near, far = merged[:, :width], merged[:, width:]
    keep_ref[...] = own_ref[...].astype(F32) + jnp.where(first, near, far)
    pass_ref[...] = jnp.where(first, far, near)


def add_attention(parts_ref, keep_ref, passed_ref, out_ref):
    rows, width = out_ref.shape
    blocks = 4
    slices = parts_ref.shape[0] // blocks
    attn = jnp.concatenate(
        [
            jnp.sum(parts_ref[b * slices : (b + 1) * slices].astype(F32), axis=0)[
                :, : width // blocks
            ]
            for b in range(blocks)
        ],
        axis=1,
    )
    out_ref[...] = (keep_ref[...] + passed_ref[...] + attn).astype(BF16)


def shift(value, axis, k):
    size = lax.axis_size(axis)
    return lax.ppermute(value, axis, [(i, (i + k) % size) for i in range(size)])


def pair_up(value, axis):
    return jnp.stack([value, shift(value, axis, 1)])


def gather(value, axis):
    return [value] + [shift(value, axis, k) for k in range(1, lax.axis_size(axis))]


def swap(value, axis, k):
    return lax.ppermute(value, axis, [(i, i ^ k) for i in range(lax.axis_size(axis))])


def trade(value, axis):
    return [value] + [swap(value, axis, k) for k in range(1, lax.axis_size(axis))]


def on_device(
    hidden,
    norm_gain,
    queries,
    latent_cache,
    lengths,
    expert_ids,
    router,
    w_gate,
    w_up,
    w_down,
    w_uv,
    w_out,
):
    rows, model_width = hidden.shape
    ep_size = lax.axis_size(EP)
    tp_size = lax.axis_size("y")
    slots = ep_size * SLOTS
    width = model_width // tp_size
    hidden_units = w_gate.shape[2]
    heads, latent, value_width = w_uv.shape
    out_cols, depth = w_out.shape[1], w_out.shape[0]
    tp = lax.axis_index("y")

    router_rows = router.reshape(tp_size, width).astype(F32)

    send, place = kernel_call(
        prepare,
        [((ep_size, SLOTS, 3 * width + 64), BF16), ((slots, rows), F32)],
        hidden,
        norm_gain,
        expert_ids.T,
        load=(0, 1, 2),
        store=(0, 1),
        vmem=60,
    )
    named_rows = lax.all_to_all(send, EP, 0, 0, tiled=True)

    down = kernel_call(
        split_down,
        [((hidden_units, 2 * width), BF16)] * GROUP,
        w_down[0],
        load=(0,),
        store=(0,),
    )
    down = [down[0]] + [swap(down[k], "y", k) for k in range(1, GROUP)]

    (context,) = kernel_call(
        attend,
        [((tp_size, 2 * heads, latent), BF16)],
        lengths,
        queries,
        jnp.swapaxes(latent_cache, 1, 2),
        smem=(0,),
        load=(0, 1, 2),
    )

    out_pair = pair_up(w_out.T, "c")
    out_other = shift(out_pair, "zh", 1)
    (crossed,) = kernel_call(mark, [((8, 128), F32)], after=(out_other,))
    (moved,) = kernel_call(mark, [((8, 128), F32)], after=down[1:], flops=20_000_000_000)

    held, up, below = kernel_call(
        relay,
        [
            ((slots, 3 * width + 64), BF16),
            ((slots, 2 * width + 256), BF16),
            ((slots, 2 * width + 256), BF16),
        ],
        named_rows,
        after=(context,),
    )

    inner, score = kernel_call(
        lift_experts,
        [((tp_size, slots + 8 * heads, hidden_units), BF16), ((slots, 128), BF16)],
        held,
        shift(up, "y", 1),
        shift(below, "y", -1),
        w_gate[0],
        w_up[0],
        router_rows,
        context,
        load=(3, 4),
        store=(0, 1),
        after=(moved, crossed),
    )
    inner = lax.all_to_all(inner, "y", 0, 0, tiled=True)

    out_weights = gather(jnp.stack([out_pair, out_other]), "x")
    (values,) = kernel_call(
        lift_heads,
        [((rows, depth), BF16)],
        inner,
        w_uv,
        load=(1,),
        flops=10_000_000_000,
    )

    all_values = trade(values, "zl")
    (gathered,) = kernel_call(
        mark, [((8, 128), F32)], after=out_weights[1:], flops=10_000_000_000
    )
    (attn_parts,) = kernel_call(
        project,
        [((4 * tp_size, rows, 128), BF16)],
        *all_values,
        *out_weights,
        after=(gathered,),
    )
    attn_parts = lax.all_to_all(attn_parts, ("zl", "y"), 0, 0, tiled=True)

    (back,) = kernel_call(
        lower_experts,
        [((ep_size, SLOTS, PADDED), BF16)],
        inner,
        *down,
        score,
        load=(1, 1 + GROUP),
    )
    back = lax.all_to_all(back, EP, 0, 0, tiled=True)
    own = lax.dynamic_slice_in_dim(hidden, tp * width, width, 1)
    keep, passed = kernel_call(
        merge_experts, [((rows, width), F32)] * 2, back, place, own, load=(1,)
    )
    passed = swap(passed, "y", GROUP)
    (out,) = kernel_call(
        add_attention, [((rows, width), BF16)], attn_parts, keep, passed
    )
    return out


def solution(mesh):
    split = Mesh(mesh.devices.reshape(4, 2, 4, 2, 8), ("x", "zh", "zl", "c", "y"))
    return jax.shard_map(
        on_device,
        mesh=split,
        in_specs=(
            P(EP, None),
            P(),
            P(EP + ("y",), None, None),
            P(EP + ("y",), None, None),
            P(EP + ("y",)),
            P(EP, None),
            P(EP, None),
            P(EP, None, "y"),
            P(EP, None, "y"),
            P(EP, "y", None),
            P("y", None, None),
            P("y", EP),
        ),
        out_specs=P(EP, "y"),
        check_vma=False,
    )
```

```python
import jax
import jax.numpy as jnp
from jax import lax
from jax.experimental import pallas as pl
from jax.experimental.pallas import tpu as pltpu
from jax.sharding import Mesh, PartitionSpec as P

ROUTE_SCALE = 2.5
EPSILON = 1e-06
SCORE_SCALE = 192.0 ** (-0.5)
SLOTS = 4
EP = ("x", "zh", "zl", "c")
PADDED = 1024
GROUP = 4
HELD = (0, 3, 5)
NT = (((1,), (1,)), ((), ()))
TN = (((0,), (0,)), ((), ()))
F32 = jnp.float32
BF16 = jnp.bfloat16


def kernel_call(body, outs, *args, smem=(), load=(), store=(), after=(), flops=0, vmem=16):
    def place(n, moved):
        space = pltpu.HBM if n in moved else pltpu.VMEM
        return pl.BlockSpec(memory_space=space)

    def scratch(a, n):
        return (pltpu.SMEM if n in smem else pltpu.VMEM)(a.shape, a.dtype)

    shapes = [jax.ShapeDtypeStruct(s, d) for s, d in outs]
    count = len(args) + len(after)

    def kernel(*refs):
        given = list(refs[: len(args)])
        made = list(refs[count : count + len(outs)])
        held = list(refs[count + len(outs) :])
        sems = held.pop() if load or store else None
        copies = []
        for i, n in enumerate(load):
            copies.append(pltpu.make_async_copy(given[n], held[i], sems.at[i]))
            copies[-1].start()
            given[n] = held[i]
        for copy in copies:
            copy.wait()
        copies = []
        for i, n in enumerate(store, len(load)):
            copies.append(pltpu.make_async_copy(held[i], made[n], sems.at[i]))
            made[n] = held[i]
        body(*given, *made)
        for copy in copies:
            copy.start()
        for copy in copies:
            copy.wait()

    scratch_shapes = [scratch(args[n], n) for n in load]
    scratch_shapes += [pltpu.VMEM(shapes[n].shape, shapes[n].dtype) for n in store]
    if scratch_shapes:
        scratch_shapes.append(pltpu.SemaphoreType.DMA((len(load) + len(store),)))
    nbytes = sum(a.size * a.dtype.itemsize for a in args)
    return pl.pallas_call(
        kernel,
        out_shape=tuple(shapes),
        in_specs=[place(n, load) for n in range(len(args))]
        + [pl.BlockSpec(memory_space=pl.ANY) for _ in after],
        out_specs=tuple(place(n, store) for n in range(len(outs))),
        scratch_shapes=scratch_shapes,
        compiler_params=pltpu.CompilerParams(vmem_limit_bytes=vmem << 20),
        cost_estimate=pl.CostEstimate(flops=flops, bytes_accessed=nbytes, transcendentals=0),
    )(*args, *after)


def one_hot(condition):
    return condition.astype(F32).astype(BF16)


def iotas(*shape):
    return lax.broadcasted_iota(jnp.int32, shape, 0), lax.broadcasted_iota(jnp.int32, shape, 1)


def prepare(hidden_ref, gain_ref, ids_ref, send_ref, place_ref):
    values = hidden_ref[...].astype(F32)
    factor = lax.rsqrt(jnp.mean(values * values, axis=-1, keepdims=True) + EPSILON)
    gain = gain_ref[...].astype(F32).reshape(1, values.shape[1])
    normalized = values * factor * gain
    width = values.shape[1] // 8
    pad = jnp.zeros((values.shape[0], send_ref.shape[2] - 3 * width), F32)
    sent = jnp.zeros((values.shape[0], send_ref.shape[2]), F32)
    for s in range(8):
        taken = [
            normalized[:, (s + k) % 8 * width : ((s + k) % 8 + 1) * width] for k in HELD
        ]
        taken = jnp.concatenate([*taken, pad], axis=1)
        sent = jnp.where(lax.axis_index("y") == s, taken, sent)
    normalized = sent.astype(BF16)
    slots, rows = place_ref.shape
    slot = lax.broadcasted_iota(jnp.int32, (slots, rows), 0)
    named = jnp.zeros((slots, rows), jnp.bool_)
    for k in range(ids_ref.shape[0]):
        named = named | (ids_ref[k : k + 1, :] == slot // SLOTS)
    named = named.astype(F32)
    earlier = lax.broadcasted_iota(jnp.int32, (rows, rows), 0) < lax.broadcasted_iota(
        jnp.int32, (rows, rows), 1
    )
    rank = jnp.dot(
        named.astype(BF16), earlier.astype(F32).astype(BF16), preferred_element_type=F32
    )
    place = jnp.where(rank == (slot % SLOTS).astype(F32), named, 0.0)
    place_ref[...] = place
    sent = jnp.dot(place.astype(BF16), normalized, preferred_element_type=F32)
    send_ref[...] = sent.reshape(send_ref.shape).astype(BF16)


def attend(lengths_ref, queries_ref, cache_ref, context_ref):
    rows, heads, _ = queries_ref.shape
    groups, _, latent = context_ref.shape
    found = []
    for r in range(rows):
        keys = cache_ref[r]
        scores = jnp.dot(queries_ref[r], keys, preferred_element_type=F32) * SCORE_SCALE
        positions = lax.broadcasted_iota(jnp.int32, scores.shape, 1)
        scores = jnp.where(positions < lengths_ref[r], scores, -1e30)
        raised = jnp.exp(scores - jnp.max(scores, axis=-1, keepdims=True))
        soft = (raised / jnp.sum(raised, axis=-1, keepdims=True)).astype(BF16)
        context = lax.dot_general(soft, keys[:latent], NT, preferred_element_type=F32)
        found.append(context.reshape(groups, heads // groups, latent))
    context_ref[...] = jnp.concatenate(found, axis=1).astype(BF16)


def lift_heads(context_ref, w_uv_ref, values_ref):
    heads, latent, width = w_uv_ref.shape
    rows = values_ref.shape[0]
    context = context_ref[...].reshape(rows * heads, latent)
    token, entry = iotas(rows, rows * heads)
    for h in range(heads):
        lifted = jnp.dot(context, w_uv_ref[h], preferred_element_type=F32).astype(BF16)
        pick = one_hot(entry == token * heads + h)
        mine = jnp.dot(pick, lifted, preferred_element_type=F32).astype(BF16)
        values_ref[:, h * width : (h + 1) * width] = mine


def split_down(w_down_ref, *out_refs):
    group = len(out_refs)
    width = out_refs[0].shape[1] // 2
    for s in range(group):
        for k in range(group):

            @pl.when(lax.axis_index("y") % group ^ k == s)
            def _(s=s, k=k):
                for half in range(2):
                    first = (half * group + s) * width
                    out_refs[k][:, half * width : (half + 1) * width] = w_down_ref[
                        :, first : first + width
                    ]


def mark(out_ref):
    out_ref[...] = jnp.zeros(out_ref.shape, F32)


def project(*refs):
    *parts, out_ref = refs
    blocks, slices = 4, 8
    rows = parts[0].shape[0]
    values = jnp.concatenate([part[...] for part in parts[:blocks]], axis=0)
    first = lax.axis_index("c") == 0
    for k in range(4):
        for j in range(2):
            cols = parts[blocks + k].shape[2]
            mine, other = [
                lax.dot_general(
                    values, parts[blocks + k][j, core], NT, preferred_element_type=F32
                )
                for core in range(2)
            ]
            pad = jnp.zeros((mine.shape[0], 128 - 2 * cols), F32)
            part = jnp.concatenate(
                [jnp.where(first, mine, other), jnp.where(first, other, mine), pad], axis=1
            )
            part = part.reshape(blocks, rows, 128).astype(BF16)
            tp = (lax.axis_index("x") - k + 4) % 4 * 2 + (lax.axis_index("zh") + j) % 2
            for b in range(blocks):
                out_ref[(lax.axis_index("zl") ^ b) * slices + tp] = part[b]


def relay(rows_ref, held_ref, up_ref, down_ref):
    slots, width = held_ref.shape
    rows = rows_ref[...].astype(F32).reshape(slots, width)
    held_ref[...] = rows.astype(BF16)
    w = 448
    pad = jnp.zeros((slots, 64), F32)
    up_ref[...] = jnp.concatenate(
        [rows[:, : 2 * w], rows[:, 2 * w + 256 : 3 * w], pad], axis=1
    ).astype(BF16)
    down_ref[...] = jnp.concatenate(
        [rows[:, :w], rows[:, 2 * w : 3 * w], rows[:, w : w + 256]], axis=1
    ).astype(BF16)


def lift_experts(
    held_ref,
    before_ref,
    after_ref,
    w_gate_ref,
    w_up_ref,
    router_ref,
    inner_ref,
    score_ref,
):
    slots = score_ref.shape[0]
    w = router_ref.shape[1]
    units = w_gate_ref.shape[1]
    tp = lax.axis_index("y")

    def weights(pieces):
        both, scores = [], []
        total = 0
        for k, first, size in pieces:
            s = (tp + k) % 8
            rows = pl.ds(pl.multiple_of(s * w + first, 64), size)
            both.append(jnp.concatenate([w_gate_ref[rows, :], w_up_ref[rows, :]], axis=1))
            scores.append(router_ref[pl.ds(s, 1), :][:, first : first + size])
            total += size
        pad = -total % 128
        if pad:
            both.append(jnp.zeros((pad, 2 * units), BF16))
            scores.append(jnp.zeros((1, pad), F32))
        scores = jnp.concatenate(scores, axis=1)
        return jnp.concatenate(both, axis=0), scores.astype(BF16)

    lifted = jnp.zeros((slots, 2 * units), F32)
    logits = jnp.zeros((slots, 128), F32)
    for ref, pieces in (
        (held_ref, [(k, 0, w) for k in HELD]),
        (before_ref, [(7, 0, w), (2, 0, w), (4, 256, w - 256)]),
        (after_ref, [(1, 0, w), (6, 0, w), (4, 0, 256)]),
    ):
        both, scores = weights(pieces)
        rows = ref[...]
        lifted += jnp.dot(rows, both, preferred_element_type=F32)
        column = jnp.broadcast_to(scores, (128, scores.shape[1]))
        logits += lax.dot_general(rows, column, NT, preferred_element_type=F32)
    gate, lifted = lifted[:, :units], lifted[:, units:]
    inner = (gate / (1.0 + jnp.exp(-gate)) * lifted).astype(BF16)
    for copy in range(inner_ref.shape[0]):
        inner_ref[copy] = inner
    score_ref[...] = (1.0 / (1.0 + jnp.exp(-logits))).astype(BF16)


def lower_experts(*refs):
    inner_ref, *parts, score_ref, back_ref = refs
    blocks, _, padded = back_ref.shape
    slots = score_ref.shape[0]
    width = parts[0].shape[1]
    total = jnp.zeros((slots, width), F32)
    for k in range(len(parts)):
        source = lax.axis_index("y") % len(parts) ^ k
        total += jnp.dot(inner_ref[source], parts[k][...], preferred_element_type=F32)
    total = jnp.concatenate([total, score_ref[:, : padded - width].astype(F32)], axis=1)
    back_ref[...] = total.reshape(blocks, SLOTS, padded).astype(BF16)


def merge_experts(back_ref, slot_ref, own_ref, keep_ref, pass_ref):
    slots, width = slot_ref.shape[0], own_ref.shape[1]
    back = back_ref[...].astype(F32).reshape(slots, back_ref.shape[2])
    share = slot_ref[...] * back[:, 2 * width : 2 * width + 1]
    share = ROUTE_SCALE * share / jnp.sum(share, axis=0, keepdims=True)
    upper = share.astype(BF16)
    lower = (share - upper.astype(F32)).astype(BF16)
    parts = back[:, : 2 * width].astype(BF16)
    merged = lax.dot_general(upper, parts, TN, preferred_element_type=F32) + lax.dot_general(
        lower, parts, TN, preferred_element_type=F32
    )
    first = lax.axis_index("y") < 4
    near, far = merged[:, :width], merged[:, width:]
    keep_ref[...] = own_ref[...].astype(F32) + jnp.where(first, near, far)
    pass_ref[...] = jnp.where(first, far, near)


def add_attention(parts_ref, keep_ref, passed_ref, out_ref):
    rows, width = out_ref.shape
    blocks = 4
    slices = parts_ref.shape[0] // blocks
    attn = jnp.concatenate(
        [
            jnp.sum(parts_ref[b * slices : (b + 1) * slices].astype(F32), axis=0)[
                :, : width // blocks
            ]
            for b in range(blocks)
        ],
        axis=1,
    )
    out_ref[...] = (keep_ref[...] + passed_ref[...] + attn).astype(BF16)


def shift(value, axis, k):
    size = lax.axis_size(axis)
    return lax.ppermute(value, axis, [(i, (i + k) % size) for i in range(size)])


def pair_up(value, axis):
    return jnp.stack([value, shift(value, axis, 1)])


def gather(value, axis):
    return [value] + [shift(value, axis, k) for k in range(1, lax.axis_size(axis))]


def swap(value, axis, k):
    return lax.ppermute(value, axis, [(i, i ^ k) for i in range(lax.axis_size(axis))])


def trade(value, axis):
    return [value] + [swap(value, axis, k) for k in range(1, lax.axis_size(axis))]


def on_device(
    hidden,
    norm_gain,
    queries,
    latent_cache,
    lengths,
    expert_ids,
    router,
    w_gate,
    w_up,
    w_down,
    w_uv,
    w_out,
):
    rows, model_width = hidden.shape
    ep_size = lax.axis_size(EP)
    tp_size = lax.axis_size("y")
    slots = ep_size * SLOTS
    width = model_width // tp_size
    hidden_units = w_gate.shape[2]
    heads, latent, value_width = w_uv.shape
    out_cols, depth = w_out.shape[1], w_out.shape[0]
    tp = lax.axis_index("y")

    router_rows = router.reshape(tp_size, width).astype(F32)

    send, place = kernel_call(
        prepare,
        [((ep_size, SLOTS, 3 * width + 64), BF16), ((slots, rows), F32)],
        hidden,
        norm_gain,
        expert_ids.T,
        load=(0, 1, 2),
        store=(0, 1),
        vmem=60,
    )
    named_rows = lax.all_to_all(send, EP, 0, 0, tiled=True)

    down = kernel_call(
        split_down,
        [((hidden_units, 2 * width), BF16)] * GROUP,
        w_down[0],
        load=(0,),
        store=(0,),
    )
    down = [down[0]] + [swap(down[k], "y", k) for k in range(1, GROUP)]

    (context,) = kernel_call(
        attend,
        [((tp_size, 2 * heads, latent), BF16)],
        lengths,
        queries,
        jnp.swapaxes(latent_cache, 1, 2),
        smem=(0,),
        load=(0, 1, 2),
        after=(place,),
    )

    (moved,) = kernel_call(mark, [((8, 128), F32)], after=down[1:], flops=20_000_000_000)

    held, up, below = kernel_call(
        relay,
        [
            ((slots, 3 * width + 64), BF16),
            ((slots, 2 * width + 256), BF16),
            ((slots, 2 * width + 256), BF16),
        ],
        named_rows,
        after=(context,),
    )

    contexts = lax.all_to_all(context, "y", 0, 0, tiled=True)
    out_pair = pair_up(w_out.T, "c")
    out_other = shift(out_pair, "zh", 1)

    (crossed,) = kernel_call(mark, [((8, 128), F32)], after=(out_other,))

    inner, score = kernel_call(
        lift_experts,
        [((GROUP, slots, hidden_units), BF16), ((slots, 128), BF16)],
        held,
        shift(up, "y", 1),
        shift(below, "y", -1),
        w_gate[0],
        w_up[0],
        router_rows,
        load=(3, 4),
        store=(0, 1),
        after=(moved, crossed),
    )
    groups = [list(range(i, i + GROUP)) for i in range(0, tp_size, GROUP)]
    inner = lax.all_to_all(inner, "y", 0, 0, tiled=True, axis_index_groups=groups)

    out_weights = gather(jnp.stack([out_pair, out_other]), "x")
    (values,) = kernel_call(
        lift_heads,
        [((rows, depth), BF16)],
        contexts,
        w_uv,
        load=(1,),
        flops=10_000_000_000,
    )

    all_values = trade(values, "zl")
    (gathered,) = kernel_call(
        mark, [((8, 128), F32)], after=out_weights[1:], flops=15_000_000_000
    )
    (attn_parts,) = kernel_call(
        project,
        [((4 * tp_size, rows, 128), BF16)],
        *all_values,
        *out_weights,
        after=(gathered,),
    )
    attn_parts = lax.all_to_all(attn_parts, ("zl", "y"), 0, 0, tiled=True)

    (back,) = kernel_call(
        lower_experts,
        [((ep_size, SLOTS, PADDED), BF16)],
        inner,
        *down,
        score,
        load=(1, 1 + GROUP),
        after=(contexts,),
    )
    back = lax.all_to_all(back, EP, 0, 0, tiled=True)
    own = lax.dynamic_slice_in_dim(hidden, tp * width, width, 1)
    keep, passed = kernel_call(
        merge_experts, [((rows, width), F32)] * 2, back, place, own, load=(1,)
    )
    passed = swap(passed, "y", GROUP)
    (out,) = kernel_call(
        add_attention, [((rows, width), BF16)], attn_parts, keep, passed
    )
    return out


def solution(mesh):
    split = Mesh(mesh.devices.reshape(4, 2, 4, 2, 8), ("x", "zh", "zl", "c", "y"))
    return jax.shard_map(
        on_device,
        mesh=split,
        in_specs=(
            P(EP, None),
            P(),
            P(EP + ("y",), None, None),
            P(EP + ("y",), None, None),
            P(EP + ("y",)),
            P(EP, None),
            P(EP, None),
            P(EP, None, "y"),
            P(EP, None, "y"),
            P(EP, "y", None),
            P("y", None, None),
            P("y", EP),
        ),
        out_specs=P(EP, "y"),
        check_vma=False,
    )
```

```python
import jax
import jax.numpy as jnp
from jax import lax
from jax.experimental import pallas as pl
from jax.experimental.pallas import tpu as pltpu
from jax.sharding import Mesh, PartitionSpec as P

ROUTE_SCALE = 2.5
EPSILON = 1e-06
SCORE_SCALE = 192.0 ** (-0.5)
SLOTS = 4
EP = ("x", "zh", "zl", "c")
PADDED = 1024
GROUP = 4
HELD = (0, 3, 5)
NT = (((1,), (1,)), ((), ()))
TN = (((0,), (0,)), ((), ()))
F32 = jnp.float32
BF16 = jnp.bfloat16


def kernel_call(body, outs, *args, smem=(), load=(), store=(), after=(), flops=0, vmem=16):
    def place(n, moved):
        space = pltpu.HBM if n in moved else pltpu.VMEM
        return pl.BlockSpec(memory_space=space)

    def scratch(a, n):
        return (pltpu.SMEM if n in smem else pltpu.VMEM)(a.shape, a.dtype)

    shapes = [jax.ShapeDtypeStruct(s, d) for s, d in outs]
    count = len(args) + len(after)

    def kernel(*refs):
        given = list(refs[: len(args)])
        made = list(refs[count : count + len(outs)])
        held = list(refs[count + len(outs) :])
        sems = held.pop() if load or store else None
        copies = []
        for i, n in enumerate(load):
            copies.append(pltpu.make_async_copy(given[n], held[i], sems.at[i]))
            copies[-1].start()
            given[n] = held[i]
        for copy in copies:
            copy.wait()
        copies = []
        for i, n in enumerate(store, len(load)):
            copies.append(pltpu.make_async_copy(held[i], made[n], sems.at[i]))
            made[n] = held[i]
        body(*given, *made)
        for copy in copies:
            copy.start()
        for copy in copies:
            copy.wait()

    scratch_shapes = [scratch(args[n], n) for n in load]
    scratch_shapes += [pltpu.VMEM(shapes[n].shape, shapes[n].dtype) for n in store]
    if scratch_shapes:
        scratch_shapes.append(pltpu.SemaphoreType.DMA((len(load) + len(store),)))
    nbytes = sum(a.size * a.dtype.itemsize for a in args)
    return pl.pallas_call(
        kernel,
        out_shape=tuple(shapes),
        in_specs=[place(n, load) for n in range(len(args))]
        + [pl.BlockSpec(memory_space=pl.ANY) for _ in after],
        out_specs=tuple(place(n, store) for n in range(len(outs))),
        scratch_shapes=scratch_shapes,
        compiler_params=pltpu.CompilerParams(vmem_limit_bytes=vmem << 20),
        cost_estimate=pl.CostEstimate(flops=flops, bytes_accessed=nbytes, transcendentals=0),
    )(*args, *after)


def one_hot(condition):
    return condition.astype(F32).astype(BF16)


def iotas(*shape):
    return lax.broadcasted_iota(jnp.int32, shape, 0), lax.broadcasted_iota(jnp.int32, shape, 1)


def prepare(hidden_ref, gain_ref, ids_ref, send_ref, place_ref, own_ref):
    values = hidden_ref[...].astype(F32)
    factor = lax.rsqrt(jnp.mean(values * values, axis=-1, keepdims=True) + EPSILON)
    gain = gain_ref[...].astype(F32).reshape(1, values.shape[1])
    normalized = values * factor * gain
    width = values.shape[1] // 8
    pad = jnp.zeros((values.shape[0], send_ref.shape[2] - 3 * width), F32)
    sent = jnp.zeros((values.shape[0], send_ref.shape[2]), F32)
    own = jnp.zeros((values.shape[0], width), F32)
    for s in range(8):
        here = lax.axis_index("y") == s
        own = jnp.where(here, values[:, s * width : (s + 1) * width], own)
        taken = [
            normalized[:, (s + k) % 8 * width : ((s + k) % 8 + 1) * width] for k in HELD
        ]
        taken = jnp.concatenate([*taken, pad], axis=1)
        sent = jnp.where(here, taken, sent)
    own_ref[...] = own
    normalized = sent.astype(BF16)
    slots, rows = place_ref.shape
    slot = lax.broadcasted_iota(jnp.int32, (slots, rows), 0)
    named = jnp.zeros((slots, rows), jnp.bool_)
    for k in range(ids_ref.shape[0]):
        named = named | (ids_ref[k : k + 1, :] == slot // SLOTS)
    named = named.astype(F32)
    earlier = lax.broadcasted_iota(jnp.int32, (rows, rows), 0) < lax.broadcasted_iota(
        jnp.int32, (rows, rows), 1
    )
    rank = jnp.dot(
        named.astype(BF16), earlier.astype(F32).astype(BF16), preferred_element_type=F32
    )
    place = jnp.where(rank == (slot % SLOTS).astype(F32), named, 0.0)
    place_ref[...] = place
    sent = jnp.dot(place.astype(BF16), normalized, preferred_element_type=F32)
    send_ref[...] = sent.reshape(send_ref.shape).astype(BF16)


def attend(lengths_ref, queries_ref, cache_ref, context_ref):
    rows, heads, _ = queries_ref.shape
    groups, _, latent = context_ref.shape
    found = []
    for r in range(rows):
        keys = cache_ref[r]
        scores = jnp.dot(queries_ref[r], keys, preferred_element_type=F32) * SCORE_SCALE
        positions = lax.broadcasted_iota(jnp.int32, scores.shape, 1)
        scores = jnp.where(positions < lengths_ref[r], scores, -1e30)
        raised = jnp.exp(scores - jnp.max(scores, axis=-1, keepdims=True))
        soft = (raised / jnp.sum(raised, axis=-1, keepdims=True)).astype(BF16)
        context = lax.dot_general(soft, keys[:latent], NT, preferred_element_type=F32)
        found.append(context.reshape(groups, heads // groups, latent))
    context_ref[...] = jnp.concatenate(found, axis=1).astype(BF16)


def lift_heads(context_ref, w_uv_ref, values_ref):
    heads, latent, width = w_uv_ref.shape
    rows = values_ref.shape[0]
    context = context_ref[...].reshape(rows * heads, latent)
    token, entry = iotas(rows, rows * heads)
    for h in range(heads):
        lifted = jnp.dot(context, w_uv_ref[h], preferred_element_type=F32).astype(BF16)
        pick = one_hot(entry == token * heads + h)
        mine = jnp.dot(pick, lifted, preferred_element_type=F32).astype(BF16)
        values_ref[:, h * width : (h + 1) * width] = mine


def split_down(w_down_ref, *out_refs):
    width = out_refs[0].shape[1] // 2
    for d in range(8):
        for k in range(len(out_refs)):

            @pl.when(lax.axis_index("y") ^ k == d)
            def _(d=d, k=k):
                for half, s in enumerate((d, 7 - d)):
                    out_refs[k][:, half * width : (half + 1) * width] = w_down_ref[
                        :, s * width : (s + 1) * width
                    ]


def mark(out_ref):
    out_ref[...] = jnp.zeros(out_ref.shape, F32)


def project(*refs):
    *parts, out_ref = refs
    blocks, slices = 4, 8
    rows = parts[0].shape[0]
    values = jnp.concatenate([part[...] for part in parts[:blocks]], axis=0)
    first = lax.axis_index("c") == 0
    for k in range(4):
        for j in range(2):
            cols = parts[blocks + k].shape[2]
            mine, other = [
                lax.dot_general(
                    values, parts[blocks + k][j, core], NT, preferred_element_type=F32
                )
                for core in range(2)
            ]
            pad = jnp.zeros((mine.shape[0], 128 - 2 * cols), F32)
            part = jnp.concatenate(
                [jnp.where(first, mine, other), jnp.where(first, other, mine), pad], axis=1
            )
            part = part.reshape(blocks, rows, 128).astype(BF16)
            tp = (lax.axis_index("x") - k + 4) % 4 * 2 + (lax.axis_index("zh") + j) % 2
            for b in range(blocks):
                out_ref[(lax.axis_index("zl") ^ b) * slices + tp] = part[b]


def relay(rows_ref, held_ref, up_ref, down_ref):
    slots, width = held_ref.shape
    rows = rows_ref[...].astype(F32).reshape(slots, width)
    held_ref[...] = rows.astype(BF16)
    w = 448
    pad = jnp.zeros((slots, 64), F32)
    up_ref[...] = jnp.concatenate(
        [rows[:, : 2 * w], rows[:, 2 * w + 256 : 3 * w], pad], axis=1
    ).astype(BF16)
    down_ref[...] = jnp.concatenate(
        [rows[:, :w], rows[:, 2 * w : 3 * w], rows[:, w : w + 256]], axis=1
    ).astype(BF16)


def lift_experts(
    held_ref,
    before_ref,
    after_ref,
    w_gate_ref,
    w_up_ref,
    router_ref,
    inner_ref,
    score_ref,
):
    slots = score_ref.shape[0]
    w = router_ref.shape[1]
    units = w_gate_ref.shape[1]
    tp = lax.axis_index("y")

    def weights(pieces):
        both, scores = [], []
        total = 0
        for k, first, size in pieces:
            s = (tp + k) % 8
            rows = pl.ds(pl.multiple_of(s * w + first, 64), size)
            both.append(jnp.concatenate([w_gate_ref[rows, :], w_up_ref[rows, :]], axis=1))
            scores.append(router_ref[pl.ds(s, 1), :][:, first : first + size])
            total += size
        pad = -total % 128
        if pad:
            both.append(jnp.zeros((pad, 2 * units), BF16))
            scores.append(jnp.zeros((1, pad), F32))
        scores = jnp.concatenate(scores, axis=1)
        return jnp.concatenate(both, axis=0), scores.astype(BF16)

    lifted = jnp.zeros((slots, 2 * units), F32)
    logits = jnp.zeros((slots, 128), F32)
    for ref, pieces in (
        (held_ref, [(k, 0, w) for k in HELD]),
        (before_ref, [(7, 0, w), (2, 0, w), (4, 256, w - 256)]),
        (after_ref, [(1, 0, w), (6, 0, w), (4, 0, 256)]),
    ):
        both, scores = weights(pieces)
        rows = ref[...]
        lifted += jnp.dot(rows, both, preferred_element_type=F32)
        column = jnp.broadcast_to(scores, (128, scores.shape[1]))
        logits += lax.dot_general(rows, column, NT, preferred_element_type=F32)
    gate, lifted = lifted[:, :units], lifted[:, units:]
    inner = (gate / (1.0 + jnp.exp(-gate)) * lifted).astype(BF16)
    for copy in range(inner_ref.shape[0]):
        inner_ref[copy] = inner
    score_ref[...] = (1.0 / (1.0 + jnp.exp(-logits))).astype(BF16)


def lower_experts(*refs):
    inner_ref, *parts, score_ref, back_ref = refs
    blocks, _, padded = back_ref.shape
    slots = score_ref.shape[0]
    width = parts[0].shape[1]
    total = jnp.zeros((slots, width), F32)
    for k in range(len(parts)):
        source = lax.axis_index("y") % len(parts) ^ k
        total += jnp.dot(inner_ref[source], parts[k][...], preferred_element_type=F32)
    total = jnp.concatenate([total, score_ref[:, : padded - width].astype(F32)], axis=1)
    back_ref[...] = total.reshape(blocks, SLOTS, padded).astype(BF16)


def merge_experts(back_ref, slot_ref, own_ref, keep_ref, pass_ref):
    slots, width = slot_ref.shape[0], own_ref.shape[1]
    back = back_ref[...].astype(F32).reshape(slots, back_ref.shape[2])
    share = slot_ref[...] * back[:, 2 * width : 2 * width + 1]
    share = ROUTE_SCALE * share / jnp.sum(share, axis=0, keepdims=True)
    upper = share.astype(BF16)
    lower = (share - upper.astype(F32)).astype(BF16)
    parts = back[:, : 2 * width].astype(BF16)
    merged = lax.dot_general(upper, parts, TN, preferred_element_type=F32) + lax.dot_general(
        lower, parts, TN, preferred_element_type=F32
    )
    keep_ref[...] = own_ref[...] + merged[:, :width]
    pass_ref[...] = merged[:, width:]


def add_attention(parts_ref, keep_ref, passed_ref, out_ref):
    rows, width = out_ref.shape
    blocks = 4
    slices = parts_ref.shape[0] // blocks
    sums = [
        jnp.sum(parts_ref[b * slices : (b + 1) * slices].astype(F32), axis=0)[
            :, : width // blocks
        ]
        for b in range(blocks)
    ]
    straight = lax.axis_index("y") % 2 == lax.axis_index("zh")
    attn = jnp.where(
        straight, jnp.concatenate(sums, axis=1), jnp.concatenate(sums[::-1], axis=1)
    )
    out_ref[...] = (keep_ref[...] + passed_ref[...] + attn).astype(BF16)


def shift(value, axis, k):
    size = lax.axis_size(axis)
    return lax.ppermute(value, axis, [(i, (i + k) % size) for i in range(size)])


def pair_up(value, axis):
    return jnp.stack([value, shift(value, axis, 1)])


def gather(value, axis):
    return [value] + [shift(value, axis, k) for k in range(1, lax.axis_size(axis))]


def swap(value, axis, k):
    return lax.ppermute(value, axis, [(i, i ^ k) for i in range(lax.axis_size(axis))])


def mirror(value, axis):
    size = lax.axis_size(axis)
    return lax.ppermute(value, axis, [(i, size - 1 - i) for i in range(size)])


def trade(value, axis):
    return [value] + [swap(value, axis, k) for k in range(1, lax.axis_size(axis))]


def on_device(
    hidden,
    norm_gain,
    queries,
    latent_cache,
    lengths,
    expert_ids,
    router,
    w_gate,
    w_up,
    w_down,
    w_uv,
    w_out,
):
    rows, model_width = hidden.shape
    ep_size = lax.axis_size(EP)
    tp_size = lax.axis_size("y")
    slots = ep_size * SLOTS
    width = model_width // tp_size
    hidden_units = w_gate.shape[2]
    heads, latent, value_width = w_uv.shape
    out_cols, depth = w_out.shape[1], w_out.shape[0]
    router_rows = router.reshape(tp_size, width).astype(F32)

    send, place, own = kernel_call(
        prepare,
        [
            ((ep_size, SLOTS, 3 * width + 64), BF16),
            ((slots, rows), F32),
            ((rows, width), F32),
        ],
        hidden,
        norm_gain,
        expert_ids.T,
        load=(0, 1, 2),
        store=(0, 1, 2),
        vmem=60,
    )
    named_rows = lax.all_to_all(send, EP, 0, 0, tiled=True)

    down = kernel_call(
        split_down,
        [((hidden_units, 2 * width), BF16)] * GROUP,
        w_down[0],
        load=(0,),
        store=(0,),
    )
    down = [down[0]] + [swap(down[k], "y", k) for k in range(1, GROUP)]

    (context,) = kernel_call(
        attend,
        [((tp_size, 2 * heads, latent), BF16)],
        lengths,
        queries,
        jnp.swapaxes(latent_cache, 1, 2),
        smem=(0,),
        load=(0, 1, 2),
        after=(place,),
    )

    (moved,) = kernel_call(mark, [((8, 128), F32)], after=down[1:], flops=20_000_000_000)

    held, up, below = kernel_call(
        relay,
        [
            ((slots, 3 * width + 64), BF16),
            ((slots, 2 * width + 256), BF16),
            ((slots, 2 * width + 256), BF16),
        ],
        named_rows,
        after=(context,),
    )

    contexts = lax.all_to_all(context, "y", 0, 0, tiled=True)
    out_pair = pair_up(w_out.T, "c")
    out_other = mirror(out_pair, ("zh", "zl"))

    (crossed,) = kernel_call(mark, [((8, 128), F32)], after=(out_other,))

    inner, score = kernel_call(
        lift_experts,
        [((GROUP, slots, hidden_units), BF16), ((slots, 128), BF16)],
        held,
        shift(up, "y", 1),
        shift(below, "y", -1),
        w_gate[0],
        w_up[0],
        router_rows,
        load=(3, 4),
        store=(0, 1),
        after=(moved, crossed),
    )
    groups = [list(range(i, i + GROUP)) for i in range(0, tp_size, GROUP)]
    inner = lax.all_to_all(inner, "y", 0, 0, tiled=True, axis_index_groups=groups)

    out_weights = gather(jnp.stack([out_pair, out_other]), "x")
    (values,) = kernel_call(
        lift_heads,
        [((rows, depth), BF16)],
        contexts,
        w_uv,
        load=(1,),
        flops=10_000_000_000,
    )

    all_values = trade(values, "zl")
    (gathered,) = kernel_call(
        mark, [((8, 128), F32)], after=out_weights[1:], flops=15_000_000_000
    )
    (attn_parts,) = kernel_call(
        project,
        [((4 * tp_size, rows, 128), BF16)],
        *all_values,
        *out_weights,
        after=(gathered,),
    )
    attn_parts = lax.all_to_all(attn_parts, ("zl", "y"), 0, 0, tiled=True)

    (back,) = kernel_call(
        lower_experts,
        [((ep_size, SLOTS, PADDED), BF16)],
        inner,
        *down,
        score,
        load=(1, 1 + GROUP),
        after=(contexts,),
    )
    back = lax.all_to_all(back, EP, 0, 0, tiled=True)
    keep, passed = kernel_call(
        merge_experts, [((rows, width), F32)] * 2, back, place, own, load=(1, 2)
    )
    passed = mirror(passed, "y")
    (out,) = kernel_call(
        add_attention, [((rows, width), BF16)], attn_parts, keep, passed
    )
    return out


def solution(mesh):
    split = Mesh(mesh.devices.reshape(4, 2, 4, 2, 8), ("x", "zh", "zl", "c", "y"))
    return jax.shard_map(
        on_device,
        mesh=split,
        in_specs=(
            P(EP, None),
            P(),
            P(EP + ("y",), None, None),
            P(EP + ("y",), None, None),
            P(EP + ("y",)),
            P(EP, None),
            P(EP, None),
            P(EP, None, "y"),
            P(EP, None, "y"),
            P(EP, "y", None),
            P("y", None, None),
            P("y", EP),
        ),
        out_specs=P(EP, "y"),
        check_vma=False,
    )
```

```python
import jax
import jax.numpy as jnp
from jax import lax
from jax.experimental import pallas as pl
from jax.experimental.pallas import tpu as pltpu
from jax.sharding import Mesh, PartitionSpec as P

ROUTE_SCALE = 2.5
EPSILON = 1e-06
SCORE_SCALE = 192.0 ** (-0.5)
SLOTS = 4
EP = ("x", "zh", "zl", "c")
PADDED = 1024
GROUP = 4
HELD = (0, 3, 5)
NT = (((1,), (1,)), ((), ()))
TN = (((0,), (0,)), ((), ()))
F32 = jnp.float32
BF16 = jnp.bfloat16


def kernel_call(body, outs, *args, smem=(), load=(), store=(), after=(), flops=0, vmem=16):
    def place(n, moved):
        space = pltpu.HBM if n in moved else pltpu.VMEM
        return pl.BlockSpec(memory_space=space)

    def scratch(a, n):
        return (pltpu.SMEM if n in smem else pltpu.VMEM)(a.shape, a.dtype)

    shapes = [jax.ShapeDtypeStruct(s, d) for s, d in outs]
    count = len(args) + len(after)

    def kernel(*refs):
        given = list(refs[: len(args)])
        made = list(refs[count : count + len(outs)])
        held = list(refs[count + len(outs) :])
        sems = held.pop() if load or store else None
        copies = []
        for i, n in enumerate(load):
            copies.append(pltpu.make_async_copy(given[n], held[i], sems.at[i]))
            copies[-1].start()
            given[n] = held[i]
        for copy in copies:
            copy.wait()
        copies = []
        for i, n in enumerate(store, len(load)):
            copies.append(pltpu.make_async_copy(held[i], made[n], sems.at[i]))
            made[n] = held[i]
        body(*given, *made)
        for copy in copies:
            copy.start()
        for copy in copies:
            copy.wait()

    scratch_shapes = [scratch(args[n], n) for n in load]
    scratch_shapes += [pltpu.VMEM(shapes[n].shape, shapes[n].dtype) for n in store]
    if scratch_shapes:
        scratch_shapes.append(pltpu.SemaphoreType.DMA((len(load) + len(store),)))
    nbytes = sum(a.size * a.dtype.itemsize for a in args)
    return pl.pallas_call(
        kernel,
        out_shape=tuple(shapes),
        in_specs=[place(n, load) for n in range(len(args))]
        + [pl.BlockSpec(memory_space=pl.ANY) for _ in after],
        out_specs=tuple(place(n, store) for n in range(len(outs))),
        scratch_shapes=scratch_shapes,
        compiler_params=pltpu.CompilerParams(vmem_limit_bytes=vmem << 20),
        cost_estimate=pl.CostEstimate(flops=flops, bytes_accessed=nbytes, transcendentals=0),
    )(*args, *after)


def one_hot(condition):
    return condition.astype(F32).astype(BF16)


def iotas(*shape):
    return lax.broadcasted_iota(jnp.int32, shape, 0), lax.broadcasted_iota(jnp.int32, shape, 1)


def prepare(hidden_ref, gain_ref, ids_ref, send_ref, place_ref, own_ref):
    values = hidden_ref[...].astype(F32)
    factor = lax.rsqrt(jnp.mean(values * values, axis=-1, keepdims=True) + EPSILON)
    gain = gain_ref[...].astype(F32).reshape(1, values.shape[1])
    normalized = values * factor * gain
    width = values.shape[1] // 8
    pad = jnp.zeros((values.shape[0], send_ref.shape[2] - 3 * width), F32)
    sent = jnp.zeros((values.shape[0], send_ref.shape[2]), F32)
    own = jnp.zeros((values.shape[0], width), F32)
    for s in range(8):
        here = lax.axis_index("y") == s
        own = jnp.where(here, values[:, s * width : (s + 1) * width], own)
        taken = [
            normalized[:, (s + k) % 8 * width : ((s + k) % 8 + 1) * width] for k in HELD
        ]
        taken = jnp.concatenate([*taken, pad], axis=1)
        sent = jnp.where(here, taken, sent)
    own_ref[...] = own
    normalized = sent.astype(BF16)
    slots, rows = place_ref.shape
    slot = lax.broadcasted_iota(jnp.int32, (slots, rows), 0)
    named = jnp.zeros((slots, rows), jnp.bool_)
    for k in range(ids_ref.shape[0]):
        named = named | (ids_ref[k : k + 1, :] == slot // SLOTS)
    named = named.astype(F32)
    earlier = lax.broadcasted_iota(jnp.int32, (rows, rows), 0) < lax.broadcasted_iota(
        jnp.int32, (rows, rows), 1
    )
    rank = jnp.dot(
        named.astype(BF16), earlier.astype(F32).astype(BF16), preferred_element_type=F32
    )
    place = jnp.where(rank == (slot % SLOTS).astype(F32), named, 0.0)
    place_ref[...] = place
    sent = jnp.dot(place.astype(BF16), normalized, preferred_element_type=F32)
    send_ref[...] = sent.reshape(send_ref.shape).astype(BF16)


def attend(lengths_ref, queries_ref, cache_ref, context_ref):
    rows, heads, _ = queries_ref.shape
    groups, _, latent = context_ref.shape
    found = []
    for r in range(rows):
        keys = cache_ref[r]
        scores = jnp.dot(queries_ref[r], keys, preferred_element_type=F32) * SCORE_SCALE
        positions = lax.broadcasted_iota(jnp.int32, scores.shape, 1)
        scores = jnp.where(positions < lengths_ref[r], scores, -1e30)
        raised = jnp.exp(scores - jnp.max(scores, axis=-1, keepdims=True))
        soft = (raised / jnp.sum(raised, axis=-1, keepdims=True)).astype(BF16)
        context = lax.dot_general(soft, keys[:latent], NT, preferred_element_type=F32)
        found.append(context.reshape(groups, heads // groups, latent))
    context_ref[...] = jnp.concatenate(found, axis=1).astype(BF16)


def lift_heads(context_ref, w_uv_ref, values_ref):
    heads, latent, width = w_uv_ref.shape
    rows = values_ref.shape[0]
    context = context_ref[...].reshape(rows * heads, latent)
    token, entry = iotas(rows, rows * heads)
    for h in range(heads):
        lifted = jnp.dot(context, w_uv_ref[h], preferred_element_type=F32).astype(BF16)
        pick = one_hot(entry == token * heads + h)
        mine = jnp.dot(pick, lifted, preferred_element_type=F32).astype(BF16)
        values_ref[:, h * width : (h + 1) * width] = mine


def repeat(value_ref, out_ref):
    out_ref[...] = value_ref[...]


def split_down(w_down_ref, *out_refs):
    width = out_refs[0].shape[1] // 2
    for d in range(8):
        for k in range(len(out_refs)):

            @pl.when(lax.axis_index("y") ^ k == d)
            def _(d=d, k=k):
                for half, s in enumerate((d, 7 - d)):
                    out_refs[k][:, half * width : (half + 1) * width] = w_down_ref[
                        :, s * width : (s + 1) * width
                    ]


def mark(out_ref):
    out_ref[...] = jnp.zeros(out_ref.shape, F32)


def project(*refs):
    *parts, out_ref = refs
    blocks, slices = 4, 8
    rows = parts[0].shape[0]
    values = jnp.concatenate([part[...] for part in parts[:blocks]], axis=0)
    first = lax.axis_index("c") == 0
    for k in range(4):
        for j in range(2):
            cols = parts[blocks + k].shape[2]
            mine, other = [
                lax.dot_general(
                    values, parts[blocks + k][j, core], NT, preferred_element_type=F32
                )
                for core in range(2)
            ]
            pad = jnp.zeros((mine.shape[0], 128 - 2 * cols), F32)
            part = jnp.concatenate(
                [jnp.where(first, mine, other), jnp.where(first, other, mine), pad], axis=1
            )
            part = part.reshape(blocks, rows, 128).astype(BF16)
            tp = (lax.axis_index("x") - k + 4) % 4 * 2 + (lax.axis_index("zh") + j) % 2
            for b in range(blocks):
                out_ref[(lax.axis_index("zl") ^ b) * slices + tp] = part[b]


def relay(rows_ref, held_ref, up_ref, down_ref):
    slots, width = held_ref.shape
    rows = rows_ref[...].astype(F32).reshape(slots, width)
    held_ref[...] = rows.astype(BF16)
    w = 448
    pad = jnp.zeros((slots, 64), F32)
    up_ref[...] = jnp.concatenate(
        [rows[:, : 2 * w], rows[:, 2 * w + 256 : 3 * w], pad], axis=1
    ).astype(BF16)
    down_ref[...] = jnp.concatenate(
        [rows[:, :w], rows[:, 2 * w : 3 * w], rows[:, w : w + 256]], axis=1
    ).astype(BF16)


def lift_experts(
    held_ref,
    before_ref,
    after_ref,
    w_gate_ref,
    w_up_ref,
    router_ref,
    inner_ref,
    score_ref,
):
    slots = score_ref.shape[0]
    w = router_ref.shape[1]
    units = w_gate_ref.shape[1]
    tp = lax.axis_index("y")

    def weights(pieces):
        both, scores = [], []
        total = 0
        for k, first, size in pieces:
            s = (tp + k) % 8
            rows = pl.ds(pl.multiple_of(s * w + first, 64), size)
            both.append(jnp.concatenate([w_gate_ref[rows, :], w_up_ref[rows, :]], axis=1))
            scores.append(router_ref[pl.ds(s, 1), :][:, first : first + size])
            total += size
        pad = -total % 128
        if pad:
            both.append(jnp.zeros((pad, 2 * units), BF16))
            scores.append(jnp.zeros((1, pad), F32))
        scores = jnp.concatenate(scores, axis=1)
        return jnp.concatenate(both, axis=0), scores.astype(BF16)

    lifted = jnp.zeros((slots, 2 * units), F32)
    logits = jnp.zeros((slots, 128), F32)
    for ref, pieces in (
        (held_ref, [(k, 0, w) for k in HELD]),
        (before_ref, [(7, 0, w), (2, 0, w), (4, 256, w - 256)]),
        (after_ref, [(1, 0, w), (6, 0, w), (4, 0, 256)]),
    ):
        both, scores = weights(pieces)
        rows = ref[...]
        lifted += jnp.dot(rows, both, preferred_element_type=F32)
        column = jnp.broadcast_to(scores, (128, scores.shape[1]))
        logits += lax.dot_general(rows, column, NT, preferred_element_type=F32)
    gate, lifted = lifted[:, :units], lifted[:, units:]
    inner = (gate / (1.0 + jnp.exp(-gate)) * lifted).astype(BF16)
    for copy in range(inner_ref.shape[0]):
        inner_ref[copy] = inner
    score_ref[...] = (1.0 / (1.0 + jnp.exp(-logits))).astype(BF16)


def lower_experts(*refs):
    inner_ref, *parts, score_ref, back_ref = refs
    blocks, _, padded = back_ref.shape
    slots = score_ref.shape[0]
    width = parts[0].shape[1]
    total = jnp.zeros((slots, width), F32)
    for k in range(len(parts)):
        source = lax.axis_index("y") % len(parts) ^ k
        total += jnp.dot(inner_ref[source], parts[k][...], preferred_element_type=F32)
    total = jnp.concatenate([total, score_ref[:, : padded - width].astype(F32)], axis=1)
    back_ref[...] = total.reshape(blocks, SLOTS, padded).astype(BF16)


def merge_experts(back_ref, slot_ref, own_ref, keep_ref, pass_ref):
    slots, width = slot_ref.shape[0], own_ref.shape[1]
    back = back_ref[...].astype(F32).reshape(slots, back_ref.shape[2])
    share = slot_ref[...] * back[:, 2 * width : 2 * width + 1]
    share = ROUTE_SCALE * share / jnp.sum(share, axis=0, keepdims=True)
    upper = share.astype(BF16)
    lower = (share - upper.astype(F32)).astype(BF16)
    parts = back[:, : 2 * width].astype(BF16)
    merged = lax.dot_general(upper, parts, TN, preferred_element_type=F32) + lax.dot_general(
        lower, parts, TN, preferred_element_type=F32
    )
    keep_ref[...] = own_ref[...] + merged[:, :width]
    pass_ref[...] = merged[:, width:]


def add_attention(parts_ref, keep_ref, passed_ref, out_ref):
    rows, width = out_ref.shape
    blocks = 4
    slices = parts_ref.shape[0] // blocks
    sums = [
        jnp.sum(parts_ref[b * slices : (b + 1) * slices].astype(F32), axis=0)[
            :, : width // blocks
        ]
        for b in range(blocks)
    ]
    straight = lax.axis_index("y") % 2 == lax.axis_index("zh")
    attn = jnp.where(
        straight, jnp.concatenate(sums, axis=1), jnp.concatenate(sums[::-1], axis=1)
    )
    out_ref[...] = (keep_ref[...] + passed_ref[...] + attn).astype(BF16)


def shift(value, axis, k):
    size = lax.axis_size(axis)
    return lax.ppermute(value, axis, [(i, (i + k) % size) for i in range(size)])


def pair_up(value, axis):
    return jnp.stack([value, shift(value, axis, 1)])


def gather(value, axis):
    return [value] + [shift(value, axis, k) for k in range(1, lax.axis_size(axis))]


def swap(value, axis, k):
    return lax.ppermute(value, axis, [(i, i ^ k) for i in range(lax.axis_size(axis))])


def mirror(value, axis):
    size = lax.axis_size(axis)
    return lax.ppermute(value, axis, [(i, size - 1 - i) for i in range(size)])


def trade(value, axis):
    return [value] + [swap(value, axis, k) for k in range(1, lax.axis_size(axis))]


def on_device(
    hidden,
    norm_gain,
    queries,
    latent_cache,
    lengths,
    expert_ids,
    router,
    w_gate,
    w_up,
    w_down,
    w_uv,
    w_out,
):
    rows, model_width = hidden.shape
    ep_size = lax.axis_size(EP)
    tp_size = lax.axis_size("y")
    slots = ep_size * SLOTS
    width = model_width // tp_size
    hidden_units = w_gate.shape[2]
    heads, latent, value_width = w_uv.shape
    out_cols, depth = w_out.shape[1], w_out.shape[0]
    router_rows = router.reshape(tp_size, width).astype(F32)

    send, place, own = kernel_call(
        prepare,
        [
            ((ep_size, SLOTS, 3 * width + 64), BF16),
            ((slots, rows), F32),
            ((rows, width), F32),
        ],
        hidden,
        norm_gain,
        expert_ids.T,
        load=(0, 1, 2),
        store=(0, 1, 2),
        vmem=60,
    )
    named_rows = lax.all_to_all(send, EP, 0, 0, tiled=True)

    down = kernel_call(
        split_down,
        [((hidden_units, 2 * width), BF16)] * GROUP,
        w_down[0],
        load=(0,),
        store=(0,),
    )
    down = [down[0]] + [swap(down[k], "y", k) for k in range(1, GROUP)]

    (context,) = kernel_call(
        attend,
        [((tp_size, 2 * heads, latent), BF16)],
        lengths,
        queries,
        jnp.swapaxes(latent_cache, 1, 2),
        smem=(0,),
        load=(0, 1, 2),
        after=(place,),
    )

    (moved,) = kernel_call(mark, [((8, 128), F32)], after=down[1:], flops=20_000_000_000)

    held, up, below = kernel_call(
        relay,
        [
            ((slots, 3 * width + 64), BF16),
            ((slots, 2 * width + 256), BF16),
            ((slots, 2 * width + 256), BF16),
        ],
        named_rows,
        after=(context,),
    )

    contexts = lax.all_to_all(context, "y", 0, 0, tiled=True)
    out_pair = pair_up(w_out.T, "c")
    out_other = mirror(out_pair, ("zh", "zl"))

    (crossed,) = kernel_call(mark, [((8, 128), F32)], after=(out_other,))

    inner, score = kernel_call(
        lift_experts,
        [((GROUP, slots, hidden_units), BF16), ((slots, 128), BF16)],
        held,
        shift(up, "y", 1),
        shift(below, "y", -1),
        w_gate[0],
        w_up[0],
        router_rows,
        load=(3, 4),
        store=(0, 1),
        after=(moved, crossed),
    )
    groups = [list(range(i, i + GROUP)) for i in range(0, tp_size, GROUP)]
    inner = lax.all_to_all(inner, "y", 0, 0, tiled=True, axis_index_groups=groups)

    out_weights = gather(jnp.stack([out_pair, out_other]), "x")
    (values,) = kernel_call(
        lift_heads,
        [((rows, depth), BF16)],
        contexts,
        w_uv,
        load=(1,),
        flops=10_000_000_000,
    )

    (gathered,) = kernel_call(
        mark, [((8, 128), F32)], after=out_weights[1:], flops=15_000_000_000
    )
    (back,) = kernel_call(
        lower_experts,
        [((ep_size, SLOTS, PADDED), BF16)],
        inner,
        *down,
        score,
        load=(1, 1 + GROUP),
        after=(contexts,),
    )
    (again,) = kernel_call(repeat, [((rows, depth), BF16)], values, after=(back,))
    all_values = [values, swap(values, "zl", 1)]
    all_values += [swap(again, "zl", k) for k in (2, 3)]
    (attn_parts,) = kernel_call(
        project,
        [((4 * tp_size, rows, 128), BF16)],
        *all_values,
        *out_weights,
        after=(gathered,),
    )
    attn_parts = lax.all_to_all(attn_parts, ("zl", "y"), 0, 0, tiled=True)

    back = lax.all_to_all(back, EP, 0, 0, tiled=True)
    keep, passed = kernel_call(
        merge_experts, [((rows, width), F32)] * 2, back, place, own, load=(1, 2)
    )
    passed = mirror(passed, "y")
    (out,) = kernel_call(
        add_attention, [((rows, width), BF16)], attn_parts, keep, passed
    )
    return out


def solution(mesh):
    split = Mesh(mesh.devices.reshape(4, 2, 4, 2, 8), ("x", "zh", "zl", "c", "y"))
    return jax.shard_map(
        on_device,
        mesh=split,
        in_specs=(
            P(EP, None),
            P(),
            P(EP + ("y",), None, None),
            P(EP + ("y",), None, None),
            P(EP + ("y",)),
            P(EP, None),
            P(EP, None),
            P(EP, None, "y"),
            P(EP, None, "y"),
            P(EP, "y", None),
            P("y", None, None),
            P("y", EP),
        ),
        out_specs=P(EP, "y"),
        check_vma=False,
    )
```

```python
import jax
import jax.numpy as jnp
from jax import lax
from jax.experimental import pallas as pl
from jax.experimental.pallas import tpu as pltpu
from jax.sharding import Mesh, PartitionSpec as P

ROUTE_SCALE = 2.5
EPSILON = 1e-06
SCORE_SCALE = 192.0 ** (-0.5)
SLOTS = 4
EP = ("x", "zh", "zl", "c")
PADDED = 1024
GROUP = 4
HELD = (0, 3, 5)
NT = (((1,), (1,)), ((), ()))
TN = (((0,), (0,)), ((), ()))
F32 = jnp.float32
BF16 = jnp.bfloat16


def kernel_call(body, outs, *args, smem=(), load=(), store=(), after=(), flops=0, vmem=16):
    def place(n, moved):
        space = pltpu.HBM if n in moved else pltpu.VMEM
        return pl.BlockSpec(memory_space=space)

    def scratch(a, n):
        return (pltpu.SMEM if n in smem else pltpu.VMEM)(a.shape, a.dtype)

    shapes = [jax.ShapeDtypeStruct(s, d) for s, d in outs]
    count = len(args) + len(after)

    def kernel(*refs):
        given = list(refs[: len(args)])
        made = list(refs[count : count + len(outs)])
        held = list(refs[count + len(outs) :])
        sems = held.pop() if load or store else None
        copies = []
        for i, n in enumerate(load):
            copies.append(pltpu.make_async_copy(given[n], held[i], sems.at[i]))
            copies[-1].start()
            given[n] = held[i]
        for copy in copies:
            copy.wait()
        copies = []
        for i, n in enumerate(store, len(load)):
            copies.append(pltpu.make_async_copy(held[i], made[n], sems.at[i]))
            made[n] = held[i]
        body(*given, *made)
        for copy in copies:
            copy.start()
        for copy in copies:
            copy.wait()

    scratch_shapes = [scratch(args[n], n) for n in load]
    scratch_shapes += [pltpu.VMEM(shapes[n].shape, shapes[n].dtype) for n in store]
    if scratch_shapes:
        scratch_shapes.append(pltpu.SemaphoreType.DMA((len(load) + len(store),)))
    nbytes = sum(a.size * a.dtype.itemsize for a in args)
    return pl.pallas_call(
        kernel,
        out_shape=tuple(shapes),
        in_specs=[place(n, load) for n in range(len(args))]
        + [pl.BlockSpec(memory_space=pl.ANY) for _ in after],
        out_specs=tuple(place(n, store) for n in range(len(outs))),
        scratch_shapes=scratch_shapes,
        compiler_params=pltpu.CompilerParams(vmem_limit_bytes=vmem << 20),
        cost_estimate=pl.CostEstimate(flops=flops, bytes_accessed=nbytes, transcendentals=0),
    )(*args, *after)


def one_hot(condition):
    return condition.astype(F32).astype(BF16)


def iotas(*shape):
    return lax.broadcasted_iota(jnp.int32, shape, 0), lax.broadcasted_iota(jnp.int32, shape, 1)


def prepare(hidden_ref, gain_ref, ids_ref, send_ref, place_ref, own_ref):
    values = hidden_ref[...].astype(F32)
    factor = lax.rsqrt(jnp.mean(values * values, axis=-1, keepdims=True) + EPSILON)
    gain = gain_ref[...].astype(F32).reshape(1, values.shape[1])
    normalized = values * factor * gain
    width = values.shape[1] // 8
    pad = jnp.zeros((values.shape[0], send_ref.shape[2] - 3 * width), F32)
    sent = jnp.zeros((values.shape[0], send_ref.shape[2]), F32)
    own = jnp.zeros((values.shape[0], width), F32)
    for s in range(8):
        here = lax.axis_index("y") == s
        own = jnp.where(here, values[:, s * width : (s + 1) * width], own)
        taken = [
            normalized[:, (s + k) % 8 * width : ((s + k) % 8 + 1) * width] for k in HELD
        ]
        taken = jnp.concatenate([*taken, pad], axis=1)
        sent = jnp.where(here, taken, sent)
    own_ref[...] = own
    normalized = sent.astype(BF16)
    slots, rows = place_ref.shape
    slot = lax.broadcasted_iota(jnp.int32, (slots, rows), 0)
    named = jnp.zeros((slots, rows), jnp.bool_)
    for k in range(ids_ref.shape[0]):
        named = named | (ids_ref[k : k + 1, :] == slot // SLOTS)
    named = named.astype(F32)
    earlier = lax.broadcasted_iota(jnp.int32, (rows, rows), 0) < lax.broadcasted_iota(
        jnp.int32, (rows, rows), 1
    )
    rank = jnp.dot(
        named.astype(BF16), earlier.astype(F32).astype(BF16), preferred_element_type=F32
    )
    place = jnp.where(rank == (slot % SLOTS).astype(F32), named, 0.0)
    place_ref[...] = place
    sent = jnp.dot(place.astype(BF16), normalized, preferred_element_type=F32)
    send_ref[...] = sent.reshape(send_ref.shape).astype(BF16)


def attend(lengths_ref, queries_ref, cache_ref, context_ref):
    rows, heads, _ = queries_ref.shape
    groups, _, latent = context_ref.shape
    found = []
    for r in range(rows):
        keys = cache_ref[r]
        scores = jnp.dot(queries_ref[r], keys, preferred_element_type=F32) * SCORE_SCALE
        positions = lax.broadcasted_iota(jnp.int32, scores.shape, 1)
        scores = jnp.where(positions < lengths_ref[r], scores, -1e30)
        raised = jnp.exp(scores - jnp.max(scores, axis=-1, keepdims=True))
        soft = (raised / jnp.sum(raised, axis=-1, keepdims=True)).astype(BF16)
        context = lax.dot_general(soft, keys[:latent], NT, preferred_element_type=F32)
        found.append(context.reshape(groups, heads // groups, latent))
    context_ref[...] = jnp.concatenate(found, axis=1).astype(BF16)


def lift_heads(context_ref, w_uv_ref, values_ref):
    heads, latent, width = w_uv_ref.shape
    rows = values_ref.shape[0]
    context = context_ref[...].reshape(rows * heads, latent)
    token, entry = iotas(rows, rows * heads)
    for h in range(heads):
        lifted = jnp.dot(context, w_uv_ref[h], preferred_element_type=F32).astype(BF16)
        pick = one_hot(entry == token * heads + h)
        mine = jnp.dot(pick, lifted, preferred_element_type=F32).astype(BF16)
        values_ref[:, h * width : (h + 1) * width] = mine


def repeat(value_ref, out_ref):
    out_ref[...] = value_ref[...]


def split_down(w_down_ref, *out_refs):
    width = out_refs[0].shape[1] // 2
    for d in range(8):
        for k in range(len(out_refs)):

            @pl.when(lax.axis_index("y") ^ k == d)
            def _(d=d, k=k):
                for half, s in enumerate((d, 7 - d)):
                    out_refs[k][:, half * width : (half + 1) * width] = w_down_ref[
                        :, s * width : (s + 1) * width
                    ]


def mark(out_ref):
    out_ref[...] = jnp.zeros(out_ref.shape, F32)


def project(*refs):
    *parts, out_ref = refs
    blocks, slices = 4, 8
    rows = parts[0].shape[0]
    values = jnp.concatenate([part[...] for part in parts[:blocks]], axis=0)
    first = lax.axis_index("c") == 0
    for k in range(4):
        for j in range(2):
            cols = parts[blocks + k].shape[2]
            mine, other = [
                lax.dot_general(
                    values, parts[blocks + k][j, core], NT, preferred_element_type=F32
                )
                for core in range(2)
            ]
            pad = jnp.zeros((mine.shape[0], 128 - 2 * cols), F32)
            part = jnp.concatenate(
                [jnp.where(first, mine, other), jnp.where(first, other, mine), pad], axis=1
            )
            part = part.reshape(blocks, rows, 128).astype(BF16)
            tp = (lax.axis_index("x") - k + 4) % 4 * 2 + (lax.axis_index("zh") + j) % 2
            for b in range(blocks):
                out_ref[(lax.axis_index("zl") ^ b) * slices + tp] = part[b]


def relay(rows_ref, held_ref, up_ref, down_ref):
    slots, width = held_ref.shape
    rows = rows_ref[...].astype(F32).reshape(slots, width)
    held_ref[...] = rows.astype(BF16)
    w = 448
    pad = jnp.zeros((slots, 64), F32)
    up_ref[...] = jnp.concatenate(
        [rows[:, : 2 * w], rows[:, 2 * w + 256 : 3 * w], pad], axis=1
    ).astype(BF16)
    down_ref[...] = jnp.concatenate(
        [rows[:, :w], rows[:, 2 * w : 3 * w], rows[:, w : w + 256]], axis=1
    ).astype(BF16)


def lift_experts(
    held_ref,
    before_ref,
    after_ref,
    w_gate_ref,
    w_up_ref,
    router_ref,
    inner_ref,
    score_ref,
):
    slots = score_ref.shape[0]
    w = router_ref.shape[1]
    units = w_gate_ref.shape[1]
    tp = lax.axis_index("y")

    def weights(pieces):
        both, scores = [], []
        total = 0
        for k, first, size in pieces:
            s = (tp + k) % 8
            rows = pl.ds(pl.multiple_of(s * w + first, 64), size)
            both.append(jnp.concatenate([w_gate_ref[rows, :], w_up_ref[rows, :]], axis=1))
            scores.append(router_ref[pl.ds(s, 1), :][:, first : first + size])
            total += size
        pad = -total % 128
        if pad:
            both.append(jnp.zeros((pad, 2 * units), BF16))
            scores.append(jnp.zeros((1, pad), F32))
        scores = jnp.concatenate(scores, axis=1)
        return jnp.concatenate(both, axis=0), scores.astype(BF16)

    lifted = jnp.zeros((slots, 2 * units), F32)
    logits = jnp.zeros((slots, 128), F32)
    for ref, pieces in (
        (held_ref, [(k, 0, w) for k in HELD]),
        (before_ref, [(7, 0, w), (2, 0, w), (4, 256, w - 256)]),
        (after_ref, [(1, 0, w), (6, 0, w), (4, 0, 256)]),
    ):
        both, scores = weights(pieces)
        rows = ref[...]
        lifted += jnp.dot(rows, both, preferred_element_type=F32)
        column = jnp.broadcast_to(scores, (128, scores.shape[1]))
        logits += lax.dot_general(rows, column, NT, preferred_element_type=F32)
    gate, lifted = lifted[:, :units], lifted[:, units:]
    inner = (gate / (1.0 + jnp.exp(-gate)) * lifted).astype(BF16)
    for copy in range(inner_ref.shape[0]):
        inner_ref[copy] = inner
    score_ref[...] = (1.0 / (1.0 + jnp.exp(-logits))).astype(BF16)


def lower_experts(*refs):
    inner_ref, *parts, score_ref, back_ref = refs
    blocks, _, padded = back_ref.shape
    slots = score_ref.shape[0]
    width = parts[0].shape[1]
    total = jnp.zeros((slots, width), F32)
    for k in range(len(parts)):
        source = lax.axis_index("y") % len(parts) ^ k
        total += jnp.dot(inner_ref[source], parts[k][...], preferred_element_type=F32)
    total = jnp.concatenate([total, score_ref[:, : padded - width].astype(F32)], axis=1)
    back_ref[...] = total.reshape(blocks, SLOTS, padded).astype(BF16)


def merge_experts(back_ref, slot_ref, own_ref, keep_ref, pass_ref):
    slots, width = slot_ref.shape[0], own_ref.shape[1]
    back = back_ref[...].astype(F32).reshape(slots, back_ref.shape[2])
    share = slot_ref[...] * back[:, 2 * width : 2 * width + 1]
    share = ROUTE_SCALE * share / jnp.sum(share, axis=0, keepdims=True)
    upper = share.astype(BF16)
    lower = (share - upper.astype(F32)).astype(BF16)
    parts = back[:, : 2 * width].astype(BF16)
    merged = lax.dot_general(upper, parts, TN, preferred_element_type=F32) + lax.dot_general(
        lower, parts, TN, preferred_element_type=F32
    )
    keep_ref[...] = own_ref[...] + merged[:, :width]
    pass_ref[...] = merged[:, width:]


def add_attention(parts_ref, keep_ref, passed_ref, out_ref):
    rows, width = out_ref.shape
    blocks = 4
    slices = parts_ref.shape[0] // blocks
    sums = [
        jnp.sum(parts_ref[b * slices : (b + 1) * slices].astype(F32), axis=0)[
            :, : width // blocks
        ]
        for b in range(blocks)
    ]
    straight = lax.axis_index("y") % 2 == lax.axis_index("zh")
    attn = jnp.where(
        straight, jnp.concatenate(sums, axis=1), jnp.concatenate(sums[::-1], axis=1)
    )
    out_ref[...] = (keep_ref[...] + passed_ref[...] + attn).astype(BF16)


def shift(value, axis, k):
    size = lax.axis_size(axis)
    return lax.ppermute(value, axis, [(i, (i + k) % size) for i in range(size)])


def pair_up(value, axis):
    return jnp.stack([value, shift(value, axis, 1)])


def gather(value, axis):
    return [value] + [shift(value, axis, k) for k in range(1, lax.axis_size(axis))]


def swap(value, axis, k):
    return lax.ppermute(value, axis, [(i, i ^ k) for i in range(lax.axis_size(axis))])


def mirror(value, axis):
    size = lax.axis_size(axis)
    return lax.ppermute(value, axis, [(i, size - 1 - i) for i in range(size)])


def trade(value, axis):
    return [value] + [swap(value, axis, k) for k in range(1, lax.axis_size(axis))]


def on_device(
    hidden,
    norm_gain,
    queries,
    latent_cache,
    lengths,
    expert_ids,
    router,
    w_gate,
    w_up,
    w_down,
    w_uv,
    w_out,
):
    rows, model_width = hidden.shape
    ep_size = lax.axis_size(EP)
    tp_size = lax.axis_size("y")
    slots = ep_size * SLOTS
    width = model_width // tp_size
    hidden_units = w_gate.shape[2]
    heads, latent, value_width = w_uv.shape
    out_cols, depth = w_out.shape[1], w_out.shape[0]
    router_rows = router.reshape(tp_size, width).astype(F32)

    send, place, own = kernel_call(
        prepare,
        [
            ((ep_size, SLOTS, 3 * width + 64), BF16),
            ((slots, rows), F32),
            ((rows, width), F32),
        ],
        hidden,
        norm_gain,
        expert_ids.T,
        load=(0, 1, 2),
        store=(0, 1, 2),
        vmem=60,
    )
    named_rows = lax.all_to_all(send, EP, 0, 0, tiled=True)

    down = kernel_call(
        split_down,
        [((hidden_units, 2 * width), BF16)] * GROUP,
        w_down[0],
        load=(0,),
        store=(0,),
    )
    down = [down[0]] + [swap(down[k], "y", k) for k in range(1, GROUP)]

    (context,) = kernel_call(
        attend,
        [((tp_size, 2 * heads, latent), BF16)],
        lengths,
        queries,
        jnp.swapaxes(latent_cache, 1, 2),
        smem=(0,),
        load=(0, 1, 2),
        after=(place,),
    )

    (moved,) = kernel_call(mark, [((8, 128), F32)], after=down[1:], flops=20_000_000_000)

    held, up, below = kernel_call(
        relay,
        [
            ((slots, 3 * width + 64), BF16),
            ((slots, 2 * width + 256), BF16),
            ((slots, 2 * width + 256), BF16),
        ],
        named_rows,
        after=(context,),
    )

    contexts = lax.all_to_all(context, "y", 0, 0, tiled=True)
    out_pair = pair_up(w_out.T, "c")
    out_other = mirror(out_pair, ("zh", "zl"))

    (crossed,) = kernel_call(mark, [((8, 128), F32)], after=(out_other,))

    inner, score = kernel_call(
        lift_experts,
        [((GROUP, slots, hidden_units), BF16), ((slots, 128), BF16)],
        held,
        shift(up, "y", 1),
        shift(below, "y", -1),
        w_gate[0],
        w_up[0],
        router_rows,
        load=(3, 4),
        store=(0, 1),
        after=(moved, crossed),
    )
    groups = [list(range(i, i + GROUP)) for i in range(0, tp_size, GROUP)]
    inner = lax.all_to_all(inner, "y", 0, 0, tiled=True, axis_index_groups=groups)

    out_weights = gather(jnp.stack([out_pair, out_other]), "x")
    (values,) = kernel_call(
        lift_heads,
        [((rows, depth), BF16)],
        contexts,
        w_uv,
        flops=10_000_000_000,
    )

    (gathered,) = kernel_call(
        mark, [((8, 128), F32)], after=out_weights[1:], flops=15_000_000_000
    )
    (back,) = kernel_call(
        lower_experts,
        [((ep_size, SLOTS, PADDED), BF16)],
        inner,
        *down,
        score,
        load=(1, 1 + GROUP),
        after=(contexts,),
    )
    (again,) = kernel_call(repeat, [((rows, depth), BF16)], values, after=(back,))
    all_values = [values, swap(again, "zl", 1), swap(values, "zl", 2), swap(again, "zl", 3)]
    (attn_parts,) = kernel_call(
        project,
        [((4 * tp_size, rows, 128), BF16)],
        *all_values,
        *out_weights,
        after=(gathered,),
    )
    attn_parts = lax.all_to_all(attn_parts, ("zl", "y"), 0, 0, tiled=True)

    back = lax.all_to_all(back, EP, 0, 0, tiled=True)
    keep, passed = kernel_call(
        merge_experts, [((rows, width), F32)] * 2, back, place, own, load=(1, 2)
    )
    passed = mirror(passed, "y")
    (out,) = kernel_call(
        add_attention, [((rows, width), BF16)], attn_parts, keep, passed
    )
    return out


def solution(mesh):
    split = Mesh(mesh.devices.reshape(4, 2, 4, 2, 8), ("x", "zh", "zl", "c", "y"))
    return jax.shard_map(
        on_device,
        mesh=split,
        in_specs=(
            P(EP, None),
            P(),
            P(EP + ("y",), None, None),
            P(EP + ("y",), None, None),
            P(EP + ("y",)),
            P(EP, None),
            P(EP, None),
            P(EP, None, "y"),
            P(EP, None, "y"),
            P(EP, "y", None),
            P("y", None, None),
            P("y", EP),
        ),
        out_specs=P(EP, "y"),
        check_vma=False,
    )
```

```python
import jax
import jax.numpy as jnp
from jax import lax
from jax.experimental import pallas as pl
from jax.experimental.pallas import tpu as pltpu
from jax.sharding import Mesh, PartitionSpec as P

ROUTE_SCALE = 2.5
EPSILON = 1e-06
SCORE_SCALE = 192.0 ** (-0.5)
SLOTS = 4
EP = ("x", "zh", "zl", "c")
PADDED = 1024
GROUP = 4
HELD = (0, 3, 5)
NT = (((1,), (1,)), ((), ()))
TN = (((0,), (0,)), ((), ()))
F32 = jnp.float32
BF16 = jnp.bfloat16


def kernel_call(body, outs, *args, smem=(), load=(), store=(), after=(), flops=0, vmem=16):
    def place(n, moved):
        space = pltpu.HBM if n in moved else pltpu.VMEM
        return pl.BlockSpec(memory_space=space)

    def scratch(a, n):
        return (pltpu.SMEM if n in smem else pltpu.VMEM)(a.shape, a.dtype)

    shapes = [jax.ShapeDtypeStruct(s, d) for s, d in outs]
    count = len(args) + len(after)

    def kernel(*refs):
        given = list(refs[: len(args)])
        made = list(refs[count : count + len(outs)])
        held = list(refs[count + len(outs) :])
        sems = held.pop() if load or store else None
        copies = []
        for i, n in enumerate(load):
            copies.append(pltpu.make_async_copy(given[n], held[i], sems.at[i]))
            copies[-1].start()
            given[n] = held[i]
        for copy in copies:
            copy.wait()
        copies = []
        for i, n in enumerate(store, len(load)):
            copies.append(pltpu.make_async_copy(held[i], made[n], sems.at[i]))
            made[n] = held[i]
        body(*given, *made)
        for copy in copies:
            copy.start()
        for copy in copies:
            copy.wait()

    scratch_shapes = [scratch(args[n], n) for n in load]
    scratch_shapes += [pltpu.VMEM(shapes[n].shape, shapes[n].dtype) for n in store]
    if scratch_shapes:
        scratch_shapes.append(pltpu.SemaphoreType.DMA((len(load) + len(store),)))
    nbytes = sum(a.size * a.dtype.itemsize for a in args)
    return pl.pallas_call(
        kernel,
        out_shape=tuple(shapes),
        in_specs=[place(n, load) for n in range(len(args))]
        + [pl.BlockSpec(memory_space=pl.ANY) for _ in after],
        out_specs=tuple(place(n, store) for n in range(len(outs))),
        scratch_shapes=scratch_shapes,
        compiler_params=pltpu.CompilerParams(vmem_limit_bytes=vmem << 20),
        cost_estimate=pl.CostEstimate(flops=flops, bytes_accessed=nbytes, transcendentals=0),
    )(*args, *after)


def one_hot(condition):
    return condition.astype(F32).astype(BF16)


def iotas(*shape):
    return lax.broadcasted_iota(jnp.int32, shape, 0), lax.broadcasted_iota(jnp.int32, shape, 1)


def prepare(hidden_ref, gain_ref, ids_ref, send_ref, place_ref, own_ref):
    values = hidden_ref[...].astype(F32)
    factor = lax.rsqrt(jnp.mean(values * values, axis=-1, keepdims=True) + EPSILON)
    gain = gain_ref[...].astype(F32).reshape(1, values.shape[1])
    normalized = values * factor * gain
    width = values.shape[1] // 8
    pad = jnp.zeros((values.shape[0], send_ref.shape[2] - 3 * width), F32)
    sent = jnp.zeros((values.shape[0], send_ref.shape[2]), F32)
    own = jnp.zeros((values.shape[0], width), F32)
    for s in range(8):
        here = lax.axis_index("y") == s
        own = jnp.where(here, values[:, s * width : (s + 1) * width], own)
        taken = [
            normalized[:, (s + k) % 8 * width : ((s + k) % 8 + 1) * width] for k in HELD
        ]
        taken = jnp.concatenate([*taken, pad], axis=1)
        sent = jnp.where(here, taken, sent)
    own_ref[...] = own
    normalized = sent.astype(BF16)
    slots, rows = place_ref.shape
    slot = lax.broadcasted_iota(jnp.int32, (slots, rows), 0)
    named = jnp.zeros((slots, rows), jnp.bool_)
    for k in range(ids_ref.shape[0]):
        named = named | (ids_ref[k : k + 1, :] == slot // SLOTS)
    named = named.astype(F32)
    earlier = lax.broadcasted_iota(jnp.int32, (rows, rows), 0) < lax.broadcasted_iota(
        jnp.int32, (rows, rows), 1
    )
    rank = jnp.dot(
        named.astype(BF16), earlier.astype(F32).astype(BF16), preferred_element_type=F32
    )
    place = jnp.where(rank == (slot % SLOTS).astype(F32), named, 0.0)
    place_ref[...] = place
    sent = jnp.dot(place.astype(BF16), normalized, preferred_element_type=F32)
    send_ref[...] = sent.reshape(send_ref.shape).astype(BF16)


def attend(lengths_ref, queries_ref, cache_ref, context_ref):
    rows, heads, _ = queries_ref.shape
    groups, _, latent = context_ref.shape
    found = []
    for r in range(rows):
        keys = cache_ref[r]
        scores = jnp.dot(queries_ref[r], keys, preferred_element_type=F32) * SCORE_SCALE
        positions = lax.broadcasted_iota(jnp.int32, scores.shape, 1)
        scores = jnp.where(positions < lengths_ref[r], scores, -1e30)
        raised = jnp.exp(scores - jnp.max(scores, axis=-1, keepdims=True))
        soft = (raised / jnp.sum(raised, axis=-1, keepdims=True)).astype(BF16)
        context = lax.dot_general(soft, keys[:latent], NT, preferred_element_type=F32)
        found.append(context.reshape(groups, heads // groups, latent))
    context_ref[...] = jnp.concatenate(found, axis=1).astype(BF16)


def lift_heads(context_ref, w_uv_ref, values_ref):
    heads, latent, width = w_uv_ref.shape
    rows = values_ref.shape[0]
    context = context_ref[...].reshape(rows * heads, latent)
    token, entry = iotas(rows, rows * heads)
    for h in range(heads):
        lifted = jnp.dot(context, w_uv_ref[h], preferred_element_type=F32).astype(BF16)
        pick = one_hot(entry == token * heads + h)
        mine = jnp.dot(pick, lifted, preferred_element_type=F32).astype(BF16)
        values_ref[:, h * width : (h + 1) * width] = mine


def repeat(value_ref, out_ref):
    out_ref[...] = value_ref[...]


def split_down(w_down_ref, *out_refs):
    width = out_refs[0].shape[1] // 2
    for d in range(8):
        for k in range(len(out_refs)):

            @pl.when(lax.axis_index("y") ^ k == d)
            def _(d=d, k=k):
                for half, s in enumerate((d, 7 - d)):
                    out_refs[k][:, half * width : (half + 1) * width] = w_down_ref[
                        :, s * width : (s + 1) * width
                    ]


def mark(out_ref):
    out_ref[...] = jnp.zeros(out_ref.shape, F32)


def project(*refs):
    *parts, out_ref = refs
    blocks, slices = 4, 8
    rows = parts[0].shape[0]
    values = jnp.concatenate([part[...] for part in parts[:blocks]], axis=0)
    first = lax.axis_index("c") == 0
    for k in range(4):
        for j in range(2):
            cols = parts[blocks + k].shape[2]
            mine, other = [
                lax.dot_general(
                    values, parts[blocks + k][j, core], NT, preferred_element_type=F32
                )
                for core in range(2)
            ]
            pad = jnp.zeros((mine.shape[0], 128 - 2 * cols), F32)
            part = jnp.concatenate(
                [jnp.where(first, mine, other), jnp.where(first, other, mine), pad], axis=1
            )
            part = part.reshape(blocks, rows, 128).astype(BF16)
            tp = (lax.axis_index("x") - k + 4) % 4 * 2 + (lax.axis_index("zh") + j) % 2
            for b in range(blocks):
                out_ref[(lax.axis_index("zl") ^ b) * slices + tp] = part[b]


def relay(rows_ref, held_ref, up_ref, down_ref):
    slots, width = held_ref.shape
    rows = rows_ref[...].astype(F32).reshape(slots, width)
    held_ref[...] = rows.astype(BF16)
    w = 448
    pad = jnp.zeros((slots, 64), F32)
    up_ref[...] = jnp.concatenate(
        [rows[:, : 2 * w], rows[:, 2 * w + 256 : 3 * w], pad], axis=1
    ).astype(BF16)
    down_ref[...] = jnp.concatenate(
        [rows[:, :w], rows[:, 2 * w : 3 * w], rows[:, w : w + 256]], axis=1
    ).astype(BF16)


def lift_experts(
    held_ref,
    before_ref,
    after_ref,
    w_gate_ref,
    w_up_ref,
    router_ref,
    inner_ref,
    score_ref,
):
    slots = score_ref.shape[0]
    w = router_ref.shape[1]
    units = w_gate_ref.shape[1]
    tp = lax.axis_index("y")

    def weights(pieces):
        both, scores = [], []
        total = 0
        for k, first, size in pieces:
            s = (tp + k) % 8
            rows = pl.ds(pl.multiple_of(s * w + first, 64), size)
            both.append(jnp.concatenate([w_gate_ref[rows, :], w_up_ref[rows, :]], axis=1))
            scores.append(router_ref[pl.ds(s, 1), :][:, first : first + size])
            total += size
        pad = -total % 128
        if pad:
            both.append(jnp.zeros((pad, 2 * units), BF16))
            scores.append(jnp.zeros((1, pad), F32))
        scores = jnp.concatenate(scores, axis=1)
        return jnp.concatenate(both, axis=0), scores.astype(BF16)

    lifted = jnp.zeros((slots, 2 * units), F32)
    logits = jnp.zeros((slots, 128), F32)
    for ref, pieces in (
        (held_ref, [(k, 0, w) for k in HELD]),
        (before_ref, [(7, 0, w), (2, 0, w), (4, 256, w - 256)]),
        (after_ref, [(1, 0, w), (6, 0, w), (4, 0, 256)]),
    ):
        both, scores = weights(pieces)
        rows = ref[...]
        lifted += jnp.dot(rows, both, preferred_element_type=F32)
        column = jnp.broadcast_to(scores, (128, scores.shape[1]))
        logits += lax.dot_general(rows, column, NT, preferred_element_type=F32)
    gate, lifted = lifted[:, :units], lifted[:, units:]
    inner = (gate / (1.0 + jnp.exp(-gate)) * lifted).astype(BF16)
    for copy in range(inner_ref.shape[0]):
        inner_ref[copy] = inner
    score_ref[...] = (1.0 / (1.0 + jnp.exp(-logits))).astype(BF16)


def lower_experts(*refs):
    inner_ref, *parts, score_ref, back_ref = refs
    blocks, _, padded = back_ref.shape
    slots = score_ref.shape[0]
    width = parts[0].shape[1]
    total = jnp.zeros((slots, width), F32)
    for k in range(len(parts)):
        source = lax.axis_index("y") % len(parts) ^ k
        total += jnp.dot(inner_ref[source], parts[k][...], preferred_element_type=F32)
    total = jnp.concatenate([total, score_ref[:, : padded - width].astype(F32)], axis=1)
    back_ref[...] = total.reshape(blocks, SLOTS, padded).astype(BF16)


def merge_experts(back_ref, slot_ref, own_ref, keep_ref, pass_ref):
    slots, width = slot_ref.shape[0], own_ref.shape[1]
    back = back_ref[...].astype(F32).reshape(slots, back_ref.shape[2])
    share = slot_ref[...] * back[:, 2 * width : 2 * width + 1]
    share = ROUTE_SCALE * share / jnp.sum(share, axis=0, keepdims=True)
    upper = share.astype(BF16)
    lower = (share - upper.astype(F32)).astype(BF16)
    parts = back[:, : 2 * width].astype(BF16)
    merged = lax.dot_general(upper, parts, TN, preferred_element_type=F32) + lax.dot_general(
        lower, parts, TN, preferred_element_type=F32
    )
    keep_ref[...] = own_ref[...] + merged[:, :width]
    pass_ref[...] = merged[:, width:]


def add_attention(parts_ref, keep_ref, passed_ref, out_ref):
    rows, width = out_ref.shape
    blocks = 4
    slices = parts_ref.shape[0] // blocks
    sums = [
        jnp.sum(parts_ref[b * slices : (b + 1) * slices].astype(F32), axis=0)[
            :, : width // blocks
        ]
        for b in range(blocks)
    ]
    straight = lax.axis_index("y") % 2 == lax.axis_index("zh")
    attn = jnp.where(
        straight, jnp.concatenate(sums, axis=1), jnp.concatenate(sums[::-1], axis=1)
    )
    out_ref[...] = (keep_ref[...] + passed_ref[...] + attn).astype(BF16)


def shift(value, axis, k):
    size = lax.axis_size(axis)
    return lax.ppermute(value, axis, [(i, (i + k) % size) for i in range(size)])


def pair_up(value, axis):
    return jnp.stack([value, shift(value, axis, 1)])


def gather(value, axis):
    return [value] + [shift(value, axis, k) for k in range(1, lax.axis_size(axis))]


def swap(value, axis, k):
    return lax.ppermute(value, axis, [(i, i ^ k) for i in range(lax.axis_size(axis))])


def mirror(value, axis):
    size = lax.axis_size(axis)
    return lax.ppermute(value, axis, [(i, size - 1 - i) for i in range(size)])


def trade(value, axis):
    return [value] + [swap(value, axis, k) for k in range(1, lax.axis_size(axis))]


def on_device(
    hidden,
    norm_gain,
    queries,
    latent_cache,
    lengths,
    expert_ids,
    router,
    w_gate,
    w_up,
    w_down,
    w_uv,
    w_out,
):
    rows, model_width = hidden.shape
    ep_size = lax.axis_size(EP)
    tp_size = lax.axis_size("y")
    slots = ep_size * SLOTS
    width = model_width // tp_size
    hidden_units = w_gate.shape[2]
    heads, latent, value_width = w_uv.shape
    out_cols, depth = w_out.shape[1], w_out.shape[0]
    router_rows = router.reshape(tp_size, width).astype(F32)

    send, place, own = kernel_call(
        prepare,
        [
            ((ep_size, SLOTS, 3 * width + 64), BF16),
            ((slots, rows), F32),
            ((rows, width), F32),
        ],
        hidden,
        norm_gain,
        expert_ids.T,
        load=(0, 1, 2),
        store=(0, 1, 2),
        vmem=60,
    )
    named_rows = lax.all_to_all(send, EP, 0, 0, tiled=True)

    down = kernel_call(
        split_down,
        [((hidden_units, 2 * width), BF16)] * GROUP,
        w_down[0],
        store=(0,),
    )
    down = [down[0]] + [swap(down[k], "y", k) for k in range(1, GROUP)]

    (context,) = kernel_call(
        attend,
        [((tp_size, 2 * heads, latent), BF16)],
        lengths,
        queries,
        jnp.swapaxes(latent_cache, 1, 2),
        smem=(0,),
        after=(place,),
    )

    (moved,) = kernel_call(mark, [((8, 128), F32)], after=down[1:], flops=20_000_000_000)

    held, up, below = kernel_call(
        relay,
        [
            ((slots, 3 * width + 64), BF16),
            ((slots, 2 * width + 256), BF16),
            ((slots, 2 * width + 256), BF16),
        ],
        named_rows,
        after=(context,),
    )

    contexts = lax.all_to_all(context, "y", 0, 0, tiled=True)
    out_pair = pair_up(w_out.T, "c")
    out_other = mirror(out_pair, ("zh", "zl"))

    (crossed,) = kernel_call(mark, [((8, 128), F32)], after=(out_other,))

    inner, score = kernel_call(
        lift_experts,
        [((GROUP, slots, hidden_units), BF16), ((slots, 128), BF16)],
        held,
        shift(up, "y", 1),
        shift(below, "y", -1),
        w_gate[0],
        w_up[0],
        router_rows,
        store=(0, 1),
        after=(moved, crossed),
    )
    groups = [list(range(i, i + GROUP)) for i in range(0, tp_size, GROUP)]
    inner = lax.all_to_all(inner, "y", 0, 0, tiled=True, axis_index_groups=groups)

    out_weights = gather(jnp.stack([out_pair, out_other]), "x")
    (values,) = kernel_call(
        lift_heads,
        [((rows, depth), BF16)],
        contexts,
        w_uv,
        flops=10_000_000_000,
    )

    (gathered,) = kernel_call(
        mark, [((8, 128), F32)], after=out_weights[1:], flops=15_000_000_000
    )
    (back,) = kernel_call(
        lower_experts,
        [((ep_size, SLOTS, PADDED), BF16)],
        inner,
        *down,
        score,
        load=(1, 1 + GROUP),
        after=(contexts,),
    )
    (again,) = kernel_call(repeat, [((rows, depth), BF16)], values, after=(back,))
    all_values = [values, swap(values, "zl", 1)]
    all_values += [swap(again, "zl", k) for k in (2, 3)]
    (attn_parts,) = kernel_call(
        project,
        [((4 * tp_size, rows, 128), BF16)],
        *all_values,
        *out_weights,
        after=(gathered,),
    )
    attn_parts = lax.all_to_all(attn_parts, ("zl", "y"), 0, 0, tiled=True)

    back = lax.all_to_all(back, EP, 0, 0, tiled=True)
    keep, passed = kernel_call(
        merge_experts, [((rows, width), F32)] * 2, back, place, own, load=(1, 2)
    )
    passed = mirror(passed, "y")
    (out,) = kernel_call(
        add_attention, [((rows, width), BF16)], attn_parts, keep, passed
    )
    return out


def solution(mesh):
    split = Mesh(mesh.devices.reshape(4, 2, 4, 2, 8), ("x", "zh", "zl", "c", "y"))
    return jax.shard_map(
        on_device,
        mesh=split,
        in_specs=(
            P(EP, None),
            P(),
            P(EP + ("y",), None, None),
            P(EP + ("y",), None, None),
            P(EP + ("y",)),
            P(EP, None),
            P(EP, None),
            P(EP, None, "y"),
            P(EP, None, "y"),
            P(EP, "y", None),
            P("y", None, None),
            P("y", EP),
        ),
        out_specs=P(EP, "y"),
        check_vma=False,
    )
```
